32 devices in a mesh: groups: 2 (over x), leaf: 16 (over z, y, core).
Axes of the slice: x: 2, y: 2, z: 4, core: 2. Of those that a mesh axis runs over, the one named last changes fastest.
Arguments:
- points: float32 [3, 32768], P(None, ('groups', 'leaf')), parts along dimension 1, may hold values from 0 to 1
- leaf_order: int32 [32768], P(('groups', 'leaf')), parts along dimension 0, may hold values from 0 to 1023, as said below
- skeleton: int32 [32, 256], P(('groups', 'leaf')), parts along dimension 0, may hold values from 0 to 1023, as said below
- basis: bfloat16 [32768, 256], P(('groups', 'leaf')), parts along dimension 0, may hold values from -0.1875 to 0.1875
- transfer: bfloat16 [32, 3, 512, 256], P(('groups', 'leaf')), parts along dimension 0, as said below
- coupling: bfloat16 [32, 4, 256, 256], P(('groups', 'leaf')), parts along dimension 0, as said below
- solution: float32 [32768, 256], P(('groups', 'leaf')), parts along dimension 0, may hold values from -6 to 6
- residual: float32 [32768, 256], P(('groups', 'leaf')), parts along dimension 0, may hold values from -6 to 6
- direction: float32 [32768, 256], P(('groups', 'leaf')), parts along dimension 0, may hold values from -6 to 6
Outputs:
- solution_out: float32 [32768, 256], P(('groups', 'leaf')), parts along dimension 0
- residual_out: float32 [32768, 256], P(('groups', 'leaf')), parts along dimension 0
- direction_out: float32 [32768, 256], P(('groups', 'leaf')), parts along dimension 0
The draws below stay inside these ranges and needn't reach their ends.
There are 2 independent parts, one for each index of `groups`. The reference program is written for one: setup_inputs(seed, part) draws one part's arguments, and reference() takes and returns one part's arrays. A program takes and returns all parts, laid end to end along the dimension named above; each array names one. Nothing has to cross between parts.
Inputs may be any that keep to these rules, and one draw needn't show every extreme that they name: `leaf_order`: each aligned block of 1024 entries is an ordering of 0 to 1023. `skeleton`: each row holds 256 different row numbers of its leaf. transfer[d, k] is equal for all leaves d under the same node at level k + 1. coupling[d, k] is equal for all leaves under the same node at level k, and the two sibling nodes hold transposes of each other.
All inputs are finite; a program needn't handle non-finite values.
Results may differ from the reference program's by a relative error of at most 0.0075.
Values may be sent and summed in bfloat16 or wider, within the bound.
No kernel may reach another device: no remote copies, remote signals or barrier semaphores. Data moves between devices by JAX's collectives and lax.ppermute only.
A program may use at most 64 MiB of HBM per device.

```python
import jax
import jax.numpy as jnp
import numpy as np
from jax import lax

R = 256
S = 256
LEAF = 1024
ITERS = 2
LEVELS = 4
NPTS = 16384
N_LEAF = 16


def draw_leaf_order(key, part):
    key = jax.random.fold_in(key, 11)
    leaf_keys = jax.random.split(key, N_LEAF)

    def one_leaf(leaf_key):
        return jax.random.permutation(leaf_key, LEAF)
    return jax.vmap(one_leaf)(leaf_keys).reshape(N_LEAF * LEAF).astype(jnp.int32)


def draw_skeleton(key, part):
    key = jax.random.fold_in(key, 12)
    leaf_keys = jax.random.split(key, N_LEAF)

    def one_leaf(leaf_key):
        return jax.random.permutation(leaf_key, LEAF)[:R]
    return jax.vmap(one_leaf)(leaf_keys).astype(jnp.int32)


def draw_transfer(key, part):
    key = jax.random.fold_in(key, 13)
    leaf_ids = jnp.arange(N_LEAF)
    levels_out = []
    for tree_level in range(LEVELS - 1):
        level_key = jax.random.fold_in(key, tree_level)

        def one_node(node):
            return jax.random.normal(jax.random.fold_in(level_key, node), (2 * R, R), jnp.float32)
        levels_out.append(jax.vmap(one_node)(leaf_ids >> tree_level + 1))
    stacked = jnp.stack(levels_out, 1) * (2.0 * R) ** (-0.5)
    return stacked.astype(jnp.bfloat16)


def draw_coupling(key, part):
    key = jax.random.fold_in(key, 14)
    leaf_ids = jnp.arange(N_LEAF)
    levels_out = []
    for tree_level in range(LEVELS):
        level_key = jax.random.fold_in(key, tree_level)

        def one_pair(pair):
            return jax.random.normal(jax.random.fold_in(level_key, pair), (R, R), jnp.float32)
        mats = jax.vmap(one_pair)(leaf_ids >> tree_level + 1)
        on_right = leaf_ids >> tree_level & 1 == 1
        mats = jnp.where(on_right[:, None, None], jnp.swapaxes(mats, 1, 2), mats)
        levels_out.append(mats)
    stacked = jnp.stack(levels_out, 1) * (0.3 * R ** (-0.5))
    return stacked.astype(jnp.bfloat16)


def steps_of(own_key, extent, pieces, least, top_value):
    gain, own = 1.0, jax.random.fold_in(own_key, 6)
    for axis_at, shards_of in pieces:
        draws = jnp.exp(jax.random.uniform(jax.random.fold_in(own, axis_at), (shards_of,), jnp.float32, least / len(pieces), top_value / len(pieces)))
        gain = gain * jnp.repeat(draws, extent[axis_at] // shards_of).reshape([-1 if axis == axis_at else 1 for axis in range(len(extent))])
    return gain


def scatter_about(stream_key, extent, deviation, bound, cuts=(), held_as=jnp.bfloat16):
    level = steps_of(stream_key, extent, cuts, -0.22, 0.18) if cuts else 1.0
    drawn = jax.random.normal(stream_key, extent, jnp.float32) * deviation * level
    return jnp.minimum(jnp.maximum(drawn, -bound), bound).astype(held_as)


def setup_inputs(seed: int = 0, part: int = 0) -> dict:
    streams_of = jax.random.split(jax.random.key(seed), 10)
    part_splits = jax.random.split(jax.random.fold_in(streams_of[9], part), 10)
    points = jnp.clip(1.0 * jax.random.uniform(part_splits[0], (3, NPTS), jnp.float32) ** steps_of(part_splits[0], (3, NPTS), ((1, 16),), -0.2, 0.2), 0.0, 1.0)
    leaf_order = draw_leaf_order(jax.random.fold_in(jax.random.fold_in(streams_of[9], part), 71), part)
    skeleton = draw_skeleton(jax.random.fold_in(jax.random.fold_in(streams_of[9], part), 71), part)
    basis = scatter_about(part_splits[3], (NPTS, R), LEAF ** -0.5, 0.1875, ((0, 16),))
    transfer = draw_transfer(jax.random.fold_in(jax.random.fold_in(streams_of[9], part), 71), part)
    coupling = draw_coupling(jax.random.fold_in(jax.random.fold_in(streams_of[9], part), 71), part)
    solution = scatter_about(part_splits[6], (NPTS, S), 1.0, 6.0, ((0, 16),), jnp.float32)
    residual = scatter_about(part_splits[7], (NPTS, S), 1.0, 6.0, ((0, 16),), jnp.float32)
    direction = scatter_about(part_splits[8], (NPTS, S), 1.0, 6.0, ((0, 16),), jnp.float32)
    return dict(points=points, leaf_order=leaf_order, skeleton=skeleton, basis=basis, transfer=transfer, coupling=coupling, solution=solution, residual=residual, direction=direction)


length_scale = 0.1
nugget = 2.0
smallest = 1e-12

def kernel_block(raw_points, order):
    ordered = jnp.take(raw_points, order, axis=1)
    dist_sq = (ordered[0][:, None] - ordered[0][None, :]) ** 2
    dist_sq = dist_sq + (ordered[1][:, None] - ordered[1][None, :]) ** 2
    dist_sq = dist_sq + (ordered[2][:, None] - ordered[2][None, :]) ** 2
    scaled = jnp.sqrt(3.0 * dist_sq + smallest) / length_scale
    count = ordered.shape[1]
    return ((1.0 + scaled) * jnp.exp(-scaled) + nugget * jnp.eye(count, dtype=jnp.float32)).astype(jnp.bfloat16)

def apply_operator(vector, points, leaf_order, skeleton, basis, transfer, coupling):
    vectors = vector.reshape(N_LEAF, LEAF, S)
    leaf_pts = points.reshape(3, N_LEAF, LEAF).transpose(1, 0, 2)
    orders = leaf_order.reshape(N_LEAF, LEAF)
    bases = basis.reshape(N_LEAF, LEAF, R)

    def leaf_start(items):
        raw_points, order, skel_rows, leaf_basis, leaf_vector = items
        vector_low = leaf_vector.astype(jnp.bfloat16)
        near = jnp.dot(kernel_block(raw_points, order).astype(jnp.float32), vector_low.astype(jnp.float32), preferred_element_type=jnp.float32)
        coef = jnp.dot(leaf_basis.T.astype(jnp.float32), vector_low.astype(jnp.float32), preferred_element_type=jnp.float32)
        coef = (coef + jnp.take(leaf_vector, skel_rows, axis=0)).astype(jnp.bfloat16)
        return (near, coef)
    near, current = lax.map(leaf_start, (leaf_pts, orders, skeleton, bases, vectors))
    leaf_ids = np.arange(N_LEAF)
    coupled = []
    for tree_level in range(LEVELS):
        sibling = current[leaf_ids ^ 1 << tree_level]
        coupled.append(jnp.einsum('nij,njs->nis', coupling[:, tree_level].astype(jnp.float32), sibling.astype(jnp.float32)))
        if tree_level < LEVELS - 1:
            on_right = (leaf_ids >> tree_level & 1 == 1)[:, None, None]
            stacked = jnp.where(on_right, jnp.concatenate([sibling, current], 1), jnp.concatenate([current, sibling], 1))
            current = jnp.einsum('nji,njs->nis', transfer[:, tree_level].astype(jnp.float32), stacked.astype(jnp.float32)).astype(jnp.bfloat16)
    downward = coupled[LEVELS - 1]
    for tree_level in reversed(range(LEVELS - 1)):
        on_right = (leaf_ids >> tree_level & 1 == 1)[:, None, None]
        halves = jnp.where(on_right, transfer[:, tree_level, R:], transfer[:, tree_level, :R]).astype(jnp.float32)
        downward = coupled[tree_level] + jnp.einsum('nij,njs->nis', halves, downward, precision=lax.Precision.HIGHEST)

    def leaf_finish(items):
        near_leaf, leaf_basis, skel_rows, down_leaf = items
        result = near_leaf + jnp.dot(leaf_basis.astype(jnp.float32), down_leaf.astype(jnp.bfloat16).astype(jnp.float32), preferred_element_type=jnp.float32)
        return result.at[skel_rows].add(down_leaf)
    result = lax.map(leaf_finish, (near, bases, skeleton, downward))
    return result.reshape(N_LEAF * LEAF, S)

def gram_matrix(left, right):
    return jnp.dot(left.T.astype(jnp.float32), right.astype(jnp.float32), precision=lax.Precision.HIGHEST, preferred_element_type=jnp.float32)

def product(left, right):
    return jnp.dot(left.astype(jnp.float32), right.astype(jnp.float32), precision=lax.Precision.HIGHEST, preferred_element_type=jnp.float32)

def solve_spd(matrix, target):
    symmetric = 0.5 * (matrix + matrix.T)
    factor = jnp.linalg.cholesky(symmetric)
    return jax.scipy.linalg.cho_solve((factor, True), target)

def reference(points, leaf_order, skeleton, basis, transfer, coupling, solution, residual, direction):
    res_gram = gram_matrix(residual, residual)
    for step_index in range(ITERS):
        image = apply_operator(direction, points, leaf_order, skeleton, basis, transfer, coupling)
        alpha = solve_spd(gram_matrix(direction, image), res_gram)
        solution = solution + product(direction, alpha)
        residual = residual - product(image, alpha)
        fresh = gram_matrix(residual, residual)
        beta = solve_spd(res_gram, fresh)
        direction = residual + product(direction, beta)
        res_gram = fresh
    return (solution, residual, direction)
```

```python
import functools

import jax
import jax.numpy as jnp
from jax import lax
from jax.experimental import pallas as pl
from jax.experimental.pallas import tpu as pltpu
from jax.sharding import PartitionSpec as P

ITERS = 2
F32 = jnp.float32
BF16 = jnp.bfloat16
VMEM = pl.BlockSpec(memory_space=pltpu.VMEM)
SMEM = pl.BlockSpec(memory_space=pltpu.SMEM)
MAX_STEPS = 60
BOUND = 1e-5


def dot(left, right):
    return jnp.dot(left, right, preferred_element_type=F32)


def dot_t(left, right):
    return lax.dot_general(left, right, (((0,), (0,)), ((), ())), preferred_element_type=F32)


def split(value):
    high = value.astype(BF16)
    return high, (value - high.astype(F32)).astype(BF16)


def dot3(left, right):
    lh, ll = split(left)
    rh, rl = split(right)
    return dot(lh, rh) + (dot(lh, rl) + dot(ll, rh))


def dot_full(left, right):
    return jnp.dot(left, right, precision=lax.Precision.HIGHEST, preferred_element_type=F32)


def iotas(rows, columns):
    return (
        lax.broadcasted_iota(jnp.int32, (rows, columns), 0),
        lax.broadcasted_iota(jnp.int32, (rows, columns), 1),
    )


def eye_mask(size):
    row, column = iotas(size, size)
    return row == column


def skeleton_columns(skel_ref, count):
    row, _ = iotas(count, skel_ref.shape[1])
    return jnp.where(row == skel_ref[...], 1.0, 0.0).astype(BF16)


def skeleton_rows(skel_ref, count):
    rank = skel_ref.shape[1]
    wide = jnp.broadcast_to(skel_ref[...].astype(F32), (128, rank)).T
    column = lax.broadcasted_iota(jnp.int32, (rank, 128), 1).astype(F32)
    tiles = [
        jnp.where(wide == column + float(start), 1.0, 0.0).astype(BF16)
        for start in range(0, count, 128)
    ]
    return jnp.concatenate(tiles, 1)


def leaf_coefficients(vector, basis_ref, skel_ref):
    high, low = split(vector)
    picks = skeleton_rows(skel_ref, vector.shape[0])
    coef = dot_t(basis_ref[...], high) + (dot(picks, high) + dot(picks, low))
    return coef.astype(BF16)


def coef_kernel(direction_ref, basis_ref, skel_ref, coef_ref):
    coef_ref[...] = leaf_coefficients(direction_ref[...], basis_ref, skel_ref)


def block_kernel(points_ref, order_ref, direction_ref, block_ref, near_ref, padded, column_ref):
    count = points_ref.shape[1]
    padded[...] = jnp.zeros_like(padded)
    padded[0:3, :] = points_ref[...]
    raw = padded[...]
    high = raw.astype(BF16).astype(F32)
    middle = (raw - high).astype(BF16).astype(F32)
    low = raw - high - middle
    parts = jnp.concatenate([high, middle, low], 0).astype(BF16)
    row, _ = iotas(count, count)
    picks = jnp.where(row == order_ref[...], 1.0, 0.0).astype(BF16)
    ordered = dot(parts, picks)
    ordered = (ordered[0:8] + ordered[8:16] + ordered[16:24]) * (300.0**0.5)
    column_ref[...] = jnp.concatenate([ordered, jnp.zeros((120, count), F32)], 0).T
    low_direction = direction_ref[...].astype(BF16)
    strip = 128

    def step(index, carry):
        start = pl.multiple_of(index * strip, strip)
        mine = column_ref[pl.ds(start, strip), :]
        square = 1e-10
        for axis in range(3):
            gap = mine[:, axis : axis + 1] - ordered[axis : axis + 1, :]
            square = gap * gap + square
        scaled = square * lax.rsqrt(square)
        values = ((1.0 + scaled) * jnp.exp(-scaled)).astype(BF16)
        block_ref[pl.ds(start, strip), :] = values
        return carry

    lax.fori_loop(0, count // strip, step, 0)
    near_ref[...] = dot(block_ref[...], low_direction) + 2.0 * low_direction.astype(F32)


def near_kernel(block_ref, direction_ref, near_ref):
    low_direction = direction_ref[...].astype(BF16)
    near_ref[...] = dot(block_ref[...], low_direction) + 2.0 * low_direction.astype(F32)


def gram_kernel(value_ref, gram_ref):
    high, low = split(value_ref[...])
    both = dot_t(high, jnp.concatenate([high, low], 1))
    size = high.shape[1]
    cross = both[:, size:]
    gram_ref[...] = both[:, :size] + (cross + cross.T)


def up_kernel(level, position_ref, current_ref, sibling_ref, transfer_ref, coef_ref):
    rank = current_ref.shape[0]
    right = (position_ref[0] >> level) & 1
    mine = transfer_ref[0, level, pl.ds(pl.multiple_of(right * rank, rank), rank), :]
    other = transfer_ref[0, level, pl.ds(pl.multiple_of((1 - right) * rank, rank), rank), :]
    coef_ref[...] = (
        dot_t(mine, current_ref[...]) + dot_t(other, sibling_ref[...])
    ).astype(BF16)


def pack_pair(first, second):
    size = first.shape[0]
    row, column = iotas(size, size)
    diagonal = jnp.sum(jnp.where(row == column, second, 0.0), axis=0, keepdims=True)
    return jnp.where(row >= column, first, second), diagonal


def unpack_pair(packed, diagonal):
    size = packed.shape[0]
    row, column = iotas(size, size)
    turned = packed.T
    first = jnp.where(row >= column, packed, turned)
    second = jnp.where(row < column, packed, turned)
    return first, jnp.where(row == column, diagonal, second)


def payload_rows(size, with_start):
    rows = 2 * size + 8 + (size // 2 if with_start else 0)
    return -(-rows // 32) * 32


def down_kernel(levels, with_start, *refs):
    position_ref, near_ref = refs[0], refs[1]
    siblings = refs[2 : 2 + levels]
    (coupling_ref, transfer_ref, basis_ref, skel_ref, direction_ref, residual_ref) = refs[
        2 + levels : 8 + levels
    ]
    rest = list(refs[8 + levels :])
    start_ref = rest.pop(0) if with_start else None
    image_ref, keep_ref, send_ref, payload = rest
    rank = basis_ref.shape[1]
    count, size = direction_ref.shape
    position = position_ref[0]
    down = dot(coupling_ref[0, levels - 1], siblings[levels - 1][...])
    for level in reversed(range(levels - 1)):
        right = (position >> level) & 1
        half = transfer_ref[0, level, pl.ds(pl.multiple_of(right * rank, rank), rank), :]
        high, low = split(down)
        down = dot(coupling_ref[0, level], siblings[level][...]) + (dot(half, high) + dot(half, low))
    high, low = split(down)
    places = skeleton_columns(skel_ref, count)
    image = near_ref[...] + dot(basis_ref[...], high) + (dot(places, high) + dot(places, low))
    image_ref[...] = image
    image_high, image_low = split(image)
    both = jnp.concatenate([image_high, image_low], 1)
    direction_high, direction_low = split(direction_ref[...])
    residual_high, residual_low = split(residual_ref[...])
    wide = dot_t(direction_high, both)
    curvature = wide[:, :size] + (wide[:, size:] + dot_t(direction_low, image_high))
    wide = dot_t(residual_high, both)
    mixed = wide[:, :size] + (wide[:, size:] + dot_t(residual_low, image_high))
    wide = dot_t(image_high, both)
    cross = wide[:, size:]
    images = wide[:, :size] + (cross + cross.T)
    curvature = 0.5 * (curvature + curvature.T)
    payload[size : 2 * size, :] = mixed
    base = 2 * size
    if with_start:
        pair, diagonal = pack_pair(curvature, start_ref[...])
        half = size // 2
        tri, tail = pack_pair(images[:half, :half], images[half:, half:])
        payload[base : base + half, :] = jnp.concatenate([images[half:, :half], tri], 1)
        base += half
        tail = jnp.concatenate([tail, tail], 1)
    else:
        pair, diagonal = pack_pair(curvature, images)
        tail = diagonal
    payload[0:size, :] = pair
    payload[base:, :] = jnp.zeros((payload.shape[0] - base, size), F32)
    payload[base : base + 1, :] = diagonal
    payload[base + 1 : base + 2, :] = tail
    quarter = payload.shape[0] // 4
    core, side = position & 1, (position >> 1) & 1

    def part(core_at, side_at):
        start = pl.multiple_of((core_at * 2 + side_at) * quarter, 8)
        return payload[pl.ds(start, quarter), :]

    keep_ref[0:quarter, :] = part(core, side)
    keep_ref[quarter:, :] = part(core, 1 - side)
    send_ref[0:quarter, :] = part(1 - core, side)
    send_ref[quarter:, :] = part(1 - core, 1 - side)


def scaled_problem(matrix):
    size = matrix.shape[0]
    eye = eye_mask(size)
    picked = jnp.where(eye, matrix, 0.0)
    row_scale = lax.rsqrt(jnp.sum(picked, axis=0, keepdims=True))
    column_scale = lax.rsqrt(jnp.sum(picked, axis=1, keepdims=True))
    scaled = matrix * column_scale * row_scale
    widest = jnp.max(jnp.sum(jnp.abs(scaled), axis=0, keepdims=True), axis=1, keepdims=True)
    return scaled, column_scale, 1.8 / widest


def inverses(matrices, store, errors):
    count = len(matrices)
    size = matrices[0].shape[0]
    eye = jnp.where(eye_mask(size), 1.0, 0.0)
    problems = [scaled_problem(matrix) for matrix in matrices]
    starts = [eye * gain for _, _, gain in problems]
    slopes = [eye - scaled * gain for scaled, _, gain in problems]
    guesses = [start + slope * gain for start, slope, (_, _, gain) in zip(starts, slopes, problems)]
    gaps = list(slopes)
    for _ in range(3):
        for at in range(count):
            rough = gaps[at].astype(BF16)
            gaps[at] = dot(rough, rough)
        for at in range(count):
            guesses[at] = guesses[at] + dot(guesses[at].astype(BF16), gaps[at].astype(BF16))
    total = 0.0
    for at in range(count):
        scaled = problems[at][0]
        gap = eye - dot_full(scaled, guesses[at])
        near = jnp.sum(jnp.sum(gap * gap, axis=0, keepdims=True), axis=1, keepdims=True) < 0.5
        guess = jnp.where(near, guesses[at], starts[at])
        gap = jnp.where(near, gap, slopes[at])
        guess = guess + dot3(guess, gap)
        gap = eye - dot_full(scaled, guess)
        store[at], errors[at] = guess, gap
        total = total + jnp.sum(gap * gap)

    def unfinished(carry):
        step, total = carry
        return (step < MAX_STEPS) & (total > BOUND)

    def refine(carry):
        step, _ = carry
        total = 0.0
        for at in range(count):
            guess = store[at] + dot3(store[at], errors[at])
            gap = eye - dot_full(problems[at][0], guess)
            store[at], errors[at] = guess, gap
            total = total + jnp.sum(gap * gap)
        return step + 1, total

    lax.while_loop(unfinished, refine, (0, total))
    results = []
    for at in range(count):
        guess = store[at]
        results.append(guess + dot(guess.astype(BF16), errors[at].astype(BF16)))
    return [(result, problem[1]) for result, problem in zip(results, problems)]


def solve_kernel(with_start, last, *refs):
    position_ref, own_ref, side_ref, core_ref, far_ref = refs[:5]
    rest = list(refs[5:])
    start_ref = None if with_start else rest.pop(0)
    image_ref, residual_ref, direction_ref = rest[:3]
    rest = rest[3:]
    if last:
        solution_ref = rest.pop(0)
        solution_out, residual_out, direction_out = rest[:3]
        rest = rest[3:]
    else:
        basis_ref, skel_ref = rest[:2]
        direction_out, coef_out, alpha_out, fresh_out = rest[2:6]
        rest = rest[6:]
    payload, store, errors = rest
    size = direction_ref.shape[1]
    quarter = payload.shape[0] // 4
    position = position_ref[0]
    core, side = position & 1, (position >> 1) & 1
    for ref, core_at, side_at in (
        (own_ref, core, side),
        (side_ref, core, 1 - side),
        (core_ref, 1 - core, side),
        (far_ref, 1 - core, 1 - side),
    ):
        start = pl.multiple_of((core_at * 2 + side_at) * quarter, 8)
        payload[pl.ds(start, quarter), :] = ref[...]
    mixed = payload[size : 2 * size, :]
    base = 2 * size
    if with_start:
        half = size // 2
        low_rows = payload[base : base + half, :]
        base += half
        curvature, res_gram = unpack_pair(payload[0:size, :], payload[base : base + 1, :])
        upper, lower = unpack_pair(low_rows[:, half:], payload[base + 1 : base + 2, :half])
        corner = low_rows[:, :half]
        images = jnp.concatenate(
            [jnp.concatenate([upper, corner.T], 1), jnp.concatenate([corner, lower], 1)], 0
        )
    else:
        curvature, images = unpack_pair(payload[0:size, :], payload[base : base + 1, :])
        res_gram = start_ref[...]
    (first, first_scale), (second, second_scale) = inverses([curvature, res_gram], store, errors)
    alpha = dot3(first, res_gram * first_scale) * first_scale
    slope = dot3(mixed, alpha)
    bend = dot3(alpha.T, dot3(images, alpha))
    change = 0.5 * bend - slope
    fresh = res_gram + (change + change.T)
    beta = dot3(second, fresh * second_scale) * second_scale
    direction = direction_ref[...]
    residual = residual_ref[...] - dot3(image_ref[...], alpha)
    moved = residual + dot3(direction, beta)
    direction_out[...] = moved
    if last:
        residual_out[...] = residual
        solution_out[...] = solution_ref[...] + dot3(direction, alpha)
    else:
        coef_out[...] = leaf_coefficients(moved, basis_ref, skel_ref)
        alpha_out[...] = alpha
        fresh_out[...] = fresh


def update_kernel(
    image_ref, residual_ref, direction_ref, solution_ref, alpha_ref, residual_out, solution_out
):
    alpha = alpha_ref[...]
    residual_out[...] = residual_ref[...] - dot3(image_ref[...], alpha)
    solution_out[...] = solution_ref[...] + dot3(direction_ref[...], alpha)


def call(kernel, name, inputs, outputs, scratch=(), flops=0, limit=32):
    specs = [SMEM if value.dtype == jnp.int32 and value.shape == (1,) else VMEM for value in inputs]
    size = sum(value.size * value.dtype.itemsize for value in inputs)
    return pl.pallas_call(
        kernel,
        name=name,
        in_specs=specs,
        out_specs=[VMEM] * len(outputs),
        out_shape=[jax.ShapeDtypeStruct(shape, dtype) for shape, dtype in outputs],
        scratch_shapes=list(scratch),
        cost_estimate=pl.CostEstimate(flops=flops, bytes_accessed=size, transcendentals=0),
        compiler_params=pltpu.CompilerParams(vmem_limit_bytes=limit * 2**20),
    )(*inputs)


def swapped(value, distance):
    mask = 2**distance
    pairs = [(source, source ^ mask) for source in range(lax.axis_size("leaf"))]
    return lax.ppermute(value, "leaf", pairs)


def body(points, leaf_order, skeleton, basis, transfer, coupling, solution, residual, direction):
    levels = lax.axis_size("leaf").bit_length() - 1
    count, size = direction.shape
    rank = basis.shape[1]
    position = lax.axis_index("leaf").astype(jnp.int32).reshape(1)
    order = leaf_order.reshape(1, count)
    tall = ((count, size), F32)
    square = ((size, size), F32)
    coef = ((rank, size), BF16)
    product = 2 * count * size * size

    (current,) = call(coef_kernel, "coef", [direction, basis, skeleton], [coef], flops=product)
    block, near = call(
        block_kernel,
        "block",
        [points, order, direction],
        [((count, count), BF16), tall],
        [pltpu.VMEM((8, count), F32), pltpu.VMEM((count, 128), F32)],
        flops=20 * product,
    )
    (res_gram,) = call(gram_kernel, "gram", [residual], [square], flops=4 * product)
    for step in range(ITERS):
        first, last = step == 0, step == ITERS - 1
        if not first:
            (near,) = call(near_kernel, "near", [block, direction], [tall], flops=8 * product)
        siblings = []
        for level in range(levels):
            sibling = swapped(current, level)
            siblings.append(sibling)
            if level < levels - 1:
                (current,) = call(
                    functools.partial(up_kernel, level),
                    "up",
                    [position, current, sibling, transfer],
                    [coef],
                    flops=product,
                )
        rows = payload_rows(size, first)
        image, keep, send = call(
            functools.partial(down_kernel, levels, first),
            "down",
            [position, near, *siblings, coupling, transfer, basis, skeleton, direction, residual]
            + ([res_gram] if first else []),
            [tall, ((rows // 2, size), F32), ((rows // 2, size), F32)],
            [pltpu.VMEM((rows, size), F32)],
            flops=10 * product,
        )
        quarter = rows // 4
        half = keep + swapped(send, 0)
        own = half[:quarter] + swapped(half[quarter:], 1)
        for level in range(2, levels):
            own = own + swapped(own, level)
        side = swapped(own, 1)
        core = swapped(own, 0)
        far = swapped(side, 0)
        pieces = [position, own, side, core, far] + ([] if first else [res_gram])
        scratch = [
            pltpu.VMEM((rows, size), F32),
            pltpu.VMEM((2, size, size), F32),
            pltpu.VMEM((2, size, size), F32),
        ]
        if last:
            solution, residual, direction = call(
                functools.partial(solve_kernel, first, True),
                "solve",
                pieces + [image, residual, direction, solution],
                [tall, tall, tall],
                scratch,
                flops=10 * product,
            )
        else:
            moved, current, alpha, res_gram = call(
                functools.partial(solve_kernel, first, False),
                "solve",
                pieces + [image, residual, direction, basis, skeleton],
                [tall, coef, square, square],
                scratch,
                flops=10 * product,
            )
            residual, solution = call(
                update_kernel,
                "update",
                [image, residual, direction, solution, alpha],
                [tall, tall],
                flops=6 * product,
            )
            direction = moved
    return (solution, residual, direction)


def solution(mesh):
    placed = (
        P(None, ("groups", "leaf")),
        P(("groups", "leaf")),
        P(("groups", "leaf"), None),
        P(("groups", "leaf"), None),
        P(("groups", "leaf"), None, None, None),
        P(("groups", "leaf"), None, None, None),
        P(("groups", "leaf"), None),
        P(("groups", "leaf"), None),
        P(("groups", "leaf"), None),
    )
    return jax.shard_map(
        body,
        mesh=mesh,
        in_specs=placed,
        out_specs=(
            P(("groups", "leaf"), None),
            P(("groups", "leaf"), None),
            P(("groups", "leaf"), None),
        ),
        check_vma=False,
    )
```

```python
import functools

import jax
import jax.numpy as jnp
from jax import lax
from jax.experimental import pallas as pl
from jax.experimental.pallas import tpu as pltpu
from jax.sharding import PartitionSpec as P

ITERS = 2
F32 = jnp.float32
BF16 = jnp.bfloat16
VMEM = pl.BlockSpec(memory_space=pltpu.VMEM)
SMEM = pl.BlockSpec(memory_space=pltpu.SMEM)
ANY = pl.BlockSpec(memory_space=pl.ANY)
MAX_STEPS = 60
BOUND = 1e-5


def dot(left, right):
    return jnp.dot(left, right, preferred_element_type=F32)


def dot_t(left, right):
    return lax.dot_general(left, right, (((0,), (0,)), ((), ())), preferred_element_type=F32)


def split(value):
    high = value.astype(BF16)
    return high, (value - high.astype(F32)).astype(BF16)


def dot3(left, right):
    lh, ll = split(left)
    rh, rl = split(right)
    return dot(lh, rh) + (dot(lh, rl) + dot(ll, rh))


def dot_full(left, right):
    return jnp.dot(left, right, precision=lax.Precision.HIGHEST, preferred_element_type=F32)


def iotas(rows, columns):
    return (
        lax.broadcasted_iota(jnp.int32, (rows, columns), 0),
        lax.broadcasted_iota(jnp.int32, (rows, columns), 1),
    )


def eye_mask(size):
    row, column = iotas(size, size)
    return row == column


def skeleton_columns(skel_ref, count):
    row, _ = iotas(count, skel_ref.shape[1])
    return jnp.where(row == skel_ref[...], 1.0, 0.0).astype(BF16)


def skeleton_rows(skel_ref, count):
    rank = skel_ref.shape[1]
    wide = jnp.broadcast_to(skel_ref[...].astype(F32), (128, rank)).T
    column = lax.broadcasted_iota(jnp.int32, (rank, 128), 1).astype(F32)
    tiles = [
        jnp.where(wide == column + float(start), 1.0, 0.0).astype(BF16)
        for start in range(0, count, 128)
    ]
    return jnp.concatenate(tiles, 1)


def leaf_coefficients(vector, basis_ref, skel_ref):
    high, low = split(vector)
    picks = skeleton_rows(skel_ref, vector.shape[0])
    coef = dot_t(basis_ref[...], high) + (dot(picks, high) + dot(picks, low))
    return coef.astype(BF16)


def coef_kernel(direction_ref, basis_ref, skel_ref, coef_ref):
    coef_ref[...] = leaf_coefficients(direction_ref[...], basis_ref, skel_ref)


def block_kernel(points_ref, order_ref, after_ref, block_ref, padded, column_ref):
    count = points_ref.shape[1]
    padded[...] = jnp.zeros_like(padded)
    padded[0:3, :] = points_ref[...]
    raw = padded[...]
    high = raw.astype(BF16).astype(F32)
    middle = (raw - high).astype(BF16).astype(F32)
    low = raw - high - middle
    parts = jnp.concatenate([high, middle, low], 0).astype(BF16)
    row, _ = iotas(count, count)
    picks = jnp.where(row == order_ref[...], 1.0, 0.0).astype(BF16)
    ordered = dot(parts, picks)
    ordered = (ordered[0:8] + ordered[8:16] + ordered[16:24]) * (300.0**0.5)
    column_ref[...] = jnp.concatenate([ordered, jnp.zeros((120, count), F32)], 0).T
    strip = 128

    def step(index, carry):
        start = pl.multiple_of(index * strip, strip)
        mine = column_ref[pl.ds(start, strip), :]
        square = 1e-10
        for axis in range(3):
            gap = mine[:, axis : axis + 1] - ordered[axis : axis + 1, :]
            square = gap * gap + square
        scaled = square * lax.rsqrt(square)
        values = ((1.0 + scaled) * jnp.exp(-scaled)).astype(BF16)
        block_ref[pl.ds(start, strip), :] = values
        return carry

    lax.fori_loop(0, count // strip, step, 0)

def near_kernel(block_ref, direction_ref, near_ref):
    low_direction = direction_ref[...].astype(BF16)
    near_ref[...] = dot(block_ref[...], low_direction) + 2.0 * low_direction.astype(F32)


def turned_splits(value, high_ref, low_ref, start):
    size = value.shape[1]
    high, low = split(value)
    high_ref[start : start + size, :] = high.T
    low_ref[start : start + size, :] = low.T
    return high, low


def prepare_kernel(direction_ref, residual_ref, high_ref, low_ref, gram_ref):
    size = direction_ref.shape[1]
    turned_splits(direction_ref[...], high_ref, low_ref, 0)
    high, low = turned_splits(residual_ref[...], high_ref, low_ref, size)
    both = dot(high_ref[size:, :], jnp.concatenate([high, low], 1))
    cross = both[:, size:]
    gram_ref[...] = both[:, :size] + (cross + cross.T)


def up_kernel(level, position_ref, current_ref, sibling_ref, transfer_ref, *rest):
    coef_ref = rest[-1]
    rank = current_ref.shape[0]
    right = (position_ref[0] >> level) & 1
    mine = transfer_ref[0, level, pl.ds(pl.multiple_of(right * rank, rank), rank), :]
    other = transfer_ref[0, level, pl.ds(pl.multiple_of((1 - right) * rank, rank), rank), :]
    coef_ref[...] = (
        dot_t(mine, current_ref[...]) + dot_t(other, sibling_ref[...])
    ).astype(BF16)


def pack_pair(first, second):
    size = first.shape[0]
    row, column = iotas(size, size)
    diagonal = jnp.sum(jnp.where(row == column, second, 0.0), axis=0, keepdims=True)
    return jnp.where(row >= column, first, second), diagonal


def unpack_pair(packed, diagonal):
    size = packed.shape[0]
    row, column = iotas(size, size)
    turned = packed.T
    first = jnp.where(row >= column, packed, turned)
    second = jnp.where(row < column, packed, turned)
    return first, jnp.where(row == column, diagonal, second)


def pack_half(matrix):
    half = matrix.shape[0] // 2
    corner, tail = pack_pair(matrix[:half, :half], matrix[half:, half:])
    return jnp.concatenate([matrix[half:, :half], corner], 1), jnp.concatenate([tail, tail], 1)


def unpack_half(packed, tail):
    half = packed.shape[0]
    upper, lower = unpack_pair(packed[:, half:], tail[:, :half])
    corner = packed[:, :half]
    return jnp.concatenate(
        [jnp.concatenate([upper, corner.T], 1), jnp.concatenate([corner, lower], 1)], 0
    )


def payload_rows(size, with_start):
    rows = size + size // 2 + 8 + (size if with_start else 0)
    return -(-rows // 32) * 32


def sides(position):
    core = position & 1
    return core, (position >> (1 + core)) & 1, (position >> (2 - core)) & 1


def down_kernel(levels, with_start, *refs):
    position_ref, near_ref = refs[0], refs[1]
    siblings = refs[2 : 2 + levels]
    coupling_ref, transfer_ref, basis_ref, skel_ref, high_ref, low_ref = refs[
        2 + levels : 8 + levels
    ]
    rest = list(refs[8 + levels :])
    start_ref = rest.pop(0)
    image_ref, keep_ref, send_ref, payload = rest
    rank = basis_ref.shape[1]
    count, size = near_ref.shape
    position = position_ref[0]
    down = dot(coupling_ref[0, levels - 1], siblings[levels - 1][...])
    for level in reversed(range(levels - 1)):
        right = (position >> level) & 1
        half = transfer_ref[0, level, pl.ds(pl.multiple_of(right * rank, rank), rank), :]
        high, low = split(down)
        down = dot(coupling_ref[0, level], siblings[level][...]) + (dot(half, high) + dot(half, low))
    high, low = split(down)
    places = skeleton_columns(skel_ref, count)
    image = near_ref[...] + dot(basis_ref[...], high) + (dot(places, high) + dot(places, low))
    image_ref[...] = image
    image_high, image_low = split(image)
    both = jnp.concatenate([image_high, image_low], 1)
    wide = dot(high_ref[...], both)
    grams = wide[:, :size] + (wide[:, size:] + dot(low_ref[...], image_high))
    wide = dot_t(image_high, both)
    cross = wide[:, size:]
    images = wide[:, :size] + (cross + cross.T)
    packed, tail = pack_half(images)
    base = 0
    if with_start:
        curvature = grams[:size]
        pair, diagonal = pack_pair(0.5 * (curvature + curvature.T), start_ref[...])
        payload[0:size, :] = pair
        base = size
    else:
        diagonal = tail
    payload[base : base + size, :] = grams[base:]
    base += size
    payload[base : base + size // 2, :] = packed
    base += size // 2
    payload[base:, :] = jnp.zeros((payload.shape[0] - base, size), F32)
    payload[base : base + 1, :] = tail
    payload[base + 1 : base + 2, :] = diagonal
    quarter = payload.shape[0] // 4
    core, side, _ = sides(position)

    def part(core_at, side_at):
        start = pl.multiple_of((core_at * 2 + side_at) * quarter, 8)
        return payload[pl.ds(start, quarter), :]

    keep_ref[0:quarter, :] = part(core, side)
    keep_ref[quarter:, :] = part(core, 1 - side)
    send_ref[0:quarter, :] = part(1 - core, sides(position ^ 1)[1])
    send_ref[quarter:, :] = part(1 - core, 1 - sides(position ^ 1)[1])


def scaled_problem(matrix):
    size = matrix.shape[0]
    eye = eye_mask(size)
    picked = jnp.where(eye, matrix, 0.0)
    row_scale = lax.rsqrt(jnp.sum(picked, axis=0, keepdims=True))
    column_scale = lax.rsqrt(jnp.sum(picked, axis=1, keepdims=True))
    scaled = matrix * column_scale * row_scale
    widest = jnp.max(jnp.sum(jnp.abs(scaled), axis=0, keepdims=True), axis=1, keepdims=True)
    return scaled, column_scale, 1.8 / widest


def inverses(matrices, store, errors):
    count = len(matrices)
    size = matrices[0].shape[0]
    eye = jnp.where(eye_mask(size), 1.0, 0.0)
    problems = [scaled_problem(matrix) for matrix in matrices]
    starts = [eye * gain for _, _, gain in problems]
    slopes = [eye - scaled * gain for scaled, _, gain in problems]
    guesses = [start + slope * gain for start, slope, (_, _, gain) in zip(starts, slopes, problems)]
    gaps = list(slopes)
    for _ in range(4):
        for at in range(count):
            rough = gaps[at].astype(BF16)
            gaps[at] = dot(rough, rough)
        for at in range(count):
            guesses[at] = guesses[at] + dot(guesses[at].astype(BF16), gaps[at].astype(BF16))
    total = 0.0
    for at in range(count):
        scaled = problems[at][0]
        gap = eye - dot3(scaled, guesses[at])
        near = jnp.sum(jnp.sum(gap * gap, axis=0, keepdims=True), axis=1, keepdims=True) < 0.5
        guess = jnp.where(near, guesses[at], starts[at])
        gap = jnp.where(near, gap, slopes[at])
        guess = guess + dot3(guess, gap)
        gap = eye - dot_full(scaled, guess)
        store[at], errors[at] = guess, gap
        total = total + jnp.sum(gap * gap)

    def unfinished(carry):
        step, total = carry
        return (step < MAX_STEPS) & (total > BOUND)

    def refine(carry):
        step, _ = carry
        total = 0.0
        for at in range(count):
            guess = store[at] + dot3(store[at], errors[at])
            gap = eye - dot_full(problems[at][0], guess)
            store[at], errors[at] = guess, gap
            total = total + jnp.sum(gap * gap)
        return step + 1, total

    lax.while_loop(unfinished, refine, (0, total))
    results = []
    for at in range(count):
        guess = store[at]
        results.append(guess + dot(guess.astype(BF16), errors[at].astype(BF16)))
    return [(result, problem[1]) for result, problem in zip(results, problems)]


def collect(position, own_ref, side_ref, core_ref, far_ref, payload):
    quarter = payload.shape[0] // 4
    core, side, _ = sides(position)
    other = sides(position ^ 1)[1]
    for ref, core_at, side_at in (
        (own_ref, core, side),
        (side_ref, core, 1 - side),
        (core_ref, 1 - core, other),
        (far_ref, 1 - core, 1 - other),
    ):
        start = pl.multiple_of((core_at * 2 + side_at) * quarter, 8)
        payload[pl.ds(start, quarter), :] = ref[...]


def fresh_gram(res_gram, mixed, images, alpha):
    bend = dot3(alpha.T, dot3(images, alpha))
    change = 0.5 * bend - dot3(mixed, alpha)
    return res_gram + (change + change.T)


def first_kernel(
    position_ref,
    own_ref,
    side_ref,
    core_ref,
    far_ref,
    image_ref,
    residual_ref,
    direction_ref,
    basis_ref,
    skel_ref,
    direction_out,
    coef_out,
    alpha_out,
    beta_out,
    fresh_out,
    mixed_out,
    images_out,
    curvature_out,
    payload,
    store,
    errors,
):
    size = direction_ref.shape[1]
    collect(position_ref[0], own_ref, side_ref, core_ref, far_ref, payload)
    mixed = payload[size : 2 * size, :]
    base = 2 * size + size // 2
    images = unpack_half(payload[2 * size : base, :], payload[base : base + 1, :])
    curvature, res_gram = unpack_pair(payload[0:size, :], payload[base + 1 : base + 2, :])
    (first, first_scale), (second, second_scale) = inverses([curvature, res_gram], store, errors)
    alpha = dot3(first, res_gram * first_scale) * first_scale
    fresh = fresh_gram(res_gram, mixed, images, alpha)
    beta = dot3(second, fresh * second_scale) * second_scale
    moved = residual_ref[...] - dot3(image_ref[...], alpha) + dot3(direction_ref[...], beta)
    direction_out[...] = moved
    coef_out[...] = leaf_coefficients(moved, basis_ref, skel_ref)
    alpha_out[...] = alpha
    beta_out[...] = beta
    fresh_out[...] = fresh
    mixed_out[...] = mixed
    images_out[...] = images
    curvature_out[...] = curvature


def carry_kernel(
    alpha_ref,
    beta_ref,
    fresh_ref,
    mixed_ref,
    images_ref,
    curvature_ref,
    inverse_out,
    turn_out,
    store,
    errors,
):
    beta = beta_ref[...]
    ((inverse, scale),) = inverses([fresh_ref[...]], store, errors)
    inverse_out[...] = inverse * scale
    across = mixed_ref[...].T - dot3(images_ref[...], alpha_ref[...])
    across = across + dot3(curvature_ref[...], beta)
    turn = dot3(beta.T, across)
    turn_out[...] = 0.5 * (turn + turn.T)


def update_kernel(
    image_ref,
    residual_ref,
    direction_ref,
    solution_ref,
    alpha_ref,
    residual_out,
    solution_out,
    high_out,
    low_out,
):
    alpha = alpha_ref[...]
    residual = residual_ref[...] - dot3(image_ref[...], alpha)
    residual_out[...] = residual
    turned_splits(residual, high_out, low_out, 0)
    solution_out[...] = solution_ref[...] + dot3(direction_ref[...], alpha)


def last_kernel(
    position_ref,
    own_ref,
    side_ref,
    core_ref,
    far_ref,
    image_ref,
    residual_ref,
    direction_ref,
    solution_ref,
    fresh_ref,
    inverse_ref,
    turn_ref,
    solution_out,
    residual_out,
    direction_out,
    payload,
    store,
    errors,
    solution_held,
    residual_held,
    direction_held,
    sems,
):
    count, size = direction_ref.shape
    collect(position_ref[0], own_ref, side_ref, core_ref, far_ref, payload)
    mixed = payload[0:size, :]
    base = size + size // 2
    images = unpack_half(payload[size:base, :], payload[base : base + 1, :])
    res_gram = fresh_ref[...]
    curvature = 0.5 * (mixed + mixed.T) + turn_ref[...]
    ((first, scale),) = inverses([curvature], store, errors)
    alpha = dot3(first, res_gram * scale) * scale
    residual = residual_ref[...] - dot3(image_ref[...], alpha)
    residual_held[...] = residual
    copies = [pltpu.make_async_copy(residual_held, residual_out, sems.at[0])]
    copies[0].start()
    solution_held[...] = solution_ref[...] + dot3(direction_ref[...], alpha)
    copies.append(pltpu.make_async_copy(solution_held, solution_out, sems.at[1]))
    copies[1].start()
    fresh = fresh_gram(res_gram, mixed, images, alpha)
    picked = jnp.where(eye_mask(size), res_gram, 0.0)
    column_scale = lax.rsqrt(jnp.sum(picked, axis=1, keepdims=True))
    beta = dot3(inverse_ref[...], fresh * column_scale)
    strip = count // 4
    for at in range(4):
        rows = pl.ds(at * strip, strip)
        direction_held[rows, :] = residual_held[rows, :] + dot3(direction_ref[rows, :], beta)
        copy = pltpu.make_async_copy(
            direction_held.at[rows, :], direction_out.at[rows, :], sems.at[2 + at]
        )
        copy.start()
        copies.append(copy)
    for copy in copies:
        copy.wait()


def call(kernel, name, inputs, outputs, scratch=(), flops=0, limit=32, unused=0, apart=False):
    specs = [SMEM if value.dtype == jnp.int32 and value.shape == (1,) else VMEM for value in inputs]
    specs[len(specs) - unused :] = [ANY] * unused
    size = sum(value.size * value.dtype.itemsize for value in inputs)
    return pl.pallas_call(
        kernel,
        name=name,
        in_specs=specs,
        out_specs=[ANY if apart else VMEM] * len(outputs),
        out_shape=[jax.ShapeDtypeStruct(shape, dtype) for shape, dtype in outputs],
        scratch_shapes=list(scratch),
        cost_estimate=pl.CostEstimate(flops=flops, bytes_accessed=size, transcendentals=0),
        compiler_params=pltpu.CompilerParams(vmem_limit_bytes=limit * 2**20),
    )(*inputs)


def swapped(value, distance, other=None):
    masks = (2**distance, 2 ** (distance if other is None else other))
    pairs = [(source, source ^ masks[source & 1]) for source in range(lax.axis_size("leaf"))]
    return lax.ppermute(value, "leaf", pairs)


def summed(keep, send, levels):
    quarter = keep.shape[0] // 2
    half = keep + swapped(send, 0)
    own = half[:quarter] + swapped(half[quarter:], 1, 2)
    own = own + swapped(own, 2, 1)
    for level in range(3, levels):
        own = own + swapped(own, level)
    side = swapped(own, 1, 2)
    return [own, side, swapped(own, 0), swapped(side, 0)]


def body(points, leaf_order, skeleton, basis, transfer, coupling, solution, residual, direction):
    levels = lax.axis_size("leaf").bit_length() - 1
    count, size = direction.shape
    rank = basis.shape[1]
    position = lax.axis_index("leaf").astype(jnp.int32).reshape(1)
    order = leaf_order.reshape(1, count)
    tall = ((count, size), F32)
    square = ((size, size), F32)
    coef = ((rank, size), BF16)
    product = 2 * count * size * size
    work = pltpu.VMEM((2, size, size), F32)

    (current,) = call(
        coef_kernel, "coef", [direction, basis, skeleton], [coef], flops=product, limit=60
    )
    for step in range(ITERS):
        first = step == 0
        siblings = []
        for level in range(levels):
            sibling = swapped(current, level)
            siblings.append(sibling)
            if level == levels - 1:
                break
            extra = []
            if first and level == 1:
                (block,) = call(
                    block_kernel,
                    "block",
                    [points, order, current],
                    [((count, count), BF16)],
                    [pltpu.VMEM((8, count), F32), pltpu.VMEM((count, 128), F32)],
                    flops=20 * product,
                    unused=1,
                )
                extra = [block]
            (current,) = call(
                functools.partial(up_kernel, level),
                "up",
                [position, current, sibling, transfer] + extra,
                [coef],
                flops=product,
                unused=len(extra),
            )
        (near,) = call(near_kernel, "near", [block, direction], [tall], flops=8 * product)
        if first:
            high, low, gram = call(
                prepare_kernel,
                "prepare",
                [direction, residual],
                [((2 * size, count), BF16), ((2 * size, count), BF16), square],
                flops=8 * product,
            )
        rows = payload_rows(size, first)
        image, keep, send = call(
            functools.partial(down_kernel, levels, first),
            "down",
            [position, near, *siblings, coupling, transfer, basis, skeleton, high, low]
            + ([gram] if first else [inverse]),
            [tall, ((rows // 2, size), F32), ((rows // 2, size), F32)],
            [pltpu.VMEM((rows, size), F32)],
            flops=10 * product,
            unused=0 if first else 1,
        )
        pieces = [position] + summed(keep, send, levels)
        scratch = [pltpu.VMEM((rows, size), F32), work, work]
        if first:
            moved, current, alpha, beta, fresh, mixed, images, curvature = call(
                first_kernel,
                "first",
                pieces + [image, residual, direction, basis, skeleton],
                [tall, coef] + [square] * 6,
                scratch,
                flops=10 * product,
            )
            inverse, turn = call(
                carry_kernel,
                "carry",
                [alpha, beta, fresh, mixed, images, curvature],
                [square, square],
                [work, work],
                flops=8 * product,
            )
            residual, solution, high, low = call(
                update_kernel,
                "update",
                [image, residual, direction, solution, alpha],
                [tall, tall, ((size, count), BF16), ((size, count), BF16)],
                flops=6 * product,
            )
            direction = moved
    tall_work = pltpu.VMEM((count, size), F32)
    return tuple(
        call(
            last_kernel,
            "last",
            pieces + [image, residual, direction, solution, fresh, inverse, turn],
            [tall, tall, tall],
            scratch + [tall_work] * 3 + [pltpu.SemaphoreType.DMA((6,))],
            flops=10 * product,
            apart=True,
        )
    )


def solution(mesh):
    placed = (
        P(None, ("groups", "leaf")),
        P(("groups", "leaf")),
        P(("groups", "leaf"), None),
        P(("groups", "leaf"), None),
        P(("groups", "leaf"), None, None, None),
        P(("groups", "leaf"), None, None, None),
        P(("groups", "leaf"), None),
        P(("groups", "leaf"), None),
        P(("groups", "leaf"), None),
    )
    return jax.shard_map(
        body,
        mesh=mesh,
        in_specs=placed,
        out_specs=(
            P(("groups", "leaf"), None),
            P(("groups", "leaf"), None),
            P(("groups", "leaf"), None),
        ),
        check_vma=False,
    )
```

```python
import functools

import jax
import jax.numpy as jnp
from jax import lax
from jax.experimental import pallas as pl
from jax.experimental.pallas import tpu as pltpu
from jax.sharding import PartitionSpec as P

F32 = jnp.float32
BF16 = jnp.bfloat16
VMEM = pl.BlockSpec(memory_space=pltpu.VMEM)
SMEM = pl.BlockSpec(memory_space=pltpu.SMEM)
ANY = pl.BlockSpec(memory_space=pl.ANY)
MAX_STEPS = 60
BOUND = 1e-5


def dot(left, right):
    return jnp.dot(left, right, preferred_element_type=F32)


def dot_t(left, right):
    return lax.dot_general(left, right, (((0,), (0,)), ((), ())), preferred_element_type=F32)


def split(value):
    high = value.astype(BF16)
    return high, (value - high.astype(F32)).astype(BF16)


def dot3(left, right):
    lh, ll = split(left)
    rh, rl = split(right)
    return dot(lh, rh) + (dot(lh, rl) + dot(ll, rh))


def dot_full(left, right):
    return jnp.dot(left, right, precision=lax.Precision.HIGHEST, preferred_element_type=F32)


def iotas(rows, columns):
    return (
        lax.broadcasted_iota(jnp.int32, (rows, columns), 0),
        lax.broadcasted_iota(jnp.int32, (rows, columns), 1),
    )


def eye_mask(size):
    row, column = iotas(size, size)
    return row == column


def skeleton_columns(skel_ref, count):
    row, _ = iotas(count, skel_ref.shape[1])
    return jnp.where(row == skel_ref[...], 1.0, 0.0).astype(BF16)


def skeleton_rows(skel_ref, count):
    rank = skel_ref.shape[1]
    wide = jnp.broadcast_to(skel_ref[...].astype(F32), (128, rank)).T
    column = lax.broadcasted_iota(jnp.int32, (rank, 128), 1).astype(F32)
    tiles = [
        jnp.where(wide == column + float(start), 1.0, 0.0).astype(BF16)
        for start in range(0, count, 128)
    ]
    return jnp.concatenate(tiles, 1)


def leaf_coefficients(vector, basis_ref, skel_ref):
    high, low = split(vector)
    picks = skeleton_rows(skel_ref, vector.shape[0])
    coef = dot_t(basis_ref[...], high) + (dot(picks, high) + dot(picks, low))
    return coef.astype(BF16)


def coef_kernel(direction_ref, basis_ref, skel_ref, coef_ref):
    coef_ref[...] = leaf_coefficients(direction_ref[...], basis_ref, skel_ref)


def block_kernel(points_ref, order_ref, after_ref, block_ref, padded, column_ref):
    count = points_ref.shape[1]
    padded[...] = jnp.zeros_like(padded)
    padded[0:3, :] = points_ref[...]
    raw = padded[...]
    high = raw.astype(BF16).astype(F32)
    middle = (raw - high).astype(BF16).astype(F32)
    low = raw - high - middle
    parts = jnp.concatenate([high, middle, low], 0).astype(BF16)
    row, _ = iotas(count, count)
    picks = jnp.where(row == order_ref[...], 1.0, 0.0).astype(BF16)
    ordered = dot(parts, picks)
    ordered = (ordered[0:8] + ordered[8:16] + ordered[16:24]) * (300.0**0.5)
    column_ref[...] = jnp.concatenate([ordered, jnp.zeros((120, count), F32)], 0).T
    strip = 128

    def step(index, carry):
        start = pl.multiple_of(index * strip, strip)
        mine = column_ref[pl.ds(start, strip), :]
        square = 1e-10
        for axis in range(3):
            gap = mine[:, axis : axis + 1] - ordered[axis : axis + 1, :]
            square = gap * gap + square
        scaled = square * lax.rsqrt(square)
        values = ((1.0 + scaled) * jnp.exp(-scaled)).astype(BF16)
        block_ref[pl.ds(start, strip), :] = values
        return carry

    lax.fori_loop(0, count // strip, step, 0)

def near_kernel(block_ref, direction_ref, near_ref):
    low_direction = direction_ref[...].astype(BF16)
    near_ref[...] = dot(block_ref[...], low_direction) + 2.0 * low_direction.astype(F32)


def turned_splits(value, high_ref, low_ref, start):
    size = value.shape[1]
    high, low = split(value)
    high_ref[start : start + size, :] = high.T
    low_ref[start : start + size, :] = low.T
    return high, low


def prepare_kernel(direction_ref, residual_ref, high_ref, low_ref, gram_ref):
    size = direction_ref.shape[1]
    turned_splits(direction_ref[...], high_ref, low_ref, 0)
    high, low = turned_splits(residual_ref[...], high_ref, low_ref, size)
    both = dot(high_ref[size:, :], jnp.concatenate([high, low], 1))
    cross = both[:, size:]
    gram_ref[...] = both[:, :size] + (cross + cross.T)


def up_kernel(level, position_ref, current_ref, sibling_ref, transfer_ref, *rest):
    coef_ref = rest[-1]
    rank = current_ref.shape[0]
    right = (position_ref[0] >> level) & 1
    mine = transfer_ref[0, level, pl.ds(pl.multiple_of(right * rank, rank), rank), :]
    other = transfer_ref[0, level, pl.ds(pl.multiple_of((1 - right) * rank, rank), rank), :]
    coef_ref[...] = (
        dot_t(mine, current_ref[...]) + dot_t(other, sibling_ref[...])
    ).astype(BF16)


def pack_pair(first, second):
    size = first.shape[0]
    row, column = iotas(size, size)
    diagonal = jnp.sum(jnp.where(row == column, second, 0.0), axis=0, keepdims=True)
    return jnp.where(row >= column, first, second), diagonal


def unpack_pair(packed, diagonal):
    size = packed.shape[0]
    row, column = iotas(size, size)
    turned = packed.T
    first = jnp.where(row >= column, packed, turned)
    second = jnp.where(row < column, packed, turned)
    return first, jnp.where(row == column, diagonal, second)


def pack_half(matrix):
    half = matrix.shape[0] // 2
    corner, tail = pack_pair(matrix[:half, :half], matrix[half:, half:])
    return jnp.concatenate([matrix[half:, :half], corner], 1), jnp.concatenate([tail, tail], 1)


def unpack_half(packed, tail):
    half = packed.shape[0]
    upper, lower = unpack_pair(packed[:, half:], tail[:, :half])
    corner = packed[:, :half]
    return jnp.concatenate(
        [jnp.concatenate([upper, corner.T], 1), jnp.concatenate([corner, lower], 1)], 0
    )


def payload_rows(size, with_start):
    rows = size + size // 2 + 8 + (size if with_start else 0)
    return -(-rows // 32) * 32


def sides(position):
    core = position & 1
    return core, (position >> (1 + core)) & 1, (position >> (2 - core)) & 1


def write_parts(position, blocks, rows, payload, keep_ref, send_ref):
    base = 0
    for block in blocks:
        payload[base : base + block.shape[0], :] = block
        base += block.shape[0]
    payload[base:, :] = jnp.zeros((payload.shape[0] - base, payload.shape[1]), F32)
    for at, row in enumerate(rows):
        payload[base + at : base + at + 1, :] = row
    quarter = payload.shape[0] // 4
    core, side, _ = sides(position)
    other = sides(position ^ 1)[1]

    def part(core_at, side_at):
        start = pl.multiple_of((core_at * 2 + side_at) * quarter, 8)
        return payload[pl.ds(start, quarter), :]

    keep_ref[0:quarter, :] = part(core, side)
    keep_ref[quarter:, :] = part(core, 1 - side)
    send_ref[0:quarter, :] = part(1 - core, other)
    send_ref[quarter:, :] = part(1 - core, 1 - other)


def down_chain(position, levels, coupling_ref, transfer_ref, siblings):
    rank = coupling_ref.shape[2]
    down = dot(coupling_ref[0, levels - 1], siblings[levels - 1])
    for level in reversed(range(levels - 1)):
        right = (position >> level) & 1
        half = transfer_ref[0, level, pl.ds(pl.multiple_of(right * rank, rank), rank), :]
        high, low = split(down)
        down = dot(coupling_ref[0, level], siblings[level]) + (dot(half, high) + dot(half, low))
    return split(down)


def down_kernel(levels, *refs):
    position_ref, near_ref = refs[0], refs[1]
    siblings = [ref[...] for ref in refs[2 : 2 + levels]]
    coupling_ref, transfer_ref, basis_ref, skel_ref, high_ref, low_ref, gram_ref = refs[
        2 + levels : 9 + levels
    ]
    image_ref, keep_ref, send_ref, payload = refs[9 + levels :]
    count, size = near_ref.shape
    position = position_ref[0]
    high, low = down_chain(position, levels, coupling_ref, transfer_ref, siblings)
    places = skeleton_columns(skel_ref, count)
    image = near_ref[...] + dot(basis_ref[...], high) + (dot(places, high) + dot(places, low))
    image_ref[...] = image
    image_high, image_low = split(image)
    both = jnp.concatenate([image_high, image_low], 1)
    wide = dot(high_ref[...], both)
    grams = wide[:, :size] + (wide[:, size:] + dot(low_ref[...], image_high))
    wide = dot_t(image_high, both)
    cross = wide[:, size:]
    packed, tail = pack_half(wide[:, :size] + (cross + cross.T))
    curvature = grams[:size]
    pair, diagonal = pack_pair(0.5 * (curvature + curvature.T), gram_ref[...])
    write_parts(
        position, [pair, grams[size:], packed], [tail, diagonal], payload, keep_ref, send_ref
    )


def pair_coef_kernel(image_ref, residual_ref, basis_ref, skel_ref, pair_ref):
    count, size = image_ref.shape
    picks = skeleton_rows(skel_ref, count)
    parts = jnp.concatenate([*split(image_ref[...]), *split(residual_ref[...])], 1)
    coef = dot_t(basis_ref[...], parts) + dot(picks, parts)
    pair_ref[0] = (coef[:, :size] + coef[:, size : 2 * size]).astype(BF16)
    pair_ref[1] = (coef[:, 2 * size : 3 * size] + coef[:, 3 * size :]).astype(BF16)


def pair_up_kernel(position_ref, pair_ref, sibling_ref, transfer_ref, coef_ref):
    core = position_ref[0] & 1
    up_kernel(0, position_ref, pair_ref.at[core], sibling_ref.at[core], transfer_ref, coef_ref)


def pair_near_kernel(block_ref, image_ref, residual_ref, near_ref):
    block = block_ref[...]
    for at, ref in enumerate((image_ref, residual_ref)):
        value = ref[...]
        high, low = split(value)
        near_ref[at] = 2.0 * value + (dot(block, high) + dot(block, low))


def pair_down_kernel(levels, *refs):
    position_ref, near_ref, pair_ref = refs[:3]
    own_refs, other_refs = refs[3 : 2 + levels], refs[2 + levels : 1 + 2 * levels]
    coupling_ref, transfer_ref, basis_ref, skel_ref, applied_ref = refs[1 + 2 * levels :]
    _, count, size = near_ref.shape
    position = position_ref[0]
    core = position & 1
    siblings = [jnp.concatenate([pair_ref[core], pair_ref[1 - core]], 1)]
    for own_ref, other_ref in zip(own_refs, other_refs):
        siblings.append(jnp.concatenate([own_ref[...], other_ref[...]], 1))
    high, low = down_chain(position, levels, coupling_ref, transfer_ref, siblings)
    places = skeleton_columns(skel_ref, count)
    spread = (dot(basis_ref[...], high) + dot(basis_ref[...], low)) + (
        dot(places, high) + dot(places, low)
    )
    applied_ref[core] = near_ref[core] + spread[:, :size]
    applied_ref[1 - core] = near_ref[1 - core] + spread[:, size:]


def scaled_problem(matrix):
    size = matrix.shape[0]
    eye = eye_mask(size)
    picked = jnp.where(eye, matrix, 0.0)
    row_scale = lax.rsqrt(jnp.sum(picked, axis=0, keepdims=True))
    column_scale = lax.rsqrt(jnp.sum(picked, axis=1, keepdims=True))
    scaled = matrix * column_scale * row_scale
    widest = jnp.max(jnp.sum(jnp.abs(scaled), axis=0, keepdims=True), axis=1, keepdims=True)
    return scaled, column_scale, 1.8 / widest


def inverses(matrices, store, errors):
    count = len(matrices)
    size = matrices[0].shape[0]
    eye = jnp.where(eye_mask(size), 1.0, 0.0)
    problems = [scaled_problem(matrix) for matrix in matrices]
    starts = [eye * gain for _, _, gain in problems]
    slopes = [eye - scaled * gain for scaled, _, gain in problems]
    guesses = [start + slope * gain for start, slope, (_, _, gain) in zip(starts, slopes, problems)]
    gaps = list(slopes)
    for _ in range(4):
        for at in range(count):
            rough = gaps[at].astype(BF16)
            gaps[at] = dot(rough, rough)
        for at in range(count):
            guesses[at] = guesses[at] + dot(guesses[at].astype(BF16), gaps[at].astype(BF16))
    total = 0.0
    for at in range(count):
        scaled = problems[at][0]
        gap = eye - dot3(scaled, guesses[at])
        near = jnp.sum(jnp.sum(gap * gap, axis=0, keepdims=True), axis=1, keepdims=True) < 0.5
        guess = jnp.where(near, guesses[at], starts[at])
        gap = jnp.where(near, gap, slopes[at])
        guess = guess + dot3(guess, gap)
        gap = eye - dot_full(scaled, guess)
        store[at], errors[at] = guess, gap
        total = total + jnp.sum(gap * gap)

    def unfinished(carry):
        step, total = carry
        return (step < MAX_STEPS) & (total > BOUND)

    def refine(carry):
        step, _ = carry
        total = 0.0
        for at in range(count):
            guess = store[at] + dot3(store[at], errors[at])
            gap = eye - dot_full(problems[at][0], guess)
            store[at], errors[at] = guess, gap
            total = total + jnp.sum(gap * gap)
        return step + 1, total

    lax.while_loop(unfinished, refine, (0, total))
    results = []
    for at in range(count):
        guess = store[at]
        results.append(guess + dot(guess.astype(BF16), errors[at].astype(BF16)))
    return [(result, problem[1]) for result, problem in zip(results, problems)]


def collect(position, own_ref, side_ref, core_ref, far_ref, payload):
    quarter = payload.shape[0] // 4
    core, side, _ = sides(position)
    other = sides(position ^ 1)[1]
    for ref, core_at, side_at in (
        (own_ref, core, side),
        (side_ref, core, 1 - side),
        (core_ref, 1 - core, other),
        (far_ref, 1 - core, 1 - other),
    ):
        start = pl.multiple_of((core_at * 2 + side_at) * quarter, 8)
        payload[pl.ds(start, quarter), :] = ref[...]


def fresh_gram(res_gram, mixed, images, alpha):
    bend = dot3(alpha.T, dot3(images, alpha))
    change = 0.5 * bend - dot3(mixed, alpha)
    return res_gram + (change + change.T)


def first_kernel(
    position_ref,
    own_ref,
    side_ref,
    core_ref,
    far_ref,
    image_ref,
    residual_ref,
    applied_ref,
    image_out,
    residual_out,
    keep_out,
    send_out,
    alpha_out,
    beta_out,
    fresh_out,
    mixed_out,
    images_out,
    curvature_out,
    payload,
    later,
    store,
    errors,
):
    size = image_ref.shape[1]
    position = position_ref[0]
    collect(position, own_ref, side_ref, core_ref, far_ref, payload)
    mixed = payload[size : 2 * size, :]
    base = 2 * size + size // 2
    images = unpack_half(payload[2 * size : base, :], payload[base : base + 1, :])
    curvature, res_gram = unpack_pair(payload[0:size, :], payload[base + 1 : base + 2, :])
    (first, first_scale), (second, second_scale) = inverses([curvature, res_gram], store, errors)
    alpha = dot3(first, res_gram * first_scale) * first_scale
    fresh = fresh_gram(res_gram, mixed, images, alpha)
    beta = dot3(second, fresh * second_scale) * second_scale
    old_image = image_ref[...]
    residual = residual_ref[...] - dot3(old_image, alpha)
    image = (applied_ref[1] - dot3(applied_ref[0], alpha)) + dot3(old_image, beta)
    residual_out[...] = residual
    image_out[...] = image
    high, low = split(image)
    both = jnp.concatenate([high, low], 1)
    residual_high, residual_low = split(residual)
    wide = dot_t(residual_high, both)
    cross_gram = wide[:, :size] + (wide[:, size:] + dot_t(residual_low, high))
    wide = dot_t(high, both)
    cross = wide[:, size:]
    packed, tail = pack_half(wide[:, :size] + (cross + cross.T))
    write_parts(position, [cross_gram, packed], [tail], later, keep_out, send_out)
    alpha_out[...] = alpha
    beta_out[...] = beta
    fresh_out[...] = fresh
    mixed_out[...] = mixed
    images_out[...] = images
    curvature_out[...] = curvature


def carry_kernel(
    alpha_ref,
    beta_ref,
    fresh_ref,
    mixed_ref,
    images_ref,
    curvature_ref,
    inverse_out,
    turn_out,
    store,
    errors,
):
    beta = beta_ref[...]
    ((inverse, scale),) = inverses([fresh_ref[...]], store, errors)
    inverse_out[...] = inverse * scale
    across = mixed_ref[...].T - dot3(images_ref[...], alpha_ref[...])
    across = across + dot3(curvature_ref[...], beta)
    turn = dot3(beta.T, across)
    turn_out[...] = 0.5 * (turn + turn.T)


def update_kernel(
    residual_ref, direction_ref, solution_ref, alpha_ref, beta_ref, direction_out, solution_out
):
    direction = direction_ref[...]
    direction_out[...] = residual_ref[...] + dot3(direction, beta_ref[...])
    solution_out[...] = solution_ref[...] + dot3(direction, alpha_ref[...])


def last_kernel(
    position_ref,
    own_ref,
    side_ref,
    core_ref,
    far_ref,
    image_ref,
    residual_ref,
    direction_ref,
    solution_ref,
    fresh_ref,
    inverse_ref,
    turn_ref,
    solution_out,
    residual_out,
    direction_out,
    payload,
    store,
    errors,
    solution_held,
    residual_held,
    direction_held,
    sems,
):
    count, size = direction_ref.shape
    collect(position_ref[0], own_ref, side_ref, core_ref, far_ref, payload)
    mixed = payload[0:size, :]
    base = size + size // 2
    images = unpack_half(payload[size:base, :], payload[base : base + 1, :])
    res_gram = fresh_ref[...]
    curvature = 0.5 * (mixed + mixed.T) + turn_ref[...]
    ((first, scale),) = inverses([curvature], store, errors)
    alpha = dot3(first, res_gram * scale) * scale
    residual = residual_ref[...] - dot3(image_ref[...], alpha)
    residual_held[...] = residual
    copies = [pltpu.make_async_copy(residual_held, residual_out, sems.at[0])]
    copies[0].start()
    solution_held[...] = solution_ref[...] + dot3(direction_ref[...], alpha)
    copies.append(pltpu.make_async_copy(solution_held, solution_out, sems.at[1]))
    copies[1].start()
    fresh = fresh_gram(res_gram, mixed, images, alpha)
    picked = jnp.where(eye_mask(size), res_gram, 0.0)
    column_scale = lax.rsqrt(jnp.sum(picked, axis=1, keepdims=True))
    beta = dot3(inverse_ref[...], fresh * column_scale)
    strip = count // 4
    for at in range(4):
        rows = pl.ds(at * strip, strip)
        direction_held[rows, :] = residual_held[rows, :] + dot3(direction_ref[rows, :], beta)
        copy = pltpu.make_async_copy(
            direction_held.at[rows, :], direction_out.at[rows, :], sems.at[2 + at]
        )
        copy.start()
        copies.append(copy)
    for copy in copies:
        copy.wait()


def call(kernel, name, inputs, outputs, scratch=(), micros=1.0, limit=32, unused=0, apart=False):
    specs = [SMEM if value.dtype == jnp.int32 and value.shape == (1,) else VMEM for value in inputs]
    specs[len(specs) - unused :] = [ANY] * unused
    return pl.pallas_call(
        kernel,
        name=name,
        in_specs=specs,
        out_specs=[ANY if apart else VMEM] * len(outputs),
        out_shape=[jax.ShapeDtypeStruct(shape, dtype) for shape, dtype in outputs],
        scratch_shapes=list(scratch),
        cost_estimate=pl.CostEstimate(
            flops=int(micros * 1.1e9), bytes_accessed=0, transcendentals=0
        ),
        compiler_params=pltpu.CompilerParams(vmem_limit_bytes=limit * 2**20),
    )(*inputs)


def swapped(value, distance, other=None):
    masks = (2**distance, 2 ** (distance if other is None else other))
    pairs = [(source, source ^ masks[source & 1]) for source in range(lax.axis_size("leaf"))]
    return lax.ppermute(value, "leaf", pairs)


def add_kernel(left_ref, right_ref, *rest):
    rest[-1][...] = left_ref[...] + right_ref[...]


def plus(left, right, after):
    if not after:
        return left + right
    result = (left.shape, F32)
    return call(add_kernel, "add", [left, right, *after], [result], micros=0.2, unused=len(after))[0]


def summed(keep, send, levels, afters=((), ())):
    quarter = keep.shape[0] // 2
    half = keep + swapped(send, 0)
    own = half[:quarter] + swapped(half[quarter:], 1, 2)
    own = plus(own, swapped(own, 2, 1), afters[0])
    for level in range(3, levels):
        own = plus(own, swapped(own, level), afters[1])
    side = swapped(own, 1, 2)
    return [own, side, swapped(own, 0), swapped(side, 0)]


def body(points, leaf_order, skeleton, basis, transfer, coupling, solution, residual, direction):
    levels = lax.axis_size("leaf").bit_length() - 1
    count, size = direction.shape
    rank = basis.shape[1]
    position = lax.axis_index("leaf").astype(jnp.int32).reshape(1)
    order = leaf_order.reshape(1, count)
    tall = ((count, size), F32)
    square = ((size, size), F32)
    coef = ((rank, size), BF16)
    tall_pair = ((2, count, size), F32)
    work = pltpu.VMEM((2, size, size), F32)
    rows, later_rows = payload_rows(size, True), payload_rows(size, False)

    def up(level, current, sibling, extra=()):
        (result,) = call(
            functools.partial(up_kernel, level),
            "up",
            [position, current, sibling, transfer, *extra],
            [coef],
            micros=0.3,
            unused=len(extra),
        )
        return result

    (current,) = call(
        coef_kernel, "coef", [direction, basis, skeleton], [coef], micros=2.7, limit=60
    )
    siblings = [swapped(current, 0)]
    current = up(0, current, siblings[0])
    siblings.append(swapped(current, 1))
    (block,) = call(
        block_kernel,
        "block",
        [points, order, current],
        [((count, count), BF16)],
        [pltpu.VMEM((8, count), F32), pltpu.VMEM((count, 128), F32)],
        micros=3.6,
        unused=1,
    )
    for level in range(1, levels - 1):
        current = up(level, current, siblings[level], [block] if level == 1 else ())
        siblings.append(swapped(current, level + 1))
    (near,) = call(near_kernel, "near", [block, direction], [tall], micros=0.7)
    high, low, gram = call(
        prepare_kernel,
        "prepare",
        [direction, residual],
        [((2 * size, count), BF16), ((2 * size, count), BF16), square],
        micros=0.8,
    )
    image, keep, send = call(
        functools.partial(down_kernel, levels),
        "down",
        [position, near, *siblings, coupling, transfer, basis, skeleton, high, low, gram],
        [tall, ((rows // 2, size), F32), ((rows // 2, size), F32)],
        [pltpu.VMEM((rows, size), F32)],
        micros=3.5,
    )

    pieces = [position] + summed(keep, send, levels)
    (pair,) = call(
        pair_coef_kernel,
        "pair_coef",
        [image, residual, basis, skeleton],
        [((2, rank, size), BF16)],
        micros=1.0,
    )
    pair_sibling = swapped(pair, 0)
    (current,) = call(
        pair_up_kernel,
        "pair_up",
        [position, pair, pair_sibling, transfer],
        [coef],
        micros=0.3,
    )
    (near,) = call(
        pair_near_kernel, "pair_near", [block, image, residual], [tall_pair], micros=2.0
    )
    own = []
    for level in range(1, levels):
        own.append(swapped(current, level))
        if level < levels - 1:
            current = up(level, current, own[-1], [near] if level == 1 else ())
    other = [swapped(value, 0) for value in own]
    (applied,) = call(
        functools.partial(pair_down_kernel, levels),
        "pair_down",
        [position, near, pair_sibling, *own, *other, coupling, transfer, basis, skeleton],
        [tall_pair],
        micros=2.5,
    )

    image, residual, keep, send, alpha, beta, fresh, mixed, images, curvature = call(
        first_kernel,
        "first",
        pieces + [image, residual, applied],
        [tall, tall, ((later_rows // 2, size), F32), ((later_rows // 2, size), F32)] + [square] * 6,
        [pltpu.VMEM((rows, size), F32), pltpu.VMEM((later_rows, size), F32), work, work],
        micros=9.0,
    )
    inverse, turn = call(
        carry_kernel,
        "carry",
        [alpha, beta, fresh, mixed, images, curvature],
        [square, square],
        [work, work],
        micros=3.7,
    )
    direction, solution = call(
        update_kernel,
        "update",
        [residual, direction, solution, alpha, beta],
        [tall, tall],
        micros=1.0,
    )
    pieces = [position] + summed(keep, send, levels, ((inverse,), (direction,)))
    held = pltpu.VMEM((count, size), F32)
    return tuple(
        call(
            last_kernel,
            "last",
            pieces + [image, residual, direction, solution, fresh, inverse, turn],
            [tall, tall, tall],
            [pltpu.VMEM((later_rows, size), F32), work, work]
            + [held] * 3
            + [pltpu.SemaphoreType.DMA((6,))],
            micros=7.0,
            apart=True,
        )
    )


def solution(mesh):
    placed = (
        P(None, ("groups", "leaf")),
        P(("groups", "leaf")),
        P(("groups", "leaf"), None),
        P(("groups", "leaf"), None),
        P(("groups", "leaf"), None, None, None),
        P(("groups", "leaf"), None, None, None),
        P(("groups", "leaf"), None),
        P(("groups", "leaf"), None),
        P(("groups", "leaf"), None),
    )
    return jax.shard_map(
        body,
        mesh=mesh,
        in_specs=placed,
        out_specs=(
            P(("groups", "leaf"), None),
            P(("groups", "leaf"), None),
            P(("groups", "leaf"), None),
        ),
        check_vma=False,
    )
```

```python
import functools

import jax
import jax.numpy as jnp
from jax import lax
from jax.experimental import pallas as pl
from jax.experimental.pallas import tpu as pltpu
from jax.sharding import PartitionSpec as P

F32 = jnp.float32
BF16 = jnp.bfloat16
VMEM = pl.BlockSpec(memory_space=pltpu.VMEM)
SMEM = pl.BlockSpec(memory_space=pltpu.SMEM)
ANY = pl.BlockSpec(memory_space=pl.ANY)
MAX_STEPS = 60
BOUND = 1e-5


def dot(left, right):
    return jnp.dot(left, right, preferred_element_type=F32)


def dot_t(left, right):
    return lax.dot_general(left, right, (((0,), (0,)), ((), ())), preferred_element_type=F32)


def split(value):
    high = value.astype(BF16)
    return high, (value - high.astype(F32)).astype(BF16)


def dot3(left, right):
    lh, ll = split(left)
    rh, rl = split(right)
    return dot(lh, rh) + (dot(lh, rl) + dot(ll, rh))


def dot_full(left, right):
    return jnp.dot(left, right, precision=lax.Precision.HIGHEST, preferred_element_type=F32)


def iotas(rows, columns):
    return (
        lax.broadcasted_iota(jnp.int32, (rows, columns), 0),
        lax.broadcasted_iota(jnp.int32, (rows, columns), 1),
    )


def eye_mask(size):
    row, column = iotas(size, size)
    return row == column


def skeleton_columns(skel_ref, count):
    row, _ = iotas(count, skel_ref.shape[1])
    return jnp.where(row == skel_ref[...], 1.0, 0.0).astype(BF16)


def skeleton_rows(skel_ref, count):
    rank = skel_ref.shape[1]
    wide = jnp.broadcast_to(skel_ref[...].astype(F32), (128, rank)).T
    column = lax.broadcasted_iota(jnp.int32, (rank, 128), 1).astype(F32)
    tiles = [
        jnp.where(wide == column + float(start), 1.0, 0.0).astype(BF16)
        for start in range(0, count, 128)
    ]
    return jnp.concatenate(tiles, 1)


def coef_kernel(direction_ref, basis_ref, skel_ref, coef_ref):
    high, low = split(direction_ref[...])
    picks = skeleton_rows(skel_ref, direction_ref.shape[0])
    coef = dot_t(basis_ref[...], high) + (dot(picks, high) + dot(picks, low))
    coef_ref[...] = coef.astype(BF16)


def hold_kernel(value_ref, held_ref):
    held_ref[...] = value_ref[...]


def block_kernel(points_ref, order_ref, after_ref, block_ref, padded, column_ref):
    count = points_ref.shape[1]
    padded[...] = jnp.zeros_like(padded)
    padded[0:3, :] = points_ref[...]
    raw = padded[...]
    high = raw.astype(BF16).astype(F32)
    middle = (raw - high).astype(BF16).astype(F32)
    low = raw - high - middle
    parts = jnp.concatenate([high, middle, low], 0).astype(BF16)
    row, _ = iotas(count, count)
    picks = jnp.where(row == order_ref[...], 1.0, 0.0).astype(BF16)
    ordered = dot(parts, picks)
    ordered = (ordered[0:8] + ordered[8:16] + ordered[16:24]) * (300.0**0.5)
    column_ref[...] = jnp.concatenate([ordered, jnp.zeros((120, count), F32)], 0).T
    strip = 128

    def step(index, carry):
        start = pl.multiple_of(index * strip, strip)
        mine = column_ref[pl.ds(start, strip), :]
        square = 1e-10
        for axis in range(3):
            gap = mine[:, axis : axis + 1] - ordered[axis : axis + 1, :]
            square = gap * gap + square
        scaled = square * lax.rsqrt(square)
        values = ((1.0 + scaled) * jnp.exp(-scaled)).astype(BF16)
        block_ref[pl.ds(start, strip), :] = values
        return carry

    lax.fori_loop(0, count // strip, step, 0)

def near_kernel(block_ref, direction_ref, near_ref):
    low_direction = direction_ref[...].astype(BF16)
    near_ref[...] = dot(block_ref[...], low_direction) + 2.0 * low_direction.astype(F32)


def turned_splits(value, high_ref, low_ref, start):
    size = value.shape[1]
    high, low = split(value)
    high_ref[start : start + size, :] = high.T
    low_ref[start : start + size, :] = low.T
    return high, low


def prepare_kernel(direction_ref, residual_ref, high_ref, low_ref, gram_ref):
    size = direction_ref.shape[1]
    turned_splits(direction_ref[...], high_ref, low_ref, 0)
    high, low = turned_splits(residual_ref[...], high_ref, low_ref, size)
    both = dot(high_ref[size:, :], jnp.concatenate([high, low], 1))
    cross = both[:, size:]
    gram_ref[...] = both[:, :size] + (cross + cross.T)


def up_kernel(level, position_ref, current_ref, sibling_ref, transfer_ref, *rest):
    coef_ref = rest[-1]
    rank = current_ref.shape[0]
    right = (position_ref[0] >> level) & 1
    mine = transfer_ref[0, level, pl.ds(pl.multiple_of(right * rank, rank), rank), :]
    other = transfer_ref[0, level, pl.ds(pl.multiple_of((1 - right) * rank, rank), rank), :]
    coef_ref[...] = (
        dot_t(mine, current_ref[...]) + dot_t(other, sibling_ref[...])
    ).astype(BF16)


def pack_pair(first, second):
    size = first.shape[0]
    row, column = iotas(size, size)
    diagonal = jnp.sum(jnp.where(row == column, second, 0.0), axis=0, keepdims=True)
    return jnp.where(row >= column, first, second), diagonal


def unpack_pair(packed, diagonal):
    size = packed.shape[0]
    row, column = iotas(size, size)
    turned = packed.T
    first = jnp.where(row >= column, packed, turned)
    second = jnp.where(row < column, packed, turned)
    return first, jnp.where(row == column, diagonal, second)


def pack_half(matrix):
    half = matrix.shape[0] // 2
    corner, tail = pack_pair(matrix[:half, :half], matrix[half:, half:])
    return jnp.concatenate([matrix[half:, :half], corner], 1), jnp.concatenate([tail, tail], 1)


def unpack_half(packed, tail):
    half = packed.shape[0]
    upper, lower = unpack_pair(packed[:, half:], tail[:, :half])
    corner = packed[:, :half]
    return jnp.concatenate(
        [jnp.concatenate([upper, corner.T], 1), jnp.concatenate([corner, lower], 1)], 0
    )


def payload_rows(size, with_start):
    rows = size + size // 2 + 8 + (size if with_start else 0)
    return -(-rows // 32) * 32


def sides(position):
    core = position & 1
    return core, (position >> (1 + core)) & 1, (position >> (2 - core)) & 1


def write_parts(position, blocks, rows, payload, keep_ref, send_ref):
    base = 0
    for block in blocks:
        payload[base : base + block.shape[0], :] = block
        base += block.shape[0]
    payload[base:, :] = jnp.zeros((payload.shape[0] - base, payload.shape[1]), F32)
    for at, row in enumerate(rows):
        payload[base + at : base + at + 1, :] = row
    quarter = payload.shape[0] // 4
    core, side, _ = sides(position)
    other = sides(position ^ 1)[1]

    def part(core_at, side_at):
        start = pl.multiple_of((core_at * 2 + side_at) * quarter, 8)
        return payload[pl.ds(start, quarter), :]

    keep_ref[0:quarter, :] = part(core, side)
    keep_ref[quarter:, :] = part(core, 1 - side)
    send_ref[0:quarter, :] = part(1 - core, other)
    send_ref[quarter:, :] = part(1 - core, 1 - other)


def down_chain(position, levels, coupling_ref, transfer_ref, siblings):
    rank = coupling_ref.shape[2]
    down = dot(coupling_ref[0, levels - 1], siblings[levels - 1])
    for level in reversed(range(levels - 1)):
        right = (position >> level) & 1
        half = transfer_ref[0, level, pl.ds(pl.multiple_of(right * rank, rank), rank), :]
        high, low = split(down)
        down = dot(coupling_ref[0, level], siblings[level]) + (dot(half, high) + dot(half, low))
    return split(down)


def factor_kernel(
    near_ref,
    high_ref,
    low_ref,
    basis_ref,
    skel_ref,
    near_gram_out,
    near_square_out,
    both_high_out,
    both_low_out,
    picked_out,
    near_both_out,
    near_picked_out,
    ties_high_out,
    ties_low_out,
    basis_picked_out,
    coef_out,
):
    count, size = near_ref.shape
    near_high, near_low = split(near_ref[...])
    near_parts = jnp.concatenate([near_high, near_low], 1)
    high, low = high_ref[...], low_ref[...]
    basis = basis_ref[...]
    places, picks = skeleton_columns(skel_ref, count), skeleton_rows(skel_ref, count)
    wide = dot(high, near_parts)
    near_gram_out[...] = wide[:, :size] + (wide[:, size:] + dot(low, near_high))
    wide = dot_t(near_high, near_parts)
    cross = wide[:, size:]
    near_square_out[...] = wide[:, :size] + (cross + cross.T)
    picked = dot(high, places) + dot(low, places)
    picked_out[...] = picked.astype(BF16)
    both = picked + (dot(high, basis) + dot(low, basis))
    both_high_out[...], both_low_out[...] = split(both)
    coef_out[...] = both[size:].T.astype(BF16)
    rank = basis.shape[1]
    wide = dot(picks, jnp.concatenate([near_parts, basis], 1))
    near_picked = wide[:, :size] + wide[:, size : 2 * size]
    basis_picked = wide[:, 2 * size :]
    near_picked_out[...] = near_picked
    basis_picked_out[...] = basis_picked.astype(BF16)
    wide = dot_t(basis, jnp.concatenate([near_parts, basis], 1))
    near_both_out[...] = near_picked + (wide[:, :size] + wide[:, size : 2 * size])
    ties = wide[:, 2 * size :] + (basis_picked + basis_picked.T)
    ties_high_out[...], ties_low_out[...] = split(ties)


def down_kernel(levels, *refs):
    position_ref = refs[0]
    siblings = [ref[...] for ref in refs[1 : 1 + levels]]
    (
        coupling_ref,
        transfer_ref,
        near_gram_ref,
        near_square_ref,
        both_high_ref,
        both_low_ref,
        picked_ref,
        near_both_ref,
        near_picked_ref,
        ties_high_ref,
        ties_low_ref,
        basis_picked_ref,
        gram_ref,
        down_out,
        coef_out,
        keep_ref,
        send_ref,
        mixed_out,
        images_out,
        payload,
    ) = refs[1 + levels :]
    size = gram_ref.shape[1]
    position = position_ref[0]
    high, low = down_chain(position, levels, coupling_ref, transfer_ref, siblings)
    down_out[0], down_out[1] = high, low
    down = high.astype(F32) + low.astype(F32)
    picked = dot(basis_picked_ref[...], high) + down
    change = dot(ties_high_ref[...], high) + dot(ties_low_ref[...], high)
    change = change + (dot_t(basis_picked_ref[...], low) + down)
    near_both = near_both_ref[...]
    coef_out[...] = (near_both + change).astype(BF16)
    half_high, half_low = split(near_both + 0.5 * change)
    other = (near_picked_ref[...] + 0.5 * picked).astype(BF16)
    half = dot_t(high, half_high) + (dot_t(high, half_low) + dot_t(low, other))
    images = near_square_ref[...] + (half + half.T)
    grams = dot(both_high_ref[...], high) + (
        dot(both_low_ref[...], high) + dot(picked_ref[...], low)
    )
    grams = near_gram_ref[...] + grams
    packed, tail = pack_half(images)
    curvature = grams[:size]
    pair, diagonal = pack_pair(0.5 * (curvature + curvature.T), gram_ref[...])
    write_parts(
        position, [pair, grams[size:], packed], [tail, diagonal], payload, keep_ref, send_ref
    )
    mixed_out[...] = grams[size:]
    images_out[...] = images


def image_kernel(near_ref, down_ref, basis_ref, skel_ref, image_ref):
    places = skeleton_columns(skel_ref, near_ref.shape[0])
    high, low = down_ref[0], down_ref[1]
    image_ref[...] = (near_ref[...] + dot(basis_ref[...], high)) + (
        dot(places, high) + dot(places, low)
    )


def pair_up_kernel(
    position_ref, image_ref, residual_ref, image_other, residual_other, transfer_ref, coef_ref
):
    core = position_ref[0] & 1

    @pl.when(core == 0)
    def _():
        up_kernel(0, position_ref, image_ref, image_other, transfer_ref, coef_ref)

    @pl.when(core == 1)
    def _():
        up_kernel(0, position_ref, residual_ref, residual_other, transfer_ref, coef_ref)


def pair_near_kernel(block_ref, image_ref, residual_ref, near_ref):
    block = block_ref[...]
    for at, ref in enumerate((image_ref, residual_ref)):
        value = ref[...]
        high, low = split(value)
        near_ref[at] = 2.0 * value + (dot(block, high) + dot(block, low))


def pair_down_kernel(levels, *refs):
    position_ref, near_ref, image_ref, residual_ref = refs[:4]
    own_refs, other_refs = refs[4 : 3 + levels], refs[3 + levels : 2 + 2 * levels]
    coupling_ref, transfer_ref, basis_ref, skel_ref, applied_ref = refs[2 + 2 * levels :]
    _, count, size = near_ref.shape
    position = position_ref[0]
    core = position & 1
    swap = core == 1
    left, right = image_ref[...], residual_ref[...]
    siblings = [
        jnp.concatenate([jnp.where(swap, right, left), jnp.where(swap, left, right)], 1)
    ]
    for own_ref, other_ref in zip(own_refs, other_refs):
        siblings.append(jnp.concatenate([own_ref[...], other_ref[...]], 1))
    high, low = down_chain(position, levels, coupling_ref, transfer_ref, siblings)
    places = skeleton_columns(skel_ref, count)
    spread = (dot(basis_ref[...], high) + dot(basis_ref[...], low)) + (
        dot(places, high) + dot(places, low)
    )
    applied_ref[core] = near_ref[core] + spread[:, :size]
    applied_ref[1 - core] = near_ref[1 - core] + spread[:, size:]


def scaled_problem(matrix):
    size = matrix.shape[0]
    eye = eye_mask(size)
    picked = jnp.where(eye, matrix, 0.0)
    row_scale = lax.rsqrt(jnp.sum(picked, axis=0, keepdims=True))
    column_scale = lax.rsqrt(jnp.sum(picked, axis=1, keepdims=True))
    scaled = matrix * column_scale * row_scale
    widest = jnp.max(jnp.sum(jnp.abs(scaled), axis=0, keepdims=True), axis=1, keepdims=True)
    return scaled, column_scale, 1.8 / widest


def inverses(matrices, coarse, store):
    count = len(matrices)
    size = matrices[0].shape[0]
    eye = jnp.where(eye_mask(size), 1.0, 0.0)
    problems = [scaled_problem(matrix) for matrix in matrices]
    gaps = [eye - scaled * gain for scaled, _, gain in problems]
    guesses = [(eye + gap) * gain for gap, (_, _, gain) in zip(gaps, problems)]
    for _ in range(coarse):
        for at in range(count):
            rough = gaps[at].astype(BF16)
            gaps[at] = dot(rough, rough)
        for at in range(count):
            guesses[at] = guesses[at] + dot(guesses[at].astype(BF16), gaps[at].astype(BF16))
    total = 0.0
    for at in range(count):
        gap = eye - dot3(problems[at][0], guesses[at])
        guess = guesses[at] + dot3(guesses[at], gap)
        rough = gap.astype(BF16)
        gap = dot(rough, rough)
        store[at] = guess + dot(guess.astype(BF16), gap.astype(BF16))
        total = total + jnp.sum(gap * gap)
    good = total < 0.5

    @pl.when(jnp.logical_not(good))
    def _():
        for at in range(count):
            store[at] = eye * problems[at][2]

    def unfinished(carry):
        step, total = carry
        return (step < MAX_STEPS) & (total > BOUND)

    def refine(carry):
        step, _ = carry
        total = 0.0
        for at in range(count):
            gap = eye - dot_full(problems[at][0], store[at])
            store[at] = store[at] + dot3(store[at], gap)
            total = total + jnp.sum(gap * gap)
        return step + 1, total

    lax.while_loop(unfinished, refine, (0, jnp.where(good, total, 1.0)))
    return [(store[at], problems[at][1]) for at in range(count)]


def collect(position, own_ref, side_ref, core_ref, far_ref, payload):
    quarter = payload.shape[0] // 4
    core, side, _ = sides(position)
    other = sides(position ^ 1)[1]
    for ref, core_at, side_at in (
        (own_ref, core, side),
        (side_ref, core, 1 - side),
        (core_ref, 1 - core, other),
        (far_ref, 1 - core, 1 - other),
    ):
        start = pl.multiple_of((core_at * 2 + side_at) * quarter, 8)
        payload[pl.ds(start, quarter), :] = ref[...]


def fresh_gram(res_gram, mixed, images, alpha):
    bend = dot3(alpha.T, dot3(images, alpha))
    change = 0.5 * bend - dot3(mixed, alpha)
    return res_gram + (change + change.T)


def first_kernel(
    position_ref,
    own_ref,
    side_ref,
    core_ref,
    far_ref,
    image_ref,
    residual_ref,
    applied_ref,
    local_mixed_ref,
    local_images_ref,
    partial_out,
    residual_out,
    keep_out,
    send_out,
    alpha_out,
    beta_out,
    fresh_out,
    mixed_out,
    images_out,
    curvature_out,
    payload,
    later,
    store,
):
    size = image_ref.shape[1]
    position = position_ref[0]
    collect(position, own_ref, side_ref, core_ref, far_ref, payload)
    mixed = payload[size : 2 * size, :]
    base = 2 * size + size // 2
    images = unpack_half(payload[2 * size : base, :], payload[base : base + 1, :])
    curvature, res_gram = unpack_pair(payload[0:size, :], payload[base + 1 : base + 2, :])
    (first, first_scale), (second, second_scale) = inverses([curvature, res_gram], 3, store)
    alpha = dot3(first, res_gram * first_scale) * first_scale
    fresh = fresh_gram(res_gram, mixed, images, alpha)
    beta = dot3(second, fresh * second_scale) * second_scale
    old_image = image_ref[...]
    residual = residual_ref[...] - dot3(old_image, alpha)
    partial = applied_ref[1] - dot3(applied_ref[0], alpha)
    residual_out[...] = residual
    partial_out[...] = partial
    partial_high, partial_low = split(partial)
    old_high, old_low = split(old_image)
    residual_high, residual_low = split(residual)
    both = jnp.concatenate([partial_high, partial_low], 1)
    wide = dot_t(residual_high, both)
    cross_gram = wide[:, :size] + (wide[:, size:] + dot_t(residual_low, partial_high))
    wide = dot_t(partial_high, jnp.concatenate([both, old_high, old_low], 1))
    cross = wide[:, size : 2 * size]
    square = wide[:, :size] + (cross + cross.T)
    old_gram = wide[:, 2 * size : 3 * size] + wide[:, 3 * size :]
    old_gram = old_gram + dot_t(partial_low, old_high)
    local_images = local_images_ref[...]
    old_cross = local_mixed_ref[...] - dot3(alpha.T, local_images)
    cross_gram = cross_gram + dot3(old_cross, beta)
    half = dot3(old_gram, beta) + 0.5 * dot3(beta.T, dot3(local_images, beta))
    packed, tail = pack_half(square + (half + half.T))
    write_parts(position, [cross_gram, packed], [tail], later, keep_out, send_out)
    alpha_out[...] = alpha
    beta_out[...] = beta
    fresh_out[...] = fresh
    mixed_out[...] = mixed
    images_out[...] = images
    curvature_out[...] = curvature


def carry_kernel(
    alpha_ref,
    beta_ref,
    fresh_ref,
    mixed_ref,
    images_ref,
    curvature_ref,
    inverse_out,
    turn_out,
    store,
):
    beta = beta_ref[...]
    ((inverse, scale),) = inverses([fresh_ref[...]], 4, store)
    inverse_out[...] = inverse * scale
    across = mixed_ref[...].T - dot3(images_ref[...], alpha_ref[...])
    across = across + dot3(curvature_ref[...], beta)
    turn = dot3(beta.T, across)
    turn_out[...] = 0.5 * (turn + turn.T)


def update_kernel(
    residual_ref,
    direction_ref,
    solution_ref,
    partial_ref,
    image_ref,
    alpha_ref,
    beta_ref,
    direction_out,
    solution_out,
    image_out,
):
    direction, beta = direction_ref[...], beta_ref[...]
    direction_out[...] = residual_ref[...] + dot3(direction, beta)
    solution_out[...] = solution_ref[...] + dot3(direction, alpha_ref[...])
    image_out[...] = partial_ref[...] + dot3(image_ref[...], beta)


def last_kernel(
    position_ref,
    own_ref,
    side_ref,
    core_ref,
    far_ref,
    image_ref,
    residual_ref,
    direction_ref,
    solution_ref,
    fresh_ref,
    inverse_ref,
    turn_ref,
    solution_out,
    residual_out,
    direction_out,
    payload,
    store,
    solution_held,
    residual_held,
    direction_held,
    sems,
):
    count, size = direction_ref.shape
    collect(position_ref[0], own_ref, side_ref, core_ref, far_ref, payload)
    mixed = payload[0:size, :]
    base = size + size // 2
    images = unpack_half(payload[size:base, :], payload[base : base + 1, :])
    res_gram = fresh_ref[...]
    curvature = 0.5 * (mixed + mixed.T) + turn_ref[...]
    ((first, scale),) = inverses([curvature], 4, store)
    alpha = dot3(first, res_gram * scale) * scale
    residual_held[...] = residual_ref[...] - dot3(image_ref[...], alpha)
    copies = [pltpu.make_async_copy(residual_held, residual_out, sems.at[0])]
    copies[0].start()
    solution_held[...] = solution_ref[...] + dot3(direction_ref[...], alpha)
    copies.append(pltpu.make_async_copy(solution_held, solution_out, sems.at[1]))
    copies[1].start()
    fresh = fresh_gram(res_gram, mixed, images, alpha)
    picked = jnp.where(eye_mask(size), res_gram, 0.0)
    column_scale = lax.rsqrt(jnp.sum(picked, axis=1, keepdims=True))
    beta = dot3(inverse_ref[...], fresh * column_scale)
    strip = count // 4
    for at in range(4):
        rows = pl.ds(at * strip, strip)
        direction_held[rows, :] = residual_held[rows, :] + dot3(direction_ref[rows, :], beta)
        copy = pltpu.make_async_copy(
            direction_held.at[rows, :], direction_out.at[rows, :], sems.at[2 + at]
        )
        copy.start()
        copies.append(copy)
    for copy in copies:
        copy.wait()


def call(kernel, name, inputs, outputs, scratch=(), micros=1.0, limit=32, unused=0, apart=False):
    specs = [SMEM if value.dtype == jnp.int32 and value.shape == (1,) else VMEM for value in inputs]
    specs[len(specs) - unused :] = [ANY] * unused
    return pl.pallas_call(
        kernel,
        name=name,
        in_specs=specs,
        out_specs=[ANY if apart else VMEM] * len(outputs),
        out_shape=[jax.ShapeDtypeStruct(shape, dtype) for shape, dtype in outputs],
        scratch_shapes=list(scratch),
        cost_estimate=pl.CostEstimate(
            flops=int(micros * 1.1e9), bytes_accessed=0, transcendentals=0
        ),
        compiler_params=pltpu.CompilerParams(vmem_limit_bytes=limit * 2**20),
    )(*inputs)


def swapped(value, distance, other=None):
    masks = (2**distance, 2 ** (distance if other is None else other))
    pairs = [(source, source ^ masks[source & 1]) for source in range(lax.axis_size("leaf"))]
    return lax.ppermute(value, "leaf", pairs)


def add_kernel(left_ref, right_ref, *rest):
    rest[-1][...] = left_ref[...] + right_ref[...]


def plus(left, right, after):
    if not after:
        return left + right
    result = (left.shape, F32)
    return call(add_kernel, "add", [left, right, *after], [result], micros=0.2, unused=len(after))[0]


def summed(keep, send, levels, afters=((), ())):
    quarter = keep.shape[0] // 2
    half = keep + swapped(send, 0)
    own = half[:quarter] + swapped(half[quarter:], 1, 2)
    for level in range(3, levels):
        own = plus(own, swapped(own, level), afters[0] if level == 3 else ())
    own = plus(own, swapped(own, 2, 1), afters[1])
    side = swapped(own, 1, 2)
    return [own, side, swapped(own, 0), swapped(side, 0)]


def body(points, leaf_order, skeleton, basis, transfer, coupling, solution, residual, direction):
    levels = lax.axis_size("leaf").bit_length() - 1
    count, size = direction.shape
    rank = basis.shape[1]
    position = lax.axis_index("leaf").astype(jnp.int32).reshape(1)
    order = leaf_order.reshape(1, count)
    tall = ((count, size), F32)
    square = ((size, size), F32)
    coef = ((rank, size), BF16)
    tall_pair = ((2, count, size), F32)
    work = pltpu.VMEM((2, size, size), F32)
    rows, later_rows = payload_rows(size, True), payload_rows(size, False)

    def up(level, current, sibling, extra=()):
        (result,) = call(
            functools.partial(up_kernel, level),
            "up",
            [position, current, sibling, transfer, *extra],
            [coef],
            micros=0.3,
            unused=len(extra),
        )
        return result

    held = pltpu.VMEM((count, size), F32)
    (current,) = call(
        coef_kernel, "coef", [direction, basis, skeleton], [coef], micros=2.7, limit=60
    )
    siblings = [swapped(current, 0)]
    (current,) = call(hold_kernel, "hold", [current], [coef], micros=0.5)
    current = up(0, current, siblings[0])
    siblings.append(swapped(current, 1))
    (block,) = call(
        block_kernel,
        "block",
        [points, order, current],
        [((count, count), BF16)],
        [pltpu.VMEM((8, count), F32), pltpu.VMEM((count, 128), F32)],
        micros=3.6,
        unused=1,
    )
    (near,) = call(near_kernel, "near", [block, direction], [tall], micros=0.7)
    high, low, gram = call(
        prepare_kernel,
        "prepare",
        [direction, residual],
        [((2 * size, count), BF16), ((2 * size, count), BF16), square],
        micros=0.8,
    )
    afters = {1: [block], 2: [near, high]}
    for level in range(1, levels - 1):
        current = up(level, current, siblings[level], afters.get(level, ()))
        siblings.append(swapped(current, level + 1))
    double, double_low = ((2 * size, rank), F32), ((2 * size, rank), BF16)
    factors = call(
        factor_kernel,
        "factor",
        [near, high, low, basis, skeleton],
        [((2 * size, size), F32), square, double_low, double_low, double_low]
        + [((rank, size), F32), ((rank, size), F32)]
        + [((rank, rank), BF16)] * 3
        + [coef],
        micros=3.0,
    )
    residual_coef = factors[-1]
    down, image_coef, keep, send, local_mixed, local_images = call(
        functools.partial(down_kernel, levels),
        "down",
        [position, *siblings, coupling, transfer, *factors[:-1], gram],
        [((2, rank, size), BF16), coef, ((rows // 2, size), F32), ((rows // 2, size), F32)]
        + [square, square],
        [pltpu.VMEM((rows, size), F32)],
        micros=2.0,
    )

    pieces = [position] + summed(keep, send, levels)
    (image,) = call(image_kernel, "image", [near, down, basis, skeleton], [tall], micros=0.7)
    others = [swapped(image_coef, 0), swapped(residual_coef, 0)]
    (current,) = call(
        pair_up_kernel,
        "pair_up",
        [position, image_coef, residual_coef, *others, transfer],
        [coef],
        micros=0.3,
    )
    (near,) = call(
        pair_near_kernel, "pair_near", [block, image, residual], [tall_pair], micros=2.0
    )
    own = []
    for level in range(1, levels):
        own.append(swapped(current, level))
        if level < levels - 1:
            current = up(level, current, own[-1], [near] if level == 1 else ())
    other = [swapped(value, 0) for value in own]
    (applied,) = call(
        functools.partial(pair_down_kernel, levels),
        "pair_down",
        [position, near, *others, *own, *other, coupling, transfer, basis, skeleton],
        [tall_pair],
        micros=2.5,
    )

    partial, residual, keep, send, alpha, beta, fresh, mixed, images, curvature = call(
        first_kernel,
        "first",
        pieces + [image, residual, applied, local_mixed, local_images],
        [tall, tall, ((later_rows // 2, size), F32), ((later_rows // 2, size), F32)] + [square] * 6,
        [pltpu.VMEM((rows, size), F32), pltpu.VMEM((later_rows, size), F32), work],
        micros=7.0,
    )
    inverse, turn = call(
        carry_kernel,
        "carry",
        [alpha, beta, fresh, mixed, images, curvature],
        [square, square],
        [work],
        micros=3.0,
    )
    direction, solution, image = call(
        update_kernel,
        "update",
        [residual, direction, solution, partial, image, alpha, beta],
        [tall, tall, tall],
        micros=1.5,
    )
    pieces = [position] + summed(keep, send, levels, ((inverse,), (direction,)))
    return tuple(
        call(
            last_kernel,
            "last",
            pieces + [image, residual, direction, solution, fresh, inverse, turn],
            [tall, tall, tall],
            [pltpu.VMEM((later_rows, size), F32), work]
            + [held] * 3
            + [pltpu.SemaphoreType.DMA((6,))],
            micros=7.0,
            apart=True,
        )
    )


def solution(mesh):
    placed = (
        P(None, ("groups", "leaf")),
        P(("groups", "leaf")),
        P(("groups", "leaf"), None),
        P(("groups", "leaf"), None),
        P(("groups", "leaf"), None, None, None),
        P(("groups", "leaf"), None, None, None),
        P(("groups", "leaf"), None),
        P(("groups", "leaf"), None),
        P(("groups", "leaf"), None),
    )
    return jax.shard_map(
        body,
        mesh=mesh,
        in_specs=placed,
        out_specs=(
            P(("groups", "leaf"), None),
            P(("groups", "leaf"), None),
            P(("groups", "leaf"), None),
        ),
        check_vma=False,
    )
```

```python
import functools

import jax
import jax.numpy as jnp
from jax import lax
from jax.experimental import pallas as pl
from jax.experimental.pallas import tpu as pltpu
from jax.sharding import PartitionSpec as P

F32 = jnp.float32
BF16 = jnp.bfloat16
VMEM = pl.BlockSpec(memory_space=pltpu.VMEM)
SMEM = pl.BlockSpec(memory_space=pltpu.SMEM)
ANY = pl.BlockSpec(memory_space=pl.ANY)
MAX_STEPS = 60
BOUND = 1e-5


def dot(left, right):
    return jnp.dot(left, right, preferred_element_type=F32)


def dot_t(left, right):
    return lax.dot_general(left, right, (((0,), (0,)), ((), ())), preferred_element_type=F32)


def split(value):
    high = value.astype(BF16)
    return high, (value - high.astype(F32)).astype(BF16)


def dot3(left, right):
    lh, ll = split(left)
    rh, rl = split(right)
    return dot(lh, rh) + (dot(lh, rl) + dot(ll, rh))


def dot_full(left, right):
    return jnp.dot(left, right, precision=lax.Precision.HIGHEST, preferred_element_type=F32)


def iotas(rows, columns):
    return (
        lax.broadcasted_iota(jnp.int32, (rows, columns), 0),
        lax.broadcasted_iota(jnp.int32, (rows, columns), 1),
    )


def eye_mask(size):
    row, column = iotas(size, size)
    return row == column


def skeleton_columns(skel_ref, count):
    row, _ = iotas(count, skel_ref.shape[1])
    return jnp.where(row == skel_ref[...], 1.0, 0.0).astype(BF16)


def skeleton_rows(skel_ref, count):
    rank = skel_ref.shape[1]
    wide = jnp.broadcast_to(skel_ref[...].astype(F32), (128, rank)).T
    column = lax.broadcasted_iota(jnp.int32, (rank, 128), 1).astype(F32)
    tiles = [
        jnp.where(wide == column + float(start), 1.0, 0.0).astype(BF16)
        for start in range(0, count, 128)
    ]
    return jnp.concatenate(tiles, 1)


def coef_kernel(direction_ref, basis_ref, skel_ref, coef_ref):
    high, low = split(direction_ref[...])
    picks = skeleton_rows(skel_ref, direction_ref.shape[0])
    coef = dot_t(basis_ref[...], high) + (dot(picks, high) + dot(picks, low))
    coef_ref[...] = coef.astype(BF16)


def hold_kernel(value_ref, *rest):
    rest[-1][...] = value_ref[...]


def block_kernel(points_ref, order_ref, after_ref, block_ref, padded, column_ref):
    count = points_ref.shape[1]
    padded[...] = jnp.zeros_like(padded)
    padded[0:3, :] = points_ref[...]
    raw = padded[...]
    high = raw.astype(BF16).astype(F32)
    middle = (raw - high).astype(BF16).astype(F32)
    low = raw - high - middle
    parts = jnp.concatenate([high, middle, low], 0).astype(BF16)
    row, _ = iotas(count, count)
    picks = jnp.where(row == order_ref[...], 1.0, 0.0).astype(BF16)
    ordered = dot(parts, picks)
    ordered = (ordered[0:8] + ordered[8:16] + ordered[16:24]) * (300.0**0.5)
    column_ref[...] = jnp.concatenate([ordered, jnp.zeros((120, count), F32)], 0).T
    strip = 128

    def step(index, carry):
        start = pl.multiple_of(index * strip, strip)
        mine = column_ref[pl.ds(start, strip), :]
        square = 1e-10
        for axis in range(3):
            gap = mine[:, axis : axis + 1] - ordered[axis : axis + 1, :]
            square = gap * gap + square
        scaled = square * lax.rsqrt(square)
        values = ((1.0 + scaled) * jnp.exp(-scaled)).astype(BF16)
        block_ref[pl.ds(start, strip), :] = values
        return carry

    lax.fori_loop(0, count // strip, step, 0)

def near_kernel(block_ref, direction_ref, near_ref):
    low_direction = direction_ref[...].astype(BF16)
    near_ref[...] = dot(block_ref[...], low_direction) + 2.0 * low_direction.astype(F32)


def turned_splits(value, high_ref, low_ref, start):
    size = value.shape[1]
    high, low = split(value)
    high_ref[start : start + size, :] = high.T
    low_ref[start : start + size, :] = low.T
    return high, low


def prepare_kernel(direction_ref, residual_ref, after_ref, high_ref, low_ref, gram_ref):
    size = direction_ref.shape[1]
    turned_splits(direction_ref[...], high_ref, low_ref, 0)
    high, low = turned_splits(residual_ref[...], high_ref, low_ref, size)
    both = dot(high_ref[size:, :], jnp.concatenate([high, low], 1))
    cross = both[:, size:]
    gram_ref[...] = both[:, :size] + (cross + cross.T)


def up_kernel(level, position_ref, current_ref, sibling_ref, transfer_ref, *rest):
    coef_ref = rest[-1]
    rank = current_ref.shape[0]
    right = (position_ref[0] >> level) & 1
    mine = transfer_ref[0, level, pl.ds(pl.multiple_of(right * rank, rank), rank), :]
    other = transfer_ref[0, level, pl.ds(pl.multiple_of((1 - right) * rank, rank), rank), :]
    coef_ref[...] = (
        dot_t(mine, current_ref[...]) + dot_t(other, sibling_ref[...])
    ).astype(BF16)


def half_up_kernel(position_ref, current_ref, sibling_ref, transfer_ref, *rest):
    whole, coef_ref = rest[-1], rest[-2]
    up_kernel(0, position_ref, current_ref, sibling_ref, transfer_ref, whole)
    half = coef_ref.shape[1]
    value = whole[...]
    odd = (position_ref[0] & 1) == 1
    coef_ref[...] = jnp.where(odd, value[:, half:], value[:, :half])


def joined(odd, own, other):
    return jnp.concatenate([jnp.where(odd, other, own), jnp.where(odd, own, other)], 1)


def pack_pair(first, second):
    size = first.shape[0]
    row, column = iotas(size, size)
    diagonal = jnp.sum(jnp.where(row == column, second, 0.0), axis=0, keepdims=True)
    return jnp.where(row >= column, first, second), diagonal


def unpack_pair(packed, diagonal):
    size = packed.shape[0]
    row, column = iotas(size, size)
    turned = packed.T
    first = jnp.where(row >= column, packed, turned)
    second = jnp.where(row < column, packed, turned)
    return first, jnp.where(row == column, diagonal, second)


def pack_half(matrix):
    half = matrix.shape[0] // 2
    corner, tail = pack_pair(matrix[:half, :half], matrix[half:, half:])
    return jnp.concatenate([matrix[half:, :half], corner], 1), jnp.concatenate([tail, tail], 1)


def unpack_half(packed, tail):
    half = packed.shape[0]
    upper, lower = unpack_pair(packed[:, half:], tail[:, :half])
    corner = packed[:, :half]
    return jnp.concatenate(
        [jnp.concatenate([upper, corner.T], 1), jnp.concatenate([corner, lower], 1)], 0
    )


def payload_rows(size, with_start):
    rows = size + size // 2 + 8 + (size if with_start else 0)
    return -(-rows // 32) * 32


def sides(position):
    core = position & 1
    return core, (position >> (1 + core)) & 1, (position >> (2 - core)) & 1


def write_parts(position, blocks, rows, payload, keep_ref, send_ref):
    base = 0
    for block in blocks:
        payload[base : base + block.shape[0], :] = block
        base += block.shape[0]
    payload[base:, :] = jnp.zeros((payload.shape[0] - base, payload.shape[1]), F32)
    for at, row in enumerate(rows):
        payload[base + at : base + at + 1, :] = row
    quarter = payload.shape[0] // 4
    core, side, _ = sides(position)
    other = sides(position ^ 1)[1]

    def part(core_at, side_at):
        start = pl.multiple_of((core_at * 2 + side_at) * quarter, 8)
        return payload[pl.ds(start, quarter), :]

    keep_ref[0:quarter, :] = part(core, side)
    keep_ref[quarter:, :] = part(core, 1 - side)
    send_ref[0:quarter, :] = part(1 - core, other)
    send_ref[quarter:, :] = part(1 - core, 1 - other)


def down_chain(position, levels, coupling_ref, transfer_ref, siblings):
    rank = coupling_ref.shape[2]
    down = dot(coupling_ref[0, levels - 1], siblings[levels - 1])
    for level in reversed(range(levels - 1)):
        right = (position >> level) & 1
        half = transfer_ref[0, level, pl.ds(pl.multiple_of(right * rank, rank), rank), :]
        high, low = split(down)
        down = dot(coupling_ref[0, level], siblings[level]) + (dot(half, high) + dot(half, low))
    return split(down)


def factor_kernel(
    high_ref,
    low_ref,
    basis_ref,
    skel_ref,
    after_ref,
    both_high_out,
    both_low_out,
    picked_out,
    ties_high_out,
    ties_low_out,
    basis_picked_out,
    coef_out,
):
    count, rank = basis_ref.shape
    high, low = high_ref[...], low_ref[...]
    size = high.shape[0] // 2
    basis = basis_ref[...]
    places, picks = skeleton_columns(skel_ref, count), skeleton_rows(skel_ref, count)
    picked = dot(high, places) + dot(low, places)
    picked_out[...] = picked.astype(BF16)
    both = picked + (dot(high, basis) + dot(low, basis))
    both_high_out[...], both_low_out[...] = split(both)
    coef_out[...] = both[size:].T.astype(BF16)
    basis_picked = dot(picks, basis)
    basis_picked_out[...] = basis_picked.astype(BF16)
    ties = dot_t(basis, basis) + (basis_picked + basis_picked.T)
    ties_high_out[...], ties_low_out[...] = split(ties)


def near_factor_kernel(
    near_ref,
    high_ref,
    low_ref,
    basis_ref,
    skel_ref,
    near_gram_out,
    near_square_out,
    near_both_out,
    near_picked_out,
):
    count, size = near_ref.shape
    near_high, near_low = split(near_ref[...])
    near_parts = jnp.concatenate([near_high, near_low], 1)
    wide = dot(high_ref[...], near_parts)
    near_gram_out[...] = wide[:, :size] + (wide[:, size:] + dot(low_ref[...], near_high))
    wide = dot_t(near_high, near_parts)
    cross = wide[:, size:]
    near_square_out[...] = wide[:, :size] + (cross + cross.T)
    wide = dot(skeleton_rows(skel_ref, count), near_parts)
    near_picked = wide[:, :size] + wide[:, size:]
    near_picked_out[...] = near_picked
    wide = dot_t(basis_ref[...], near_parts)
    near_both_out[...] = near_picked + (wide[:, :size] + wide[:, size:])


def down_kernel(levels, *refs):
    position_ref = refs[0]
    odd = (position_ref[0] & 1) == 1
    siblings = [refs[1][...]]
    for at in range(2, 1 + levels):
        siblings.append(joined(odd, refs[at][...], refs[at + levels - 1][...]))
    (
        coupling_ref,
        transfer_ref,
        near_gram_ref,
        near_square_ref,
        near_both_ref,
        near_picked_ref,
        both_high_ref,
        both_low_ref,
        picked_ref,
        ties_high_ref,
        ties_low_ref,
        basis_picked_ref,
        gram_ref,
        down_out,
        coef_out,
        image_both_out,
        keep_ref,
        send_ref,
        mixed_out,
        images_out,
        payload,
    ) = refs[2 * levels :]
    size = gram_ref.shape[1]
    position = position_ref[0]
    high, low = down_chain(position, levels, coupling_ref, transfer_ref, siblings)
    down_out[0], down_out[1] = high, low
    down = high.astype(F32) + low.astype(F32)
    picked = dot(basis_picked_ref[...], high) + down
    change = dot(ties_high_ref[...], high) + dot(ties_low_ref[...], high)
    change = change + (dot_t(basis_picked_ref[...], low) + down)
    near_both = near_both_ref[...]
    coef_out[...] = (near_both + change).astype(BF16)
    image_both_out[0], image_both_out[1] = split(near_both + change)
    half_high, half_low = split(near_both + 0.5 * change)
    other = (near_picked_ref[...] + 0.5 * picked).astype(BF16)
    half = dot_t(high, half_high) + (dot_t(high, half_low) + dot_t(low, other))
    images = near_square_ref[...] + (half + half.T)
    grams = dot(both_high_ref[...], high) + (
        dot(both_low_ref[...], high) + dot(picked_ref[...], low)
    )
    grams = near_gram_ref[...] + grams
    packed, tail = pack_half(images)
    curvature = grams[:size]
    pair, diagonal = pack_pair(0.5 * (curvature + curvature.T), gram_ref[...])
    write_parts(
        position, [pair, grams[size:], packed], [tail, diagonal], payload, keep_ref, send_ref
    )
    mixed_out[...] = grams[size:]
    images_out[...] = images


def image_kernel(near_ref, down_ref, basis_ref, skel_ref, image_ref):
    places = skeleton_columns(skel_ref, near_ref.shape[0])
    high, low = down_ref[0], down_ref[1]
    image_ref[...] = (near_ref[...] + dot(basis_ref[...], high)) + (
        dot(places, high) + dot(places, low)
    )


def pair_up_kernel(
    position_ref, image_ref, residual_ref, image_other, residual_other, transfer_ref, coef_ref
):
    core = position_ref[0] & 1

    @pl.when(core == 0)
    def _():
        up_kernel(0, position_ref, image_ref, image_other, transfer_ref, coef_ref)

    @pl.when(core == 1)
    def _():
        up_kernel(0, position_ref, residual_ref, residual_other, transfer_ref, coef_ref)


def pair_near_kernel(block_ref, image_ref, residual_ref, near_ref):
    block = block_ref[...]
    for at, ref in enumerate((image_ref, residual_ref)):
        value = ref[...]
        high, low = split(value)
        near_ref[at] = 2.0 * value + (dot(block, high) + dot(block, low))


def pair_cross_kernel(near_ref, image_ref, high_ref, low_ref, after_ref, cross_out):
    size = image_ref.shape[1]
    near_high, near_low = split(jnp.concatenate([near_ref[0], near_ref[1]], 1))
    high, low = high_ref[size:, :], low_ref[size:, :]
    cross_out[0:size, :] = dot(high, near_high) + (dot(high, near_low) + dot(low, near_high))
    high, low = split(image_ref[...])
    cross_out[size:, :] = dot_t(high, near_high) + (dot_t(high, near_low) + dot_t(low, near_high))


def pair_square_kernel(near_ref, basis_ref, skel_ref, after_ref, square_out, both_out):
    width = 2 * near_ref.shape[2]
    high, low = split(jnp.concatenate([near_ref[0], near_ref[1]], 1))
    parts = jnp.concatenate([high, low], 1)
    wide = dot_t(high, parts)
    cross = wide[:, width:]
    square_out[...] = wide[:, :width] + (cross + cross.T)
    wide = dot_t(basis_ref[...], parts) + dot(skeleton_rows(skel_ref, near_ref.shape[1]), parts)
    both_out[...] = wide[:, :width] + wide[:, width:]


def pair_down_kernel(levels, *refs):
    position_ref, image_other, residual_other = refs[:3]
    own_refs, other_refs = refs[3 : 2 + levels], refs[2 + levels : 1 + 2 * levels]
    (
        coupling_ref,
        transfer_ref,
        cross_ref,
        square_ref,
        near_both_ref,
        both_high_ref,
        both_low_ref,
        image_both_ref,
        ties_high_ref,
        ties_low_ref,
        mixed_ref,
        images_ref,
        down_out,
        alpha_out,
        base_out,
        beta_out,
    ) = refs[1 + 2 * levels :]
    size = mixed_ref.shape[0]
    position = position_ref[0]
    odd = (position & 1) == 1
    siblings = [jnp.concatenate([image_other[...], residual_other[...]], 1)]
    for own_ref, other_ref in zip(own_refs, other_refs):
        siblings.append(joined(odd, own_ref[...], other_ref[...]))
    high, low = down_chain(position, levels, coupling_ref, transfer_ref, siblings)
    down_out[0], down_out[1] = high, low

    def by(matrix_dot, first_high, first_low):
        return matrix_dot(first_high, high) + (
            matrix_dot(first_low, high) + matrix_dot(first_high, low)
        )

    residual_row = cross_ref[0:size, :] + by(dot, both_high_ref[size:, :], both_low_ref[size:, :])
    image_row = cross_ref[size:, :] + by(dot_t, image_both_ref[0], image_both_ref[1])
    tied = by(dot, ties_high_ref[...], ties_low_ref[...])
    tied = tied + (high.astype(F32) + low.astype(F32))
    half_high, half_low = split(near_both_ref[...] + 0.5 * tied)
    half = dot_t(high, half_high) + (dot_t(high, half_low) + dot_t(low, half_high))
    square = square_ref[...] + (half + half.T)
    alpha_out[0:size, :] = residual_row[:, :size]
    alpha_out[size : 2 * size, :] = image_row[:, :size]
    alpha_out[2 * size : 3 * size, :] = square[size:, :size]
    alpha_out[3 * size :, :] = square[:size, :size]
    base_out[0:size, :] = residual_row[:, size:]
    base_out[size : 2 * size, :] = image_row[:, size:]
    base_out[2 * size : 3 * size, :] = square[size:, size:]
    base_out[3 * size :, :] = square[:size, size:]
    beta_out[0:size, :] = mixed_ref[...]
    beta_out[size : 2 * size, :] = images_ref[...]
    beta_out[2 * size : 3 * size, :] = image_row[:, size:].T
    beta_out[3 * size :, :] = image_row[:, :size].T


def scaled_problem(matrix):
    size = matrix.shape[0]
    eye = eye_mask(size)
    picked = jnp.where(eye, matrix, 0.0)
    row_scale = lax.rsqrt(jnp.sum(picked, axis=0, keepdims=True))
    column_scale = lax.rsqrt(jnp.sum(picked, axis=1, keepdims=True))
    scaled = matrix * column_scale * row_scale
    widest = jnp.max(jnp.sum(jnp.abs(scaled), axis=0, keepdims=True), axis=1, keepdims=True)
    return scaled, column_scale, 1.8 / widest


def inverses(matrices, coarse, store):
    count = len(matrices)
    size = matrices[0].shape[0]
    eye = jnp.where(eye_mask(size), 1.0, 0.0)
    problems = [scaled_problem(matrix) for matrix in matrices]
    gaps = [eye - scaled * gain for scaled, _, gain in problems]
    guesses = [(eye + gap) * gain for gap, (_, _, gain) in zip(gaps, problems)]
    for _ in range(coarse):
        for at in range(count):
            rough = gaps[at].astype(BF16)
            gaps[at] = dot(rough, rough)
        for at in range(count):
            guesses[at] = guesses[at] + dot(guesses[at].astype(BF16), gaps[at].astype(BF16))
    total = 0.0
    for at in range(count):
        gap = eye - dot3(problems[at][0], guesses[at])
        guess = guesses[at] + dot3(guesses[at], gap)
        rough = gap.astype(BF16)
        gap = dot(rough, rough)
        store[at] = guess + dot(guess.astype(BF16), gap.astype(BF16))
        total = total + jnp.sum(gap * gap)
    good = total < 0.5

    @pl.when(jnp.logical_not(good))
    def _():
        for at in range(count):
            store[at] = eye * problems[at][2]

    def unfinished(carry):
        step, total = carry
        return (step < MAX_STEPS) & (total > BOUND)

    def refine(carry):
        step, _ = carry
        total = 0.0
        for at in range(count):
            gap = eye - dot_full(problems[at][0], store[at])
            store[at] = store[at] + dot3(store[at], gap)
            total = total + jnp.sum(gap * gap)
        return step + 1, total

    lax.while_loop(unfinished, refine, (0, jnp.where(good, total, 1.0)))
    return [(store[at], problems[at][1]) for at in range(count)]


def collect(position, own_ref, side_ref, core_ref, far_ref, payload):
    quarter = payload.shape[0] // 4
    core, side, _ = sides(position)
    other = sides(position ^ 1)[1]
    for ref, core_at, side_at in (
        (own_ref, core, side),
        (side_ref, core, 1 - side),
        (core_ref, 1 - core, other),
        (far_ref, 1 - core, 1 - other),
    ):
        start = pl.multiple_of((core_at * 2 + side_at) * quarter, 8)
        payload[pl.ds(start, quarter), :] = ref[...]


def beta_of(alpha, weighted, mixed_turned, inverse, scale, solved_mixed):
    eye = jnp.where(eye_mask(alpha.shape[0]), 1.0, 0.0)
    rest = dot3(inverse, (weighted - mixed_turned) * scale) * scale
    return (eye - dot3(solved_mixed, alpha)) + rest


def first_kernel(
    position_ref,
    own_ref,
    side_ref,
    core_ref,
    far_ref,
    alpha_part_ref,
    base_part_ref,
    beta_part_ref,
    keep_out,
    send_out,
    alpha_out,
    beta_out,
    fresh_out,
    mixed_out,
    images_out,
    curvature_out,
    payload,
    later,
    store,
):
    size = own_ref.shape[1]
    position = position_ref[0]
    collect(position, own_ref, side_ref, core_ref, far_ref, payload)
    mixed = payload[size : 2 * size, :]
    base = 2 * size + size // 2
    images = unpack_half(payload[2 * size : base, :], payload[base : base + 1, :])
    curvature, res_gram = unpack_pair(payload[0:size, :], payload[base + 1 : base + 2, :])
    (first, first_scale), (second, second_scale) = inverses([curvature, res_gram], 3, store)
    alpha = dot3(first, res_gram * first_scale) * first_scale
    solved_mixed = dot3(second, mixed * second_scale) * second_scale
    weighted = dot3(images, alpha)
    beta = beta_of(alpha, weighted, mixed.T, first, first_scale, solved_mixed)
    rows = (base_part_ref[...] - dot3(alpha_part_ref[...], alpha)) + dot3(beta_part_ref[...], beta)
    image_row = rows[size : 2 * size]
    turned = dot3(alpha.T, jnp.concatenate([image_row, rows[3 * size :]], 1))
    square = rows[2 * size : 3 * size] - turned[:, size:] + dot3(beta.T, image_row)
    packed, tail = pack_half(square)
    write_parts(position, [rows[:size] - turned[:, :size], packed], [tail], later, keep_out, send_out)
    change = 0.5 * dot3(alpha.T, weighted) - dot3(mixed, alpha)
    fresh_out[...] = res_gram + (change + change.T)
    alpha_out[...] = alpha
    beta_out[...] = beta
    mixed_out[...] = mixed
    images_out[...] = images
    curvature_out[...] = curvature


def carry_kernel(
    alpha_ref,
    beta_ref,
    fresh_ref,
    mixed_ref,
    images_ref,
    curvature_ref,
    inverse_out,
    turn_out,
    store,
):
    beta = beta_ref[...]
    ((inverse, scale),) = inverses([fresh_ref[...]], 4, store)
    inverse_out[...] = inverse * scale
    across = mixed_ref[...].T - dot3(images_ref[...], alpha_ref[...])
    across = across + dot3(curvature_ref[...], beta)
    turn = dot3(beta.T, across)
    turn_out[...] = 0.5 * (turn + turn.T)


def update_kernel(
    residual_ref,
    direction_ref,
    solution_ref,
    image_ref,
    near_ref,
    down_ref,
    basis_ref,
    skel_ref,
    alpha_ref,
    beta_ref,
    residual_out,
    direction_out,
    solution_out,
    image_out,
):
    count, size = image_ref.shape
    direction, image = direction_ref[...], image_ref[...]
    alpha, beta = alpha_ref[...], beta_ref[...]
    residual = residual_ref[...] - dot3(image, alpha)
    residual_out[...] = residual
    direction_out[...] = residual + dot3(direction, beta)
    solution_out[...] = solution_ref[...] + dot3(direction, alpha)
    down = down_ref[0].astype(F32) + down_ref[1].astype(F32)
    high, low = split(down[:, size:] - dot3(down[:, :size], alpha))
    places, basis = skeleton_columns(skel_ref, count), basis_ref[...]
    far = (dot(basis, high) + dot(basis, low)) + (dot(places, high) + dot(places, low))
    near = near_ref[1] - dot3(near_ref[0], alpha)
    image_out[...] = (near + far) + dot3(image, beta)


def last_kernel(
    position_ref,
    own_ref,
    side_ref,
    core_ref,
    far_ref,
    image_ref,
    residual_ref,
    direction_ref,
    solution_ref,
    fresh_ref,
    inverse_ref,
    turn_ref,
    solution_out,
    residual_out,
    direction_out,
    payload,
    store,
    solution_held,
    residual_held,
    direction_held,
    sems,
):
    count, size = direction_ref.shape
    collect(position_ref[0], own_ref, side_ref, core_ref, far_ref, payload)
    mixed = payload[0:size, :]
    base = size + size // 2
    images = unpack_half(payload[size:base, :], payload[base : base + 1, :])
    res_gram = fresh_ref[...]
    curvature = 0.5 * (mixed + mixed.T) + turn_ref[...]
    picked = jnp.where(eye_mask(size), res_gram, 0.0)
    column_scale = lax.rsqrt(jnp.sum(picked, axis=1, keepdims=True))
    solved_mixed = dot3(inverse_ref[...], mixed * column_scale)
    ((first, scale),) = inverses([curvature], 4, store)
    alpha = dot3(first, res_gram * scale) * scale
    residual_held[...] = residual_ref[...] - dot3(image_ref[...], alpha)
    copies = [pltpu.make_async_copy(residual_held, residual_out, sems.at[0])]
    copies[0].start()
    solution_held[...] = solution_ref[...] + dot3(direction_ref[...], alpha)
    copies.append(pltpu.make_async_copy(solution_held, solution_out, sems.at[1]))
    copies[1].start()
    beta = beta_of(alpha, dot3(images, alpha), mixed.T, first, scale, solved_mixed)
    strip = count // 4
    for at in range(4):
        rows = pl.ds(at * strip, strip)
        direction_held[rows, :] = residual_held[rows, :] + dot3(direction_ref[rows, :], beta)
        copy = pltpu.make_async_copy(
            direction_held.at[rows, :], direction_out.at[rows, :], sems.at[2 + at]
        )
        copy.start()
        copies.append(copy)
    for copy in copies:
        copy.wait()


def call(kernel, name, inputs, outputs, scratch=(), micros=1.0, limit=32, unused=0, apart=False):
    specs = [SMEM if value.dtype == jnp.int32 and value.shape == (1,) else VMEM for value in inputs]
    specs[len(specs) - unused :] = [ANY] * unused
    return pl.pallas_call(
        kernel,
        name=name,
        in_specs=specs,
        out_specs=[ANY if apart else VMEM] * len(outputs),
        out_shape=[jax.ShapeDtypeStruct(shape, dtype) for shape, dtype in outputs],
        scratch_shapes=list(scratch),
        cost_estimate=pl.CostEstimate(
            flops=int(micros * 1.1e9), bytes_accessed=0, transcendentals=0
        ),
        compiler_params=pltpu.CompilerParams(vmem_limit_bytes=limit * 2**20),
    )(*inputs)


def swapped(value, distance, other=None):
    masks = (2**distance, 2 ** (distance if other is None else other))
    pairs = [(source, source ^ masks[source & 1]) for source in range(lax.axis_size("leaf"))]
    return lax.ppermute(value, "leaf", pairs)


def add_kernel(left_ref, right_ref, *rest):
    rest[-1][...] = left_ref[...] + right_ref[...]


def plus(left, right, after):
    if not after:
        return left + right
    result = (left.shape, F32)
    return call(add_kernel, "add", [left, right, *after], [result], micros=0.2, unused=len(after))[0]


def summed(keep, send, levels, afters=((), (), ())):
    quarter = keep.shape[0] // 2
    half = keep + swapped(send, 0)
    own = plus(half[:quarter], swapped(half[quarter:], 1, 2), afters[0])
    for level in range(3, levels):
        own = plus(own, swapped(own, level), afters[1] if level == 3 else ())
    own = plus(own, swapped(own, 2, 1), afters[2])
    side = swapped(own, 1, 2)
    return [own, side, swapped(own, 0), swapped(side, 0)]


def body(points, leaf_order, skeleton, basis, transfer, coupling, solution, residual, direction):
    levels = lax.axis_size("leaf").bit_length() - 1
    count, size = direction.shape
    rank = basis.shape[1]
    position = lax.axis_index("leaf").astype(jnp.int32).reshape(1)
    order = leaf_order.reshape(1, count)
    tall = ((count, size), F32)
    square = ((size, size), F32)
    coef = ((rank, size), BF16)
    tall_pair = ((2, count, size), F32)
    work = pltpu.VMEM((2, size, size), F32)
    rows, later_rows = payload_rows(size, True), payload_rows(size, False)

    def up(level, current, sibling, extra=()):
        (result,) = call(
            functools.partial(up_kernel, level),
            "up",
            [position, current, sibling, transfer, *extra],
            [(current.shape, BF16)],
            micros=0.3,
            unused=len(extra),
        )
        return result

    held = pltpu.VMEM((count, size), F32)
    (current,) = call(
        coef_kernel, "coef", [direction, basis, skeleton], [coef], micros=2.7, limit=60
    )
    siblings = [swapped(current, 0)]
    (current,) = call(hold_kernel, "hold", [current], [coef], micros=0.5)
    (current,) = call(
        half_up_kernel,
        "up",
        [position, current, siblings[0], transfer],
        [((rank, size // 2), BF16)],
        [pltpu.VMEM((rank, size), BF16)],
        micros=0.3,
    )
    siblings.append(swapped(current, 1))
    (block,) = call(
        block_kernel,
        "block",
        [points, order, current],
        [((count, count), BF16)],
        [pltpu.VMEM((8, count), F32), pltpu.VMEM((count, 128), F32)],
        micros=3.6,
        unused=1,
    )
    high, low, gram = call(
        prepare_kernel,
        "prepare",
        [direction, residual, current],
        [((2 * size, count), BF16), ((2 * size, count), BF16), square],
        micros=0.8,
        unused=1,
    )
    current = up(1, current, siblings[1], [block, high])
    siblings.append(swapped(current, 2))
    (near,) = call(near_kernel, "near", [block, direction], [tall], micros=0.7)
    double_low = ((2 * size, rank), BF16)
    factors = call(
        factor_kernel,
        "factor",
        [high, low, basis, skeleton, current],
        [double_low] * 3 + [((rank, rank), BF16)] * 3 + [coef],
        micros=1.8,
        unused=1,
    )
    residual_coef = factors[-1]
    for level in range(2, levels - 1):
        extra = [near, residual_coef] if level == 2 else ()
        current = up(level, current, siblings[level], extra)
        siblings.append(swapped(current, level + 1))
    near_factors = call(
        near_factor_kernel,
        "near_factor",
        [near, high, low, basis, skeleton],
        [((2 * size, size), F32), square, ((rank, size), F32), ((rank, size), F32)],
        micros=1.8,
    )
    (ready,) = call(
        hold_kernel,
        "ready",
        [siblings[-1], near_factors[0]],
        [(siblings[-1].shape, BF16)],
        micros=0.2,
        unused=1,
    )
    siblings += [swapped(value, 0) for value in siblings[1:-1] + [ready]]
    down, image_coef, image_both, keep, send, local_mixed, local_images = call(
        functools.partial(down_kernel, levels),
        "down",
        [position, *siblings, coupling, transfer, *near_factors, *factors[:-1], gram],
        [((2, rank, size), BF16), coef, ((2, rank, size), BF16)]
        + [((rows // 2, size), F32)] * 2
        + [square, square],
        [pltpu.VMEM((rows, size), F32)],
        micros=2.0,
    )

    (image,) = call(image_kernel, "image", [near, down, basis, skeleton], [tall], micros=0.7)
    others = [swapped(image_coef, 0), swapped(residual_coef, 0)]
    (current,) = call(
        pair_up_kernel,
        "pair_up",
        [position, image_coef, residual_coef, *others, transfer],
        [coef],
        micros=0.3,
    )
    pieces = [position] + summed(keep, send, levels, ((current,), (), ()))
    (near,) = call(
        pair_near_kernel,
        "pair_near",
        [block, image, residual],
        [tall_pair],
        micros=2.4,
    )
    own = [swapped(current, 1)]
    current = up(1, current, own[0], [near])
    own.append(swapped(current, 2))
    (cross,) = call(
        pair_cross_kernel,
        "pair_cross",
        [near, image, high, low, current],
        [((2 * size, 2 * size), F32)],
        micros=2.3,
        unused=1,
    )
    for level in range(2, levels - 1):
        current = up(level, current, own[level - 1], [cross] if level == 2 else ())
        own.append(swapped(current, level + 1))
    square_part, near_both = call(
        pair_square_kernel,
        "pair_square",
        [near, basis, skeleton, pieces[1]],
        [((2 * size, 2 * size), F32), ((rank, 2 * size), F32)],
        micros=2.8,
        unused=1,
    )
    (ready,) = call(
        hold_kernel, "ready", [own[-1], near_both], [coef], micros=0.2, unused=1
    )
    other = [swapped(value, 0) for value in own[:-1] + [ready]]
    both_high, both_low, _, ties_high, ties_low, _, _ = factors
    down, alpha_part, base_part, beta_part = call(
        functools.partial(pair_down_kernel, levels),
        "pair_down",
        [position, *others, *own, *other, coupling, transfer, cross, square_part, near_both]
        + [both_high, both_low, image_both, ties_high, ties_low, local_mixed, local_images],
        [((2, rank, 2 * size), BF16)] + [((4 * size, size), F32)] * 3,
        micros=2.5,
    )

    keep, send, alpha, beta, fresh, mixed, images, curvature = call(
        first_kernel,
        "first",
        pieces + [alpha_part, base_part, beta_part],
        [((later_rows // 2, size), F32), ((later_rows // 2, size), F32)] + [square] * 6,
        [pltpu.VMEM((rows, size), F32), pltpu.VMEM((later_rows, size), F32), work],
        micros=5.0,
    )
    inverse, turn = call(
        carry_kernel,
        "carry",
        [alpha, beta, fresh, mixed, images, curvature],
        [square, square],
        [work],
        micros=3.0,
    )
    residual, direction, solution, image = call(
        update_kernel,
        "update",
        [residual, direction, solution, image, near, down, basis, skeleton, alpha, beta],
        [tall] * 4,
        micros=3.2,
    )
    pieces = [position] + summed(keep, send, levels, ((), (inverse,), (direction,)))
    return tuple(
        call(
            last_kernel,
            "last",
            pieces + [image, residual, direction, solution, fresh, inverse, turn],
            [tall, tall, tall],
            [pltpu.VMEM((later_rows, size), F32), work]
            + [held] * 3
            + [pltpu.SemaphoreType.DMA((6,))],
            micros=7.0,
            apart=True,
        )
    )


def solution(mesh):
    placed = (
        P(None, ("groups", "leaf")),
        P(("groups", "leaf")),
        P(("groups", "leaf"), None),
        P(("groups", "leaf"), None),
        P(("groups", "leaf"), None, None, None),
        P(("groups", "leaf"), None, None, None),
        P(("groups", "leaf"), None),
        P(("groups", "leaf"), None),
        P(("groups", "leaf"), None),
    )
    return jax.shard_map(
        body,
        mesh=mesh,
        in_specs=placed,
        out_specs=(
            P(("groups", "leaf"), None),
            P(("groups", "leaf"), None),
            P(("groups", "leaf"), None),
        ),
        check_vma=False,
    )
```

```python
import functools

import jax
import jax.numpy as jnp
from jax import lax
from jax.experimental import pallas as pl
from jax.experimental.pallas import tpu as pltpu
from jax.sharding import PartitionSpec as P

F32 = jnp.float32
BF16 = jnp.bfloat16
VMEM = pl.BlockSpec(memory_space=pltpu.VMEM)
SMEM = pl.BlockSpec(memory_space=pltpu.SMEM)
ANY = pl.BlockSpec(memory_space=pl.ANY)
MAX_STEPS = 60
BOUND = 1e-5


def dot(left, right):
    return jnp.dot(left, right, preferred_element_type=F32)


def dot_t(left, right):
    return lax.dot_general(left, right, (((0,), (0,)), ((), ())), preferred_element_type=F32)


def split(value):
    high = value.astype(BF16)
    return high, (value - high.astype(F32)).astype(BF16)


def dot3(left, right):
    lh, ll = split(left)
    rh, rl = split(right)
    return dot(lh, rh) + (dot(lh, rl) + dot(ll, rh))


def dot_full(left, right):
    return jnp.dot(left, right, precision=lax.Precision.HIGHEST, preferred_element_type=F32)


def iotas(rows, columns):
    return (
        lax.broadcasted_iota(jnp.int32, (rows, columns), 0),
        lax.broadcasted_iota(jnp.int32, (rows, columns), 1),
    )


def eye_mask(size):
    row, column = iotas(size, size)
    return row == column


def skeleton_columns(skel_ref, count):
    row, _ = iotas(count, skel_ref.shape[1])
    return jnp.where(row == skel_ref[...], 1.0, 0.0).astype(BF16)


def skeleton_rows(skel_ref, count):
    rank = skel_ref.shape[1]
    wide = jnp.broadcast_to(skel_ref[...].astype(F32), (128, rank)).T
    column = lax.broadcasted_iota(jnp.int32, (rank, 128), 1).astype(F32)
    tiles = [
        jnp.where(wide == column + float(start), 1.0, 0.0).astype(BF16)
        for start in range(0, count, 128)
    ]
    return jnp.concatenate(tiles, 1)


def coef_kernel(direction_ref, basis_ref, skel_ref, coef_ref):
    high, low = split(direction_ref[...])
    picks = skeleton_rows(skel_ref, direction_ref.shape[0])
    coef = dot_t(basis_ref[...], high) + (dot(picks, high) + dot(picks, low))
    coef_ref[...] = coef.astype(BF16)


def hold_kernel(value_ref, *rest):
    rest[-1][...] = value_ref[...]


def block_kernel(points_ref, order_ref, after_ref, block_ref, padded, column_ref):
    count = points_ref.shape[1]
    padded[...] = jnp.zeros_like(padded)
    padded[0:3, :] = points_ref[...]
    raw = padded[...]
    high = raw.astype(BF16).astype(F32)
    middle = (raw - high).astype(BF16).astype(F32)
    low = raw - high - middle
    parts = jnp.concatenate([high, middle, low], 0).astype(BF16)
    row, _ = iotas(count, count)
    picks = jnp.where(row == order_ref[...], 1.0, 0.0).astype(BF16)
    ordered = dot(parts, picks)
    ordered = (ordered[0:8] + ordered[8:16] + ordered[16:24]) * (300.0**0.5)
    column_ref[...] = jnp.concatenate([ordered, jnp.zeros((120, count), F32)], 0).T
    strip = 128

    def step(index, carry):
        start = pl.multiple_of(index * strip, strip)
        mine = column_ref[pl.ds(start, strip), :]
        square = 1e-10
        for axis in range(3):
            gap = mine[:, axis : axis + 1] - ordered[axis : axis + 1, :]
            square = gap * gap + square
        scaled = square * lax.rsqrt(square)
        values = ((1.0 + scaled) * jnp.exp(-scaled)).astype(BF16)
        block_ref[pl.ds(start, strip), :] = values
        return carry

    lax.fori_loop(0, count // strip, step, 0)

def near_kernel(block_ref, direction_ref, near_ref):
    low_direction = direction_ref[...].astype(BF16)
    near_ref[...] = dot(block_ref[...], low_direction) + 2.0 * low_direction.astype(F32)


def turned_splits(value, high_ref, low_ref, start):
    size = value.shape[1]
    high, low = split(value)
    high_ref[start : start + size, :] = high.T
    low_ref[start : start + size, :] = low.T
    return high, low


def prepare_kernel(direction_ref, residual_ref, after_ref, high_ref, low_ref, gram_ref):
    size = direction_ref.shape[1]
    turned_splits(direction_ref[...], high_ref, low_ref, 0)
    high, low = turned_splits(residual_ref[...], high_ref, low_ref, size)
    both = dot(high_ref[size:, :], jnp.concatenate([high, low], 1))
    cross = both[:, size:]
    gram_ref[...] = both[:, :size] + (cross + cross.T)


def up_kernel(level, position_ref, current_ref, sibling_ref, transfer_ref, *rest):
    coef_ref = rest[-1]
    rank = current_ref.shape[0]
    right = (position_ref[0] >> level) & 1
    mine = transfer_ref[0, level, pl.ds(pl.multiple_of(right * rank, rank), rank), :]
    other = transfer_ref[0, level, pl.ds(pl.multiple_of((1 - right) * rank, rank), rank), :]
    coef_ref[...] = (
        dot_t(mine, current_ref[...]) + dot_t(other, sibling_ref[...])
    ).astype(BF16)


def half_up_kernel(position_ref, current_ref, sibling_ref, transfer_ref, *rest):
    whole, coef_ref = rest[-1], rest[-2]
    up_kernel(0, position_ref, current_ref, sibling_ref, transfer_ref, whole)
    half = coef_ref.shape[1]
    value = whole[...]
    odd = (position_ref[0] & 1) == 1
    coef_ref[...] = jnp.where(odd, value[:, half:], value[:, :half])


def joined(odd, own, other):
    return jnp.concatenate([jnp.where(odd, other, own), jnp.where(odd, own, other)], 1)


def pack_pair(first, second):
    size = first.shape[0]
    row, column = iotas(size, size)
    diagonal = jnp.sum(jnp.where(row == column, second, 0.0), axis=0, keepdims=True)
    return jnp.where(row >= column, first, second), diagonal


def unpack_pair(packed, diagonal):
    size = packed.shape[0]
    row, column = iotas(size, size)
    turned = packed.T
    first = jnp.where(row >= column, packed, turned)
    second = jnp.where(row < column, packed, turned)
    return first, jnp.where(row == column, diagonal, second)


def pack_half(matrix):
    half = matrix.shape[0] // 2
    corner, tail = pack_pair(matrix[:half, :half], matrix[half:, half:])
    return jnp.concatenate([matrix[half:, :half], corner], 1), jnp.concatenate([tail, tail], 1)


def unpack_half(packed, tail):
    half = packed.shape[0]
    upper, lower = unpack_pair(packed[:, half:], tail[:, :half])
    corner = packed[:, :half]
    return jnp.concatenate(
        [jnp.concatenate([upper, corner.T], 1), jnp.concatenate([corner, lower], 1)], 0
    )


def payload_rows(size, with_start):
    rows = size + 8 + (size + size // 2 if with_start else 0)
    return -(-rows // 32) * 32


def sides(position):
    core = position & 1
    return core, (position >> (1 + core)) & 1, (position >> (2 - core)) & 1


def write_parts(position, blocks, rows, payload, keep_ref, send_ref):
    base = 0
    for block in blocks:
        payload[base : base + block.shape[0], :] = block
        base += block.shape[0]
    payload[base:, :] = jnp.zeros((payload.shape[0] - base, payload.shape[1]), F32)
    for at, row in enumerate(rows):
        payload[base + at : base + at + 1, :] = row
    quarter = payload.shape[0] // 4
    core, side, _ = sides(position)
    other = sides(position ^ 1)[1]

    def part(core_at, side_at):
        start = pl.multiple_of((core_at * 2 + side_at) * quarter, 8)
        return payload[pl.ds(start, quarter), :]

    keep_ref[0:quarter, :] = part(core, side)
    keep_ref[quarter:, :] = part(core, 1 - side)
    send_ref[0:quarter, :] = part(1 - core, other)
    send_ref[quarter:, :] = part(1 - core, 1 - other)


def down_chain(position, levels, coupling_ref, transfer_ref, siblings):
    rank = coupling_ref.shape[2]
    down = dot(coupling_ref[0, levels - 1], siblings[levels - 1])
    for level in reversed(range(levels - 1)):
        right = (position >> level) & 1
        half = transfer_ref[0, level, pl.ds(pl.multiple_of(right * rank, rank), rank), :]
        high, low = split(down)
        down = dot(coupling_ref[0, level], siblings[level]) + (dot(half, high) + dot(half, low))
    return split(down)


def factor_kernel(
    high_ref,
    low_ref,
    basis_ref,
    skel_ref,
    after_ref,
    both_high_out,
    both_low_out,
    picked_out,
    ties_high_out,
    ties_low_out,
    basis_picked_out,
    coef_out,
):
    count, rank = basis_ref.shape
    high, low = high_ref[...], low_ref[...]
    size = high.shape[0] // 2
    basis = basis_ref[...]
    places, picks = skeleton_columns(skel_ref, count), skeleton_rows(skel_ref, count)
    picked = dot(high, places) + dot(low, places)
    picked_out[...] = picked.astype(BF16)
    both = picked + (dot(high, basis) + dot(low, basis))
    both_high_out[...], both_low_out[...] = split(both)
    coef_out[...] = both[size:].T.astype(BF16)
    basis_picked = dot(picks, basis)
    basis_picked_out[...] = basis_picked.astype(BF16)
    ties = dot_t(basis, basis) + (basis_picked + basis_picked.T)
    ties_high_out[...], ties_low_out[...] = split(ties)


def near_factor_kernel(
    near_ref,
    high_ref,
    low_ref,
    basis_ref,
    skel_ref,
    near_gram_out,
    near_square_out,
    near_both_out,
    near_picked_out,
):
    count, size = near_ref.shape
    near_high, near_low = split(near_ref[...])
    near_parts = jnp.concatenate([near_high, near_low], 1)
    wide = dot(high_ref[...], near_parts)
    near_gram_out[...] = wide[:, :size] + (wide[:, size:] + dot(low_ref[...], near_high))
    wide = dot_t(near_high, near_parts)
    cross = wide[:, size:]
    near_square_out[...] = wide[:, :size] + (cross + cross.T)
    wide = dot(skeleton_rows(skel_ref, count), near_parts)
    near_picked = wide[:, :size] + wide[:, size:]
    near_picked_out[...] = near_picked
    wide = dot_t(basis_ref[...], near_parts)
    near_both_out[...] = near_picked + (wide[:, :size] + wide[:, size:])


def down_kernel(levels, *refs):
    position_ref = refs[0]
    odd = (position_ref[0] & 1) == 1
    siblings = [refs[1][...]]
    for at in range(2, 1 + levels):
        siblings.append(joined(odd, refs[at][...], refs[at + levels - 1][...]))
    (
        coupling_ref,
        transfer_ref,
        near_gram_ref,
        near_square_ref,
        near_both_ref,
        near_picked_ref,
        both_high_ref,
        both_low_ref,
        picked_ref,
        ties_high_ref,
        ties_low_ref,
        basis_picked_ref,
        gram_ref,
        down_out,
        coef_out,
        image_both_out,
        keep_ref,
        send_ref,
        mixed_out,
        images_out,
        payload,
    ) = refs[2 * levels :]
    size = gram_ref.shape[1]
    position = position_ref[0]
    high, low = down_chain(position, levels, coupling_ref, transfer_ref, siblings)
    down_out[0], down_out[1] = high, low
    down = high.astype(F32) + low.astype(F32)
    picked = dot(basis_picked_ref[...], high) + down
    change = dot(ties_high_ref[...], high) + dot(ties_low_ref[...], high)
    change = change + (dot_t(basis_picked_ref[...], low) + down)
    near_both = near_both_ref[...]
    coef_out[...] = (near_both + change).astype(BF16)
    image_both_out[0], image_both_out[1] = split(near_both + change)
    half_high, half_low = split(near_both + 0.5 * change)
    other = (near_picked_ref[...] + 0.5 * picked).astype(BF16)
    half = dot_t(high, half_high) + (dot_t(high, half_low) + dot_t(low, other))
    images = near_square_ref[...] + (half + half.T)
    grams = dot(both_high_ref[...], high) + (
        dot(both_low_ref[...], high) + dot(picked_ref[...], low)
    )
    grams = near_gram_ref[...] + grams
    packed, tail = pack_half(images)
    curvature = grams[:size]
    pair, diagonal = pack_pair(0.5 * (curvature + curvature.T), gram_ref[...])
    write_parts(
        position, [pair, grams[size:], packed], [tail, diagonal], payload, keep_ref, send_ref
    )
    mixed_out[...] = grams[size:]
    images_out[...] = images


def image_kernel(near_ref, down_ref, basis_ref, skel_ref, image_ref):
    places = skeleton_columns(skel_ref, near_ref.shape[0])
    high, low = down_ref[0], down_ref[1]
    image_ref[...] = (near_ref[...] + dot(basis_ref[...], high)) + (
        dot(places, high) + dot(places, low)
    )


def pair_up_kernel(
    position_ref, image_ref, residual_ref, image_other, residual_other, transfer_ref, coef_ref
):
    core = position_ref[0] & 1

    @pl.when(core == 0)
    def _():
        up_kernel(0, position_ref, image_ref, image_other, transfer_ref, coef_ref)

    @pl.when(core == 1)
    def _():
        up_kernel(0, position_ref, residual_ref, residual_other, transfer_ref, coef_ref)


def pair_near_kernel(block_ref, image_ref, residual_ref, near_ref):
    block = block_ref[...]
    for at, ref in enumerate((image_ref, residual_ref)):
        value = ref[...]
        high, low = split(value)
        near_ref[at] = 2.0 * value + (dot(block, high) + dot(block, low))


def pair_cross_kernel(near_ref, image_ref, high_ref, low_ref, after_ref, cross_out):
    size = image_ref.shape[1]
    near_high, near_low = split(jnp.concatenate([near_ref[0], near_ref[1]], 1))
    high, low = high_ref[size:, :], low_ref[size:, :]
    cross_out[0:size, :] = dot(high, near_high) + (dot(high, near_low) + dot(low, near_high))
    high, low = split(image_ref[...])
    cross_out[size:, :] = dot_t(high, near_high) + (dot_t(high, near_low) + dot_t(low, near_high))


def pair_square_kernel(near_ref, basis_ref, skel_ref, after_ref, square_out, both_out):
    width = 2 * near_ref.shape[2]
    high, low = split(jnp.concatenate([near_ref[0], near_ref[1]], 1))
    parts = jnp.concatenate([high, low], 1)
    wide = dot_t(high, parts)
    cross = wide[:, width:]
    square_out[...] = wide[:, :width] + (cross + cross.T)
    wide = dot_t(basis_ref[...], parts) + dot(skeleton_rows(skel_ref, near_ref.shape[1]), parts)
    both_out[...] = wide[:, :width] + wide[:, width:]


def pair_down_kernel(levels, *refs):
    position_ref, image_other, residual_other = refs[:3]
    own_refs, other_refs = refs[3 : 2 + levels], refs[2 + levels : 1 + 2 * levels]
    (
        coupling_ref,
        transfer_ref,
        cross_ref,
        square_ref,
        near_both_ref,
        both_high_ref,
        both_low_ref,
        image_both_ref,
        ties_high_ref,
        ties_low_ref,
        mixed_ref,
        images_ref,
        down_out,
        alpha_out,
        base_out,
        beta_out,
    ) = refs[1 + 2 * levels :]
    size = mixed_ref.shape[0]
    position = position_ref[0]
    odd = (position & 1) == 1
    siblings = [jnp.concatenate([image_other[...], residual_other[...]], 1)]
    for own_ref, other_ref in zip(own_refs, other_refs):
        siblings.append(joined(odd, own_ref[...], other_ref[...]))
    high, low = down_chain(position, levels, coupling_ref, transfer_ref, siblings)
    down_out[0], down_out[1] = high, low

    def by(matrix_dot, first_high, first_low):
        return matrix_dot(first_high, high) + (
            matrix_dot(first_low, high) + matrix_dot(first_high, low)
        )

    residual_row = cross_ref[0:size, :] + by(dot, both_high_ref[size:, :], both_low_ref[size:, :])
    image_row = cross_ref[size:, :] + by(dot_t, image_both_ref[0], image_both_ref[1])
    tied = by(dot, ties_high_ref[...], ties_low_ref[...])
    tied = tied + (high.astype(F32) + low.astype(F32))
    half_high, half_low = split(near_both_ref[...] + 0.5 * tied)
    half = dot_t(high, half_high) + (dot_t(high, half_low) + dot_t(low, half_high))
    square = square_ref[...] + (half + half.T)
    alpha_out[0:size, :] = residual_row[:, :size]
    alpha_out[size : 2 * size, :] = image_row[:, :size]
    alpha_out[2 * size : 3 * size, :] = square[size:, :size]
    alpha_out[3 * size :, :] = square[:size, :size]
    base_out[0:size, :] = residual_row[:, size:]
    base_out[size : 2 * size, :] = image_row[:, size:]
    base_out[2 * size : 3 * size, :] = square[size:, size:]
    base_out[3 * size :, :] = square[:size, size:]
    beta_out[0:size, :] = mixed_ref[...]
    beta_out[size : 2 * size, :] = images_ref[...]
    beta_out[2 * size : 3 * size, :] = image_row[:, size:].T
    beta_out[3 * size :, :] = image_row[:, :size].T


def scaled_problem(matrix):
    size = matrix.shape[0]
    eye = eye_mask(size)
    picked = jnp.where(eye, matrix, 0.0)
    row_scale = lax.rsqrt(jnp.sum(picked, axis=0, keepdims=True))
    column_scale = lax.rsqrt(jnp.sum(picked, axis=1, keepdims=True))
    scaled = matrix * column_scale * row_scale
    widest = jnp.max(jnp.sum(jnp.abs(scaled), axis=0, keepdims=True), axis=1, keepdims=True)
    return scaled, column_scale, 1.8 / widest


def inverses(matrices, coarse, store):
    count = len(matrices)
    size = matrices[0].shape[0]
    eye = jnp.where(eye_mask(size), 1.0, 0.0)
    problems = [scaled_problem(matrix) for matrix in matrices]
    gaps = [eye - scaled * gain for scaled, _, gain in problems]
    guesses = [(eye + gap) * gain for gap, (_, _, gain) in zip(gaps, problems)]
    for _ in range(coarse):
        for at in range(count):
            rough = gaps[at].astype(BF16)
            gaps[at] = dot(rough, rough)
        for at in range(count):
            guesses[at] = guesses[at] + dot(guesses[at].astype(BF16), gaps[at].astype(BF16))
    total = 0.0
    for at in range(count):
        gap = eye - dot3(problems[at][0], guesses[at])
        guess = guesses[at] + dot3(guesses[at], gap)
        rough = gap.astype(BF16)
        gap = dot(rough, rough)
        store[at] = guess + dot(guess.astype(BF16), gap.astype(BF16))
        total = total + jnp.sum(gap * gap)
    good = total < 0.5

    @pl.when(jnp.logical_not(good))
    def _():
        for at in range(count):
            store[at] = eye * problems[at][2]

    def unfinished(carry):
        step, total = carry
        return (step < MAX_STEPS) & (total > BOUND)

    def refine(carry):
        step, _ = carry
        total = 0.0
        for at in range(count):
            gap = eye - dot_full(problems[at][0], store[at])
            store[at] = store[at] + dot3(store[at], gap)
            total = total + jnp.sum(gap * gap)
        return step + 1, total

    lax.while_loop(unfinished, refine, (0, jnp.where(good, total, 1.0)))
    return [(store[at], problems[at][1]) for at in range(count)]


def collect(position, own_ref, side_ref, core_ref, far_ref, payload):
    quarter = payload.shape[0] // 4
    core, side, _ = sides(position)
    other = sides(position ^ 1)[1]
    for ref, core_at, side_at in (
        (own_ref, core, side),
        (side_ref, core, 1 - side),
        (core_ref, 1 - core, other),
        (far_ref, 1 - core, 1 - other),
    ):
        start = pl.multiple_of((core_at * 2 + side_at) * quarter, 8)
        payload[pl.ds(start, quarter), :] = ref[...]


def beta_of(alpha, weighted, mixed_turned, inverse, scale, solved_mixed):
    eye = jnp.where(eye_mask(alpha.shape[0]), 1.0, 0.0)
    rest = dot3(inverse, (weighted - mixed_turned) * scale) * scale
    return (eye - dot3(solved_mixed, alpha)) + rest


def first_kernel(
    position_ref,
    own_ref,
    side_ref,
    core_ref,
    far_ref,
    alpha_part_ref,
    base_part_ref,
    beta_part_ref,
    keep_out,
    send_out,
    alpha_out,
    beta_out,
    fresh_out,
    mixed_out,
    images_out,
    curvature_out,
    payload,
    later,
    store,
):
    size = own_ref.shape[1]
    position = position_ref[0]
    collect(position, own_ref, side_ref, core_ref, far_ref, payload)
    mixed = payload[size : 2 * size, :]
    base = 2 * size + size // 2
    images = unpack_half(payload[2 * size : base, :], payload[base : base + 1, :])
    curvature, res_gram = unpack_pair(payload[0:size, :], payload[base + 1 : base + 2, :])
    (first, first_scale), (second, second_scale) = inverses([curvature, res_gram], 3, store)
    alpha = dot3(first, res_gram * first_scale) * first_scale
    solved_mixed = dot3(second, mixed * second_scale) * second_scale
    weighted = dot3(images, alpha)
    beta = beta_of(alpha, weighted, mixed.T, first, first_scale, solved_mixed)
    still = base_part_ref[...] - dot3(alpha_part_ref[...], alpha)
    rows = still + dot3(beta_part_ref[...], beta)
    image_row = rows[size : 2 * size]
    turned = dot3(
        alpha.T, jnp.concatenate([still[size : 2 * size], rows[3 * size :]], 1)
    )
    square = rows[2 * size : 3 * size] - turned[:, size:] + dot3(beta.T, image_row)
    plain = still[:size] - turned[:, :size]
    packed, diagonal = pack_pair(0.5 * (plain + plain.T), square)
    write_parts(position, [packed], [diagonal], later, keep_out, send_out)
    change = 0.5 * dot3(alpha.T, weighted) - dot3(mixed, alpha)
    fresh_out[...] = res_gram + (change + change.T)
    alpha_out[...] = alpha
    beta_out[...] = beta
    mixed_out[...] = mixed
    images_out[...] = images
    curvature_out[...] = curvature


def carry_kernel(
    alpha_ref,
    beta_ref,
    fresh_ref,
    mixed_ref,
    images_ref,
    curvature_ref,
    inverse_out,
    turn_out,
    rest_out,
    store,
):
    beta, alpha = beta_ref[...], alpha_ref[...]
    ((inverse, scale),) = inverses([fresh_ref[...]], 4, store)
    inverse_out[...] = inverse * scale
    rest = dot3(mixed_ref[...] - dot3(alpha.T, images_ref[...]), beta)
    rest_out[...] = rest
    across = mixed_ref[...].T - dot3(images_ref[...], alpha)
    across = across + dot3(curvature_ref[...], beta)
    turn = dot3(beta.T, across) + rest
    turn_out[...] = 0.5 * (turn + turn.T)


def update_kernel(
    residual_ref,
    direction_ref,
    solution_ref,
    image_ref,
    near_ref,
    down_ref,
    basis_ref,
    skel_ref,
    alpha_ref,
    beta_ref,
    residual_out,
    direction_out,
    solution_out,
    image_out,
):
    count, size = image_ref.shape
    direction, image = direction_ref[...], image_ref[...]
    alpha, beta = alpha_ref[...], beta_ref[...]
    residual = residual_ref[...] - dot3(image, alpha)
    residual_out[...] = residual
    direction_out[...] = residual + dot3(direction, beta)
    solution_out[...] = solution_ref[...] + dot3(direction, alpha)
    down = down_ref[0].astype(F32) + down_ref[1].astype(F32)
    high, low = split(down[:, size:] - dot3(down[:, :size], alpha))
    places, basis = skeleton_columns(skel_ref, count), basis_ref[...]
    far = (dot(basis, high) + dot(basis, low)) + (dot(places, high) + dot(places, low))
    near = near_ref[1] - dot3(near_ref[0], alpha)
    image_out[...] = (near + far) + dot3(image, beta)


def last_kernel(
    position_ref,
    own_ref,
    side_ref,
    core_ref,
    far_ref,
    image_ref,
    residual_ref,
    direction_ref,
    solution_ref,
    fresh_ref,
    inverse_ref,
    turn_ref,
    rest_ref,
    solution_out,
    residual_out,
    direction_out,
    payload,
    store,
    solution_held,
    residual_held,
    direction_held,
    sems,
):
    count, size = direction_ref.shape
    collect(position_ref[0], own_ref, side_ref, core_ref, far_ref, payload)
    plain, images = unpack_pair(payload[0:size, :], payload[size : size + 1, :])
    mixed = plain + rest_ref[...]
    curvature = plain + turn_ref[...]
    res_gram = fresh_ref[...]
    picked = jnp.where(eye_mask(size), res_gram, 0.0)
    column_scale = lax.rsqrt(jnp.sum(picked, axis=1, keepdims=True))
    solved_mixed = dot3(inverse_ref[...], mixed * column_scale)
    ((first, scale),) = inverses([curvature], 4, store)
    alpha = dot3(first, res_gram * scale) * scale
    residual_held[...] = residual_ref[...] - dot3(image_ref[...], alpha)
    copies = [pltpu.make_async_copy(residual_held, residual_out, sems.at[0])]
    copies[0].start()
    solution_held[...] = solution_ref[...] + dot3(direction_ref[...], alpha)
    copies.append(pltpu.make_async_copy(solution_held, solution_out, sems.at[1]))
    copies[1].start()
    beta = beta_of(alpha, dot3(images, alpha), mixed.T, first, scale, solved_mixed)
    strip = count // 4
    for at in range(4):
        rows = pl.ds(at * strip, strip)
        direction_held[rows, :] = residual_held[rows, :] + dot3(direction_ref[rows, :], beta)
        copy = pltpu.make_async_copy(
            direction_held.at[rows, :], direction_out.at[rows, :], sems.at[2 + at]
        )
        copy.start()
        copies.append(copy)
    for copy in copies:
        copy.wait()


def call(kernel, name, inputs, outputs, scratch=(), micros=1.0, limit=32, unused=0, apart=False):
    specs = [SMEM if value.dtype == jnp.int32 and value.shape == (1,) else VMEM for value in inputs]
    specs[len(specs) - unused :] = [ANY] * unused
    return pl.pallas_call(
        kernel,
        name=name,
        in_specs=specs,
        out_specs=[ANY if apart else VMEM] * len(outputs),
        out_shape=[jax.ShapeDtypeStruct(shape, dtype) for shape, dtype in outputs],
        scratch_shapes=list(scratch),
        cost_estimate=pl.CostEstimate(
            flops=int(micros * 1.1e9), bytes_accessed=0, transcendentals=0
        ),
        compiler_params=pltpu.CompilerParams(vmem_limit_bytes=limit * 2**20),
    )(*inputs)


def swapped(value, distance, other=None):
    masks = (2**distance, 2 ** (distance if other is None else other))
    pairs = [(source, source ^ masks[source & 1]) for source in range(lax.axis_size("leaf"))]
    return lax.ppermute(value, "leaf", pairs)


def add_kernel(left_ref, right_ref, *rest):
    rest[-1][...] = left_ref[...] + right_ref[...]


def plus(left, right, after):
    if not after:
        return left + right
    result = (left.shape, F32)
    return call(add_kernel, "add", [left, right, *after], [result], micros=0.2, unused=len(after))[0]


def summed(keep, send, levels, afters=((), (), ())):
    quarter = keep.shape[0] // 2
    half = keep + swapped(send, 0)
    own = plus(half[:quarter], swapped(half[quarter:], 1, 2), afters[0])
    for level in range(3, levels):
        own = plus(own, swapped(own, level), afters[1] if level == 3 else ())
    own = plus(own, swapped(own, 2, 1), afters[2])
    side = swapped(own, 1, 2)
    return [own, side, swapped(own, 0), swapped(side, 0)]


def body(points, leaf_order, skeleton, basis, transfer, coupling, solution, residual, direction):
    levels = lax.axis_size("leaf").bit_length() - 1
    count, size = direction.shape
    rank = basis.shape[1]
    position = lax.axis_index("leaf").astype(jnp.int32).reshape(1)
    order = leaf_order.reshape(1, count)
    tall = ((count, size), F32)
    square = ((size, size), F32)
    coef = ((rank, size), BF16)
    tall_pair = ((2, count, size), F32)
    work = pltpu.VMEM((2, size, size), F32)
    rows, later_rows = payload_rows(size, True), payload_rows(size, False)

    def up(level, current, sibling, extra=()):
        (result,) = call(
            functools.partial(up_kernel, level),
            "up",
            [position, current, sibling, transfer, *extra],
            [(current.shape, BF16)],
            micros=0.3,
            unused=len(extra),
        )
        return result

    held = pltpu.VMEM((count, size), F32)
    (current,) = call(
        coef_kernel, "coef", [direction, basis, skeleton], [coef], micros=2.7, limit=60
    )
    siblings = [swapped(current, 0)]
    (current,) = call(hold_kernel, "hold", [current], [coef], micros=0.5)
    (current,) = call(
        half_up_kernel,
        "up",
        [position, current, siblings[0], transfer],
        [((rank, size // 2), BF16)],
        [pltpu.VMEM((rank, size), BF16)],
        micros=0.3,
    )
    siblings.append(swapped(current, 1))
    (block,) = call(
        block_kernel,
        "block",
        [points, order, current],
        [((count, count), BF16)],
        [pltpu.VMEM((8, count), F32), pltpu.VMEM((count, 128), F32)],
        micros=3.6,
        unused=1,
    )
    high, low, gram = call(
        prepare_kernel,
        "prepare",
        [direction, residual, current],
        [((2 * size, count), BF16), ((2 * size, count), BF16), square],
        micros=0.8,
        unused=1,
    )
    current = up(1, current, siblings[1], [block, high])
    siblings.append(swapped(current, 2))
    (near,) = call(near_kernel, "near", [block, direction], [tall], micros=0.7)
    double_low = ((2 * size, rank), BF16)
    factors = call(
        factor_kernel,
        "factor",
        [high, low, basis, skeleton, current],
        [double_low] * 3 + [((rank, rank), BF16)] * 3 + [coef],
        micros=1.8,
        unused=1,
    )
    residual_coef = factors[-1]
    for level in range(2, levels - 1):
        extra = [near, residual_coef] if level == 2 else ()
        current = up(level, current, siblings[level], extra)
        siblings.append(swapped(current, level + 1))
    near_factors = call(
        near_factor_kernel,
        "near_factor",
        [near, high, low, basis, skeleton],
        [((2 * size, size), F32), square, ((rank, size), F32), ((rank, size), F32)],
        micros=1.8,
    )
    (ready,) = call(
        hold_kernel,
        "ready",
        [siblings[-1], near_factors[0]],
        [(siblings[-1].shape, BF16)],
        micros=0.2,
        unused=1,
    )
    siblings += [swapped(value, 0) for value in siblings[1:-1] + [ready]]
    down, image_coef, image_both, keep, send, local_mixed, local_images = call(
        functools.partial(down_kernel, levels),
        "down",
        [position, *siblings, coupling, transfer, *near_factors, *factors[:-1], gram],
        [((2, rank, size), BF16), coef, ((2, rank, size), BF16)]
        + [((rows // 2, size), F32)] * 2
        + [square, square],
        [pltpu.VMEM((rows, size), F32)],
        micros=2.0,
    )

    (image,) = call(image_kernel, "image", [near, down, basis, skeleton], [tall], micros=0.7)
    others = [swapped(image_coef, 0), swapped(residual_coef, 0)]
    (current,) = call(
        pair_up_kernel,
        "pair_up",
        [position, image_coef, residual_coef, *others, transfer],
        [coef],
        micros=0.3,
    )
    pieces = [position] + summed(keep, send, levels, ((current,), (), ()))
    (near,) = call(
        pair_near_kernel,
        "pair_near",
        [block, image, residual],
        [tall_pair],
        micros=2.4,
    )
    own = [swapped(current, 1)]
    current = up(1, current, own[0], [near])
    own.append(swapped(current, 2))
    (cross,) = call(
        pair_cross_kernel,
        "pair_cross",
        [near, image, high, low, current],
        [((2 * size, 2 * size), F32)],
        micros=2.3,
        unused=1,
    )
    for level in range(2, levels - 1):
        current = up(level, current, own[level - 1], [cross] if level == 2 else ())
        own.append(swapped(current, level + 1))
    square_part, near_both = call(
        pair_square_kernel,
        "pair_square",
        [near, basis, skeleton, pieces[1]],
        [((2 * size, 2 * size), F32), ((rank, 2 * size), F32)],
        micros=2.8,
        unused=1,
    )
    (ready,) = call(
        hold_kernel, "ready", [own[-1], near_both], [coef], micros=0.2, unused=1
    )
    other = [swapped(value, 0) for value in own[:-1] + [ready]]
    both_high, both_low, _, ties_high, ties_low, _, _ = factors
    down, alpha_part, base_part, beta_part = call(
        functools.partial(pair_down_kernel, levels),
        "pair_down",
        [position, *others, *own, *other, coupling, transfer, cross, square_part, near_both]
        + [both_high, both_low, image_both, ties_high, ties_low, local_mixed, local_images],
        [((2, rank, 2 * size), BF16)] + [((4 * size, size), F32)] * 3,
        micros=2.5,
    )

    keep, send, alpha, beta, fresh, mixed, images, curvature = call(
        first_kernel,
        "first",
        pieces + [alpha_part, base_part, beta_part],
        [((later_rows // 2, size), F32), ((later_rows // 2, size), F32)] + [square] * 6,
        [pltpu.VMEM((rows, size), F32), pltpu.VMEM((later_rows, size), F32), work],
        micros=5.0,
    )
    inverse, turn, rest = call(
        carry_kernel,
        "carry",
        [alpha, beta, fresh, mixed, images, curvature],
        [square] * 3,
        [work],
        micros=3.0,
    )
    residual, direction, solution, image = call(
        update_kernel,
        "update",
        [residual, direction, solution, image, near, down, basis, skeleton, alpha, beta],
        [tall] * 4,
        micros=3.2,
    )
    pieces = [position] + summed(keep, send, levels, ((), (inverse,), (direction,)))
    return tuple(
        call(
            last_kernel,
            "last",
            pieces + [image, residual, direction, solution, fresh, inverse, turn, rest],
            [tall, tall, tall],
            [pltpu.VMEM((later_rows, size), F32), work]
            + [held] * 3
            + [pltpu.SemaphoreType.DMA((6,))],
            micros=7.0,
            apart=True,
        )
    )


def solution(mesh):
    placed = (
        P(None, ("groups", "leaf")),
        P(("groups", "leaf")),
        P(("groups", "leaf"), None),
        P(("groups", "leaf"), None),
        P(("groups", "leaf"), None, None, None),
        P(("groups", "leaf"), None, None, None),
        P(("groups", "leaf"), None),
        P(("groups", "leaf"), None),
        P(("groups", "leaf"), None),
    )
    return jax.shard_map(
        body,
        mesh=mesh,
        in_specs=placed,
        out_specs=(
            P(("groups", "leaf"), None),
            P(("groups", "leaf"), None),
            P(("groups", "leaf"), None),
        ),
        check_vma=False,
    )
```

```python
import functools

import jax
import jax.numpy as jnp
from jax import lax
from jax.experimental import pallas as pl
from jax.experimental.pallas import tpu as pltpu
from jax.sharding import PartitionSpec as P

F32 = jnp.float32
BF16 = jnp.bfloat16
VMEM = pl.BlockSpec(memory_space=pltpu.VMEM)
SMEM = pl.BlockSpec(memory_space=pltpu.SMEM)
ANY = pl.BlockSpec(memory_space=pl.ANY)
MAX_STEPS = 60
BOUND = 1e-5


def dot(left, right):
    return jnp.dot(left, right, preferred_element_type=F32)


def dot_t(left, right):
    return lax.dot_general(left, right, (((0,), (0,)), ((), ())), preferred_element_type=F32)


def split(value):
    high = value.astype(BF16)
    return high, (value - high.astype(F32)).astype(BF16)


def dot3(left, right):
    lh, ll = split(left)
    rh, rl = split(right)
    return dot(lh, rh) + (dot(lh, rl) + dot(ll, rh))


def dot_full(left, right):
    return jnp.dot(left, right, precision=lax.Precision.HIGHEST, preferred_element_type=F32)


def iotas(rows, columns):
    return (
        lax.broadcasted_iota(jnp.int32, (rows, columns), 0),
        lax.broadcasted_iota(jnp.int32, (rows, columns), 1),
    )


def eye_mask(size):
    row, column = iotas(size, size)
    return row == column


def skeleton_columns(skel_ref, count):
    row, _ = iotas(count, skel_ref.shape[1])
    return jnp.where(row == skel_ref[...], 1.0, 0.0).astype(BF16)


def skeleton_rows(skel_ref, count):
    rank = skel_ref.shape[1]
    wide = jnp.broadcast_to(skel_ref[...].astype(F32), (128, rank)).T
    column = lax.broadcasted_iota(jnp.int32, (rank, 128), 1).astype(F32)
    tiles = [
        jnp.where(wide == column + float(start), 1.0, 0.0).astype(BF16)
        for start in range(0, count, 128)
    ]
    return jnp.concatenate(tiles, 1)


def coef_kernel(direction_ref, basis_ref, skel_ref, coef_ref):
    high, low = split(direction_ref[...])
    picks = skeleton_rows(skel_ref, direction_ref.shape[0])
    coef = dot_t(basis_ref[...], high) + (dot(picks, high) + dot(picks, low))
    coef_ref[...] = coef.astype(BF16)


def hold_kernel(value_ref, *rest):
    rest[-1][...] = value_ref[...]


def block_kernel(points_ref, order_ref, after_ref, block_ref, padded, column_ref):
    count = points_ref.shape[1]
    padded[...] = jnp.zeros_like(padded)
    padded[0:3, :] = points_ref[...]
    raw = padded[...]
    high = raw.astype(BF16).astype(F32)
    middle = (raw - high).astype(BF16).astype(F32)
    low = raw - high - middle
    parts = jnp.concatenate([high, middle, low], 0).astype(BF16)
    row, _ = iotas(count, count)
    picks = jnp.where(row == order_ref[...], 1.0, 0.0).astype(BF16)
    ordered = dot(parts, picks)
    ordered = (ordered[0:8] + ordered[8:16] + ordered[16:24]) * (300.0**0.5)
    column_ref[...] = jnp.concatenate([ordered, jnp.zeros((120, count), F32)], 0).T
    strip = 128

    def step(index, carry):
        start = pl.multiple_of(index * strip, strip)
        mine = column_ref[pl.ds(start, strip), :]
        square = 1e-10
        for axis in range(3):
            gap = mine[:, axis : axis + 1] - ordered[axis : axis + 1, :]
            square = gap * gap + square
        scaled = square * lax.rsqrt(square)
        values = ((1.0 + scaled) * jnp.exp(-scaled)).astype(BF16)
        block_ref[pl.ds(start, strip), :] = values
        return carry

    lax.fori_loop(0, count // strip, step, 0)

def near_kernel(block_ref, direction_ref, after_ref, near_ref):
    low_direction = direction_ref[...].astype(BF16)
    near_ref[...] = dot(block_ref[...], low_direction) + 2.0 * low_direction.astype(F32)


def turned_splits(value, high_ref, low_ref, start):
    size = value.shape[1]
    high, low = split(value)
    high_ref[start : start + size, :] = high.T
    low_ref[start : start + size, :] = low.T
    return high, low


def prepare_kernel(direction_ref, residual_ref, after_ref, high_ref, low_ref, gram_ref):
    size = direction_ref.shape[1]
    turned_splits(direction_ref[...], high_ref, low_ref, 0)
    high, low = turned_splits(residual_ref[...], high_ref, low_ref, size)
    both = dot(high_ref[size:, :], jnp.concatenate([high, low], 1))
    cross = both[:, size:]
    gram_ref[...] = both[:, :size] + (cross + cross.T)


def up_kernel(level, position_ref, current_ref, sibling_ref, transfer_ref, *rest):
    coef_ref = rest[-1]
    rank = current_ref.shape[0]
    right = (position_ref[0] >> level) & 1
    mine = transfer_ref[0, level, pl.ds(pl.multiple_of(right * rank, rank), rank), :]
    other = transfer_ref[0, level, pl.ds(pl.multiple_of((1 - right) * rank, rank), rank), :]
    coef_ref[...] = (
        dot_t(mine, current_ref[...]) + dot_t(other, sibling_ref[...])
    ).astype(BF16)


def half_up_kernel(position_ref, current_ref, sibling_ref, transfer_ref, *rest):
    whole, coef_ref = rest[-1], rest[-2]
    up_kernel(0, position_ref, current_ref, sibling_ref, transfer_ref, whole)
    half = coef_ref.shape[1]
    value = whole[...]
    odd = (position_ref[0] & 1) == 1
    coef_ref[...] = jnp.where(odd, value[:, half:], value[:, :half])


def joined(odd, own, other):
    return jnp.concatenate([jnp.where(odd, other, own), jnp.where(odd, own, other)], 1)


def pack_pair(first, second):
    size = first.shape[0]
    row, column = iotas(size, size)
    diagonal = jnp.sum(jnp.where(row == column, second, 0.0), axis=0, keepdims=True)
    return jnp.where(row >= column, first, second), diagonal


def unpack_pair(packed, diagonal):
    size = packed.shape[0]
    row, column = iotas(size, size)
    turned = packed.T
    first = jnp.where(row >= column, packed, turned)
    second = jnp.where(row < column, packed, turned)
    return first, jnp.where(row == column, diagonal, second)


def pack_half(matrix):
    half = matrix.shape[0] // 2
    corner, tail = pack_pair(matrix[:half, :half], matrix[half:, half:])
    return jnp.concatenate([matrix[half:, :half], corner], 1), jnp.concatenate([tail, tail], 1)


def unpack_half(packed, tail):
    half = packed.shape[0]
    upper, lower = unpack_pair(packed[:, half:], tail[:, :half])
    corner = packed[:, :half]
    return jnp.concatenate(
        [jnp.concatenate([upper, corner.T], 1), jnp.concatenate([corner, lower], 1)], 0
    )


def payload_rows(size, with_start):
    rows = size + 8 + (size + size // 2 if with_start else 0)
    return -(-rows // 32) * 32


def sides(position):
    core = position & 1
    return core, (position >> (1 + core)) & 1, (position >> (2 - core)) & 1


def write_parts(position, blocks, rows, payload, keep_ref, send_ref):
    base = 0
    for block in blocks:
        payload[base : base + block.shape[0], :] = block
        base += block.shape[0]
    payload[base:, :] = jnp.zeros((payload.shape[0] - base, payload.shape[1]), F32)
    for at, row in enumerate(rows):
        payload[base + at : base + at + 1, :] = row
    quarter = payload.shape[0] // 4
    core, side, _ = sides(position)
    other = sides(position ^ 1)[1]

    def part(core_at, side_at):
        start = pl.multiple_of((core_at * 2 + side_at) * quarter, 8)
        return payload[pl.ds(start, quarter), :]

    keep_ref[0:quarter, :] = part(core, side)
    keep_ref[quarter:, :] = part(core, 1 - side)
    send_ref[0:quarter, :] = part(1 - core, other)
    send_ref[quarter:, :] = part(1 - core, 1 - other)


def down_chain(position, levels, coupling_ref, transfer_ref, siblings):
    rank = coupling_ref.shape[2]
    down = dot(coupling_ref[0, levels - 1], siblings[levels - 1])
    for level in reversed(range(levels - 1)):
        right = (position >> level) & 1
        half = transfer_ref[0, level, pl.ds(pl.multiple_of(right * rank, rank), rank), :]
        high, low = split(down)
        down = dot(coupling_ref[0, level], siblings[level]) + (dot(half, high) + dot(half, low))
    return split(down)


def factor_kernel(
    high_ref,
    low_ref,
    basis_ref,
    skel_ref,
    after_ref,
    both_high_out,
    both_low_out,
    picked_out,
    ties_high_out,
    ties_low_out,
    basis_picked_out,
    coef_out,
):
    count, rank = basis_ref.shape
    high, low = high_ref[...], low_ref[...]
    size = high.shape[0] // 2
    basis = basis_ref[...]
    places, picks = skeleton_columns(skel_ref, count), skeleton_rows(skel_ref, count)
    picked = dot(high, places) + dot(low, places)
    picked_out[...] = picked.astype(BF16)
    both = picked + (dot(high, basis) + dot(low, basis))
    both_high_out[...], both_low_out[...] = split(both)
    coef_out[...] = both[size:].T.astype(BF16)
    basis_picked = dot(picks, basis)
    basis_picked_out[...] = basis_picked.astype(BF16)
    ties = dot_t(basis, basis) + (basis_picked + basis_picked.T)
    ties_high_out[...], ties_low_out[...] = split(ties)


def near_factor_kernel(
    near_ref,
    high_ref,
    low_ref,
    basis_ref,
    skel_ref,
    near_gram_out,
    near_square_out,
    near_both_out,
    near_picked_out,
):
    count, size = near_ref.shape
    near_high, near_low = split(near_ref[...])
    near_parts = jnp.concatenate([near_high, near_low], 1)
    wide = dot(high_ref[...], near_parts)
    near_gram_out[...] = wide[:, :size] + (wide[:, size:] + dot(low_ref[...], near_high))
    wide = dot_t(near_high, near_parts)
    cross = wide[:, size:]
    near_square_out[...] = wide[:, :size] + (cross + cross.T)
    wide = dot(skeleton_rows(skel_ref, count), near_parts)
    near_picked = wide[:, :size] + wide[:, size:]
    near_picked_out[...] = near_picked
    wide = dot_t(basis_ref[...], near_parts)
    near_both_out[...] = near_picked + (wide[:, :size] + wide[:, size:])


def down_kernel(levels, *refs):
    position_ref = refs[0]
    odd = (position_ref[0] & 1) == 1
    siblings = [refs[1][...]]
    for at in range(2, 1 + levels):
        siblings.append(joined(odd, refs[at][...], refs[at + levels - 1][...]))
    (
        coupling_ref,
        transfer_ref,
        near_gram_ref,
        near_square_ref,
        near_both_ref,
        near_picked_ref,
        both_high_ref,
        both_low_ref,
        picked_ref,
        ties_high_ref,
        ties_low_ref,
        basis_picked_ref,
        gram_ref,
        down_out,
        coef_out,
        image_both_out,
        keep_ref,
        send_ref,
        mixed_out,
        images_out,
        payload,
    ) = refs[2 * levels :]
    size = gram_ref.shape[1]
    position = position_ref[0]
    high, low = down_chain(position, levels, coupling_ref, transfer_ref, siblings)
    down_out[0], down_out[1] = high, low
    down = high.astype(F32) + low.astype(F32)
    picked = dot(basis_picked_ref[...], high) + down
    change = dot(ties_high_ref[...], high) + dot(ties_low_ref[...], high)
    change = change + (dot_t(basis_picked_ref[...], low) + down)
    near_both = near_both_ref[...]
    coef_out[...] = (near_both + change).astype(BF16)
    image_both_out[0], image_both_out[1] = split(near_both + change)
    half_high, half_low = split(near_both + 0.5 * change)
    other = (near_picked_ref[...] + 0.5 * picked).astype(BF16)
    half = dot_t(high, half_high) + (dot_t(high, half_low) + dot_t(low, other))
    images = near_square_ref[...] + (half + half.T)
    grams = dot(both_high_ref[...], high) + (
        dot(both_low_ref[...], high) + dot(picked_ref[...], low)
    )
    grams = near_gram_ref[...] + grams
    packed, tail = pack_half(images)
    curvature = grams[:size]
    pair, diagonal = pack_pair(0.5 * (curvature + curvature.T), gram_ref[...])
    write_parts(
        position, [pair, grams[size:], packed], [tail, diagonal], payload, keep_ref, send_ref
    )
    mixed_out[...] = grams[size:]
    images_out[...] = images


def image_kernel(near_ref, down_ref, basis_ref, skel_ref, image_ref):
    places = skeleton_columns(skel_ref, near_ref.shape[0])
    high, low = down_ref[0], down_ref[1]
    image_ref[...] = (near_ref[...] + dot(basis_ref[...], high)) + (
        dot(places, high) + dot(places, low)
    )


def pair_up_kernel(
    position_ref, image_ref, residual_ref, image_other, residual_other, transfer_ref, coef_ref
):
    core = position_ref[0] & 1

    @pl.when(core == 0)
    def _():
        up_kernel(0, position_ref, image_ref, image_other, transfer_ref, coef_ref)

    @pl.when(core == 1)
    def _():
        up_kernel(0, position_ref, residual_ref, residual_other, transfer_ref, coef_ref)


def pair_near_kernel(block_ref, image_ref, residual_ref, near_ref):
    block = block_ref[...]
    for at, ref in enumerate((image_ref, residual_ref)):
        value = ref[...]
        high, low = split(value)
        near_ref[at] = 2.0 * value + (dot(block, high) + dot(block, low))


def pair_cross_kernel(near_ref, image_ref, high_ref, low_ref, after_ref, cross_out):
    size = image_ref.shape[1]
    near_high, near_low = split(jnp.concatenate([near_ref[0], near_ref[1]], 1))
    high, low = high_ref[size:, :], low_ref[size:, :]
    cross_out[0:size, :] = dot(high, near_high) + (dot(high, near_low) + dot(low, near_high))
    high, low = split(image_ref[...])
    cross_out[size:, :] = dot_t(high, near_high) + (dot_t(high, near_low) + dot_t(low, near_high))


def pair_square_kernel(near_ref, basis_ref, skel_ref, after_ref, square_out, both_out):
    width = 2 * near_ref.shape[2]
    high, low = split(jnp.concatenate([near_ref[0], near_ref[1]], 1))
    parts = jnp.concatenate([high, low], 1)
    wide = dot_t(high, parts)
    cross = wide[:, width:]
    square_out[...] = wide[:, :width] + (cross + cross.T)
    wide = dot_t(basis_ref[...], parts) + dot(skeleton_rows(skel_ref, near_ref.shape[1]), parts)
    both_out[...] = wide[:, :width] + wide[:, width:]


def pair_down_kernel(levels, *refs):
    position_ref, image_other, residual_other = refs[:3]
    own_refs, other_refs = refs[3 : 2 + levels], refs[2 + levels : 1 + 2 * levels]
    (
        coupling_ref,
        transfer_ref,
        cross_ref,
        square_ref,
        near_both_ref,
        both_high_ref,
        both_low_ref,
        image_both_ref,
        ties_high_ref,
        ties_low_ref,
        mixed_ref,
        images_ref,
        down_out,
        alpha_out,
        base_out,
        beta_out,
    ) = refs[1 + 2 * levels :]
    size = mixed_ref.shape[0]
    position = position_ref[0]
    odd = (position & 1) == 1
    siblings = [jnp.concatenate([image_other[...], residual_other[...]], 1)]
    for own_ref, other_ref in zip(own_refs, other_refs):
        siblings.append(joined(odd, own_ref[...], other_ref[...]))
    high, low = down_chain(position, levels, coupling_ref, transfer_ref, siblings)
    down_out[0], down_out[1] = high, low

    def by(matrix_dot, first_high, first_low):
        return matrix_dot(first_high, high) + (
            matrix_dot(first_low, high) + matrix_dot(first_high, low)
        )

    residual_row = cross_ref[0:size, :] + by(dot, both_high_ref[size:, :], both_low_ref[size:, :])
    image_row = cross_ref[size:, :] + by(dot_t, image_both_ref[0], image_both_ref[1])
    tied = by(dot, ties_high_ref[...], ties_low_ref[...])
    tied = tied + (high.astype(F32) + low.astype(F32))
    half_high, half_low = split(near_both_ref[...] + 0.5 * tied)
    half = dot_t(high, half_high) + (dot_t(high, half_low) + dot_t(low, half_high))
    square = square_ref[...] + (half + half.T)
    alpha_out[0:size, :] = residual_row[:, :size]
    alpha_out[size : 2 * size, :] = image_row[:, :size]
    alpha_out[2 * size : 3 * size, :] = square[size:, :size]
    alpha_out[3 * size :, :] = square[:size, :size]
    base_out[0:size, :] = residual_row[:, size:]
    base_out[size : 2 * size, :] = image_row[:, size:]
    base_out[2 * size : 3 * size, :] = square[size:, size:]
    base_out[3 * size :, :] = square[:size, size:]
    beta_out[0:size, :] = mixed_ref[...]
    beta_out[size : 2 * size, :] = images_ref[...]
    beta_out[2 * size : 3 * size, :] = image_row[:, size:].T
    beta_out[3 * size :, :] = image_row[:, :size].T


def scaled_problem(matrix):
    size = matrix.shape[0]
    eye = eye_mask(size)
    picked = jnp.where(eye, matrix, 0.0)
    row_scale = lax.rsqrt(jnp.sum(picked, axis=0, keepdims=True))
    column_scale = lax.rsqrt(jnp.sum(picked, axis=1, keepdims=True))
    scaled = matrix * column_scale * row_scale
    widest = jnp.max(jnp.sum(jnp.abs(scaled), axis=0, keepdims=True), axis=1, keepdims=True)
    return scaled, column_scale, 1.8 / widest


def inverses(matrices, coarse, store):
    count = len(matrices)
    size = matrices[0].shape[0]
    eye = jnp.where(eye_mask(size), 1.0, 0.0)
    problems = [scaled_problem(matrix) for matrix in matrices]
    gaps = [eye - scaled * gain for scaled, _, gain in problems]
    guesses = [(eye + gap) * gain for gap, (_, _, gain) in zip(gaps, problems)]
    for _ in range(coarse):
        for at in range(count):
            rough = gaps[at].astype(BF16)
            gaps[at] = dot(rough, rough)
        for at in range(count):
            guesses[at] = guesses[at] + dot(guesses[at].astype(BF16), gaps[at].astype(BF16))
    total = 0.0
    for at in range(count):
        gap = eye - dot3(problems[at][0], guesses[at])
        guess = guesses[at] + dot3(guesses[at], gap)
        rough = gap.astype(BF16)
        gap = dot(rough, rough)
        store[at] = guess + dot(guess.astype(BF16), gap.astype(BF16))
        total = total + jnp.sum(gap * gap)
    good = total < 0.5

    @pl.when(jnp.logical_not(good))
    def _():
        for at in range(count):
            store[at] = eye * problems[at][2]

    def unfinished(carry):
        step, total = carry
        return (step < MAX_STEPS) & (total > BOUND)

    def refine(carry):
        step, _ = carry
        total = 0.0
        for at in range(count):
            gap = eye - dot_full(problems[at][0], store[at])
            store[at] = store[at] + dot3(store[at], gap)
            total = total + jnp.sum(gap * gap)
        return step + 1, total

    lax.while_loop(unfinished, refine, (0, jnp.where(good, total, 1.0)))
    return [(store[at], problems[at][1]) for at in range(count)]


def collect(position, own_ref, side_ref, core_ref, far_ref, payload):
    quarter = payload.shape[0] // 4
    core, side, _ = sides(position)
    other = sides(position ^ 1)[1]
    for ref, core_at, side_at in (
        (own_ref, core, side),
        (side_ref, core, 1 - side),
        (core_ref, 1 - core, other),
        (far_ref, 1 - core, 1 - other),
    ):
        start = pl.multiple_of((core_at * 2 + side_at) * quarter, 8)
        payload[pl.ds(start, quarter), :] = ref[...]


def beta_of(alpha, weighted, mixed_turned, inverse, scale, solved_mixed):
    eye = jnp.where(eye_mask(alpha.shape[0]), 1.0, 0.0)
    rest = dot3(inverse, (weighted - mixed_turned) * scale) * scale
    return (eye - dot3(solved_mixed, alpha)) + rest


def first_kernel(
    position_ref,
    own_ref,
    side_ref,
    core_ref,
    far_ref,
    alpha_part_ref,
    base_part_ref,
    beta_part_ref,
    keep_out,
    send_out,
    alpha_out,
    beta_out,
    fresh_out,
    mixed_out,
    images_out,
    curvature_out,
    payload,
    later,
    store,
):
    size = own_ref.shape[1]
    position = position_ref[0]
    collect(position, own_ref, side_ref, core_ref, far_ref, payload)
    mixed = payload[size : 2 * size, :]
    base = 2 * size + size // 2
    images = unpack_half(payload[2 * size : base, :], payload[base : base + 1, :])
    curvature, res_gram = unpack_pair(payload[0:size, :], payload[base + 1 : base + 2, :])
    (first, first_scale), (second, second_scale) = inverses([curvature, res_gram], 3, store)
    alpha = dot3(first, res_gram * first_scale) * first_scale
    solved_mixed = dot3(second, mixed * second_scale) * second_scale
    weighted = dot3(images, alpha)
    beta = beta_of(alpha, weighted, mixed.T, first, first_scale, solved_mixed)
    still = base_part_ref[...] - dot3(alpha_part_ref[...], alpha)
    rows = still + dot3(beta_part_ref[...], beta)
    image_row = rows[size : 2 * size]
    turned = dot3(
        alpha.T, jnp.concatenate([still[size : 2 * size], rows[3 * size :]], 1)
    )
    square = rows[2 * size : 3 * size] - turned[:, size:] + dot3(beta.T, image_row)
    plain = still[:size] - turned[:, :size]
    packed, diagonal = pack_pair(0.5 * (plain + plain.T), square)
    write_parts(position, [packed], [diagonal], later, keep_out, send_out)
    change = 0.5 * dot3(alpha.T, weighted) - dot3(mixed, alpha)
    fresh_out[...] = res_gram + (change + change.T)
    alpha_out[...] = alpha
    beta_out[...] = beta
    mixed_out[...] = mixed
    images_out[...] = images
    curvature_out[...] = curvature


def carry_kernel(
    alpha_ref,
    beta_ref,
    fresh_ref,
    mixed_ref,
    images_ref,
    curvature_ref,
    inverse_out,
    turn_out,
    rest_out,
    store,
):
    beta, alpha = beta_ref[...], alpha_ref[...]
    ((inverse, scale),) = inverses([fresh_ref[...]], 4, store)
    inverse_out[...] = inverse * scale
    rest = dot3(mixed_ref[...] - dot3(alpha.T, images_ref[...]), beta)
    rest_out[...] = rest
    across = mixed_ref[...].T - dot3(images_ref[...], alpha)
    across = across + dot3(curvature_ref[...], beta)
    turn = dot3(beta.T, across) + rest
    turn_out[...] = 0.5 * (turn + turn.T)


def update_kernel(
    residual_ref,
    direction_ref,
    solution_ref,
    image_ref,
    near_ref,
    down_ref,
    basis_ref,
    skel_ref,
    alpha_ref,
    beta_ref,
    residual_out,
    direction_out,
    solution_out,
    image_out,
):
    count, size = image_ref.shape
    direction, image = direction_ref[...], image_ref[...]
    alpha, beta = alpha_ref[...], beta_ref[...]
    residual = residual_ref[...] - dot3(image, alpha)
    residual_out[...] = residual
    direction_out[...] = residual + dot3(direction, beta)
    solution_out[...] = solution_ref[...] + dot3(direction, alpha)
    down = down_ref[0].astype(F32) + down_ref[1].astype(F32)
    high, low = split(down[:, size:] - dot3(down[:, :size], alpha))
    places, basis = skeleton_columns(skel_ref, count), basis_ref[...]
    far = (dot(basis, high) + dot(basis, low)) + (dot(places, high) + dot(places, low))
    near = near_ref[1] - dot3(near_ref[0], alpha)
    image_out[...] = (near + far) + dot3(image, beta)


def last_kernel(
    position_ref,
    own_ref,
    side_ref,
    core_ref,
    far_ref,
    image_ref,
    residual_ref,
    direction_ref,
    solution_ref,
    fresh_ref,
    inverse_ref,
    turn_ref,
    rest_ref,
    solution_out,
    residual_out,
    direction_out,
    payload,
    store,
    solution_held,
    residual_held,
    direction_held,
    sems,
):
    count, size = direction_ref.shape
    collect(position_ref[0], own_ref, side_ref, core_ref, far_ref, payload)
    plain, images = unpack_pair(payload[0:size, :], payload[size : size + 1, :])
    mixed = plain + rest_ref[...]
    curvature = plain + turn_ref[...]
    res_gram = fresh_ref[...]
    picked = jnp.where(eye_mask(size), res_gram, 0.0)
    column_scale = lax.rsqrt(jnp.sum(picked, axis=1, keepdims=True))
    solved_mixed = dot3(inverse_ref[...], mixed * column_scale)
    ((first, scale),) = inverses([curvature], 4, store)
    alpha = dot3(first, res_gram * scale) * scale
    residual_held[...] = residual_ref[...] - dot3(image_ref[...], alpha)
    copies = [pltpu.make_async_copy(residual_held, residual_out, sems.at[0])]
    copies[0].start()
    solution_held[...] = solution_ref[...] + dot3(direction_ref[...], alpha)
    copies.append(pltpu.make_async_copy(solution_held, solution_out, sems.at[1]))
    copies[1].start()
    beta = beta_of(alpha, dot3(images, alpha), mixed.T, first, scale, solved_mixed)
    strip = count // 4
    for at in range(4):
        rows = pl.ds(at * strip, strip)
        direction_held[rows, :] = residual_held[rows, :] + dot3(direction_ref[rows, :], beta)
        copy = pltpu.make_async_copy(
            direction_held.at[rows, :], direction_out.at[rows, :], sems.at[2 + at]
        )
        copy.start()
        copies.append(copy)
    for copy in copies:
        copy.wait()


def call(kernel, name, inputs, outputs, scratch=(), micros=1.0, limit=32, unused=0, apart=False):
    specs = [SMEM if value.dtype == jnp.int32 and value.shape == (1,) else VMEM for value in inputs]
    specs[len(specs) - unused :] = [ANY] * unused
    return pl.pallas_call(
        kernel,
        name=name,
        in_specs=specs,
        out_specs=[ANY if apart else VMEM] * len(outputs),
        out_shape=[jax.ShapeDtypeStruct(shape, dtype) for shape, dtype in outputs],
        scratch_shapes=list(scratch),
        cost_estimate=pl.CostEstimate(
            flops=int(micros * 1.1e9), bytes_accessed=0, transcendentals=0
        ),
        compiler_params=pltpu.CompilerParams(vmem_limit_bytes=limit * 2**20),
    )(*inputs)


def swapped(value, distance, other=None):
    masks = (2**distance, 2 ** (distance if other is None else other))
    pairs = [(source, source ^ masks[source & 1]) for source in range(lax.axis_size("leaf"))]
    return lax.ppermute(value, "leaf", pairs)


def add_kernel(left_ref, right_ref, *rest):
    rest[-1][...] = left_ref[...] + right_ref[...]


def plus(left, right, after):
    if not after:
        return left + right
    result = (left.shape, F32)
    return call(add_kernel, "add", [left, right, *after], [result], micros=0.2, unused=len(after))[0]


def summed(keep, send, levels, afters=((), (), ())):
    quarter = keep.shape[0] // 2
    half = keep + swapped(send, 0)
    own = plus(half[:quarter], swapped(half[quarter:], 1, 2), afters[0])
    for level in range(3, levels):
        own = plus(own, swapped(own, level), afters[1] if level == 3 else ())
    own = plus(own, swapped(own, 2, 1), afters[2])
    side = swapped(own, 1, 2)
    return [own, side, swapped(own, 0), swapped(side, 0)]


def body(points, leaf_order, skeleton, basis, transfer, coupling, solution, residual, direction):
    levels = lax.axis_size("leaf").bit_length() - 1
    count, size = direction.shape
    rank = basis.shape[1]
    position = lax.axis_index("leaf").astype(jnp.int32).reshape(1)
    order = leaf_order.reshape(1, count)
    tall = ((count, size), F32)
    square = ((size, size), F32)
    coef = ((rank, size), BF16)
    tall_pair = ((2, count, size), F32)
    work = pltpu.VMEM((2, size, size), F32)
    rows, later_rows = payload_rows(size, True), payload_rows(size, False)

    def up(level, current, sibling, extra=()):
        (result,) = call(
            functools.partial(up_kernel, level),
            "up",
            [position, current, sibling, transfer, *extra],
            [(current.shape, BF16)],
            micros=0.3,
            unused=len(extra),
        )
        return result

    held = pltpu.VMEM((count, size), F32)
    (current,) = call(
        coef_kernel, "coef", [direction, basis, skeleton], [coef], micros=2.7, limit=60
    )
    siblings = [swapped(current, 0)]
    (current,) = call(hold_kernel, "hold", [current], [coef], micros=0.5)
    (current,) = call(
        half_up_kernel,
        "up",
        [position, current, siblings[0], transfer],
        [((rank, size // 2), BF16)],
        [pltpu.VMEM((rank, size), BF16)],
        micros=0.3,
    )
    siblings.append(swapped(current, 1))
    (block,) = call(
        block_kernel,
        "block",
        [points, order, current],
        [((count, count), BF16)],
        [pltpu.VMEM((8, count), F32), pltpu.VMEM((count, 128), F32)],
        micros=3.6,
        unused=1,
    )
    high, low, gram = call(
        prepare_kernel,
        "prepare",
        [direction, residual, current],
        [((2 * size, count), BF16), ((2 * size, count), BF16), square],
        micros=0.8,
        unused=1,
    )
    current = up(1, current, siblings[1], [block, high])
    siblings.append(swapped(current, 2))
    (near,) = call(
        near_kernel, "near", [block, direction, current], [tall], micros=0.7, unused=1
    )
    double_low = ((2 * size, rank), BF16)
    factors = call(
        factor_kernel,
        "factor",
        [high, low, basis, skeleton, current],
        [double_low] * 3 + [((rank, rank), BF16)] * 3 + [coef],
        micros=1.8,
        unused=1,
    )
    residual_coef = factors[-1]
    for level in range(2, levels - 1):
        extra = [near, residual_coef] if level == 2 else ()
        current = up(level, current, siblings[level], extra)
        siblings.append(swapped(current, level + 1))
    near_factors = call(
        near_factor_kernel,
        "near_factor",
        [near, high, low, basis, skeleton],
        [((2 * size, size), F32), square, ((rank, size), F32), ((rank, size), F32)],
        micros=1.8,
    )
    (ready,) = call(
        hold_kernel,
        "ready",
        [siblings[-1], near_factors[0]],
        [(siblings[-1].shape, BF16)],
        micros=0.2,
        unused=1,
    )
    siblings += [swapped(value, 0) for value in siblings[1:-1] + [ready]]
    down, image_coef, image_both, keep, send, local_mixed, local_images = call(
        functools.partial(down_kernel, levels),
        "down",
        [position, *siblings, coupling, transfer, *near_factors, *factors[:-1], gram],
        [((2, rank, size), BF16), coef, ((2, rank, size), BF16)]
        + [((rows // 2, size), F32)] * 2
        + [square, square],
        [pltpu.VMEM((rows, size), F32)],
        micros=2.0,
    )

    (image,) = call(image_kernel, "image", [near, down, basis, skeleton], [tall], micros=0.7)
    others = [swapped(image_coef, 0), swapped(residual_coef, 0)]
    (current,) = call(
        pair_up_kernel,
        "pair_up",
        [position, image_coef, residual_coef, *others, transfer],
        [coef],
        micros=0.3,
    )
    pieces = [position] + summed(keep, send, levels, ((current,), (), ()))
    (near,) = call(
        pair_near_kernel,
        "pair_near",
        [block, image, residual],
        [tall_pair],
        micros=2.4,
    )
    own = [swapped(current, 1)]
    current = up(1, current, own[0], [near])
    own.append(swapped(current, 2))
    (cross,) = call(
        pair_cross_kernel,
        "pair_cross",
        [near, image, high, low, current],
        [((2 * size, 2 * size), F32)],
        micros=2.3,
        unused=1,
    )
    for level in range(2, levels - 1):
        current = up(level, current, own[level - 1], [cross] if level == 2 else ())
        own.append(swapped(current, level + 1))
    square_part, near_both = call(
        pair_square_kernel,
        "pair_square",
        [near, basis, skeleton, pieces[1]],
        [((2 * size, 2 * size), F32), ((rank, 2 * size), F32)],
        micros=2.8,
        unused=1,
    )
    (ready,) = call(
        hold_kernel, "ready", [own[-1], near_both], [coef], micros=0.2, unused=1
    )
    other = [swapped(value, 0) for value in own[:-1] + [ready]]
    both_high, both_low, _, ties_high, ties_low, _, _ = factors
    down, alpha_part, base_part, beta_part = call(
        functools.partial(pair_down_kernel, levels),
        "pair_down",
        [position, *others, *own, *other, coupling, transfer, cross, square_part, near_both]
        + [both_high, both_low, image_both, ties_high, ties_low, local_mixed, local_images],
        [((2, rank, 2 * size), BF16)] + [((4 * size, size), F32)] * 3,
        micros=2.5,
    )

    keep, send, alpha, beta, fresh, mixed, images, curvature = call(
        first_kernel,
        "first",
        pieces + [alpha_part, base_part, beta_part],
        [((later_rows // 2, size), F32), ((later_rows // 2, size), F32)] + [square] * 6,
        [pltpu.VMEM((rows, size), F32), pltpu.VMEM((later_rows, size), F32), work],
        micros=5.0,
    )
    inverse, turn, rest = call(
        carry_kernel,
        "carry",
        [alpha, beta, fresh, mixed, images, curvature],
        [square] * 3,
        [work],
        micros=3.0,
    )
    residual, direction, solution, image = call(
        update_kernel,
        "update",
        [residual, direction, solution, image, near, down, basis, skeleton, alpha, beta],
        [tall] * 4,
        micros=3.2,
    )
    pieces = [position] + summed(keep, send, levels, ((), (inverse,), (direction,)))
    return tuple(
        call(
            last_kernel,
            "last",
            pieces + [image, residual, direction, solution, fresh, inverse, turn, rest],
            [tall, tall, tall],
            [pltpu.VMEM((later_rows, size), F32), work]
            + [held] * 3
            + [pltpu.SemaphoreType.DMA((6,))],
            micros=7.0,
            apart=True,
        )
    )


def solution(mesh):
    placed = (
        P(None, ("groups", "leaf")),
        P(("groups", "leaf")),
        P(("groups", "leaf"), None),
        P(("groups", "leaf"), None),
        P(("groups", "leaf"), None, None, None),
        P(("groups", "leaf"), None, None, None),
        P(("groups", "leaf"), None),
        P(("groups", "leaf"), None),
        P(("groups", "leaf"), None),
    )
    return jax.shard_map(
        body,
        mesh=mesh,
        in_specs=placed,
        out_specs=(
            P(("groups", "leaf"), None),
            P(("groups", "leaf"), None),
            P(("groups", "leaf"), None),
        ),
        check_vma=False,
    )
```
